32 devices in a mesh: fsdp: 4 (over y, x), ctx: 4 (over z), tp: 2 (over core).
Axes of the slice: x: 2, y: 2, z: 4, core: 2. Of those that a mesh axis runs over, the one named last changes fastest.
Arguments:
- tokens: bfloat16 [2, 4, 1024, 1152], P(None, 'fsdp', 'ctx'), may hold values from -6 to 6
- segments: int32 [2, 4, 1024], P(None, 'fsdp', 'ctx'), may hold values from 0 to 9, never falling along the last dimension, each value on 1 to 800 neighbouring positions
- cotangent: bfloat16 [2, 4, 1024, 1152], P(None, 'fsdp', 'ctx'), may hold values from -6 to 6
- norm_input: bfloat16 [1152], P(('fsdp', 'ctx')), may hold values from 0.25 to 1.75
- query_weight: bfloat16 [1152, 1024], P(('fsdp', 'ctx'), 'tp'), may hold values from -0.1875 to 0.1875
- key_weight: bfloat16 [1152, 256], P(('fsdp', 'ctx')), may hold values from -0.1875 to 0.1875
- value_weight: bfloat16 [1152, 256], P(('fsdp', 'ctx')), may hold values from -0.1875 to 0.1875
- norm_query: bfloat16 [256], P(('fsdp', 'ctx')), may hold values from 0.25 to 1.75
- norm_key: bfloat16 [256], P(('fsdp', 'ctx')), may hold values from 0.25 to 1.75
- out_weight: bfloat16 [1024, 1152], P('tp', ('fsdp', 'ctx')), may hold values from -0.1875 to 0.1875
- norm_attention: bfloat16 [1152], P(('fsdp', 'ctx')), may hold values from 0.25 to 1.75
- norm_feed: bfloat16 [1152], P(('fsdp', 'ctx')), may hold values from 0.25 to 1.75
- gate_weight: bfloat16 [1152, 6912], P(('fsdp', 'ctx'), 'tp'), may hold values from -0.1875 to 0.1875
- up_weight: bfloat16 [1152, 6912], P(('fsdp', 'ctx'), 'tp'), may hold values from -0.1875 to 0.1875
- down_weight: bfloat16 [6912, 1152], P('tp', ('fsdp', 'ctx')), may hold values from -0.078125 to 0.078125
- norm_feed_out: bfloat16 [1152], P(('fsdp', 'ctx')), may hold values from 0.25 to 1.75
Outputs:
- layer_output: bfloat16 [2, 4, 1024, 1152], P(None, 'fsdp', ('ctx', 'tp'))
- input_grad: float32 [2, 4, 1024, 1152], P(None, 'fsdp', ('ctx', 'tp'))
- grad_norm_input: float32 [1152], P(('fsdp', 'ctx'))
- grad_query_weight: float32 [1152, 1024], P(('fsdp', 'ctx'), 'tp')
- grad_key_weight: float32 [1152, 256], P(('fsdp', 'ctx'))
- grad_value_weight: float32 [1152, 256], P(('fsdp', 'ctx'))
- grad_norm_query: float32 [256], P(('fsdp', 'ctx'))
- grad_norm_key: float32 [256], P(('fsdp', 'ctx'))
- grad_out_weight: float32 [1024, 1152], P('tp', ('fsdp', 'ctx'))
- grad_norm_attention: float32 [1152], P(('fsdp', 'ctx'))
- grad_norm_feed: float32 [1152], P(('fsdp', 'ctx'))
- grad_gate_weight: float32 [1152, 6912], P(('fsdp', 'ctx'), 'tp')
- grad_up_weight: float32 [1152, 6912], P(('fsdp', 'ctx'), 'tp')
- grad_down_weight: float32 [6912, 1152], P('tp', ('fsdp', 'ctx'))
- grad_norm_feed_out: float32 [1152], P(('fsdp', 'ctx'))
The draws below stay inside these ranges and needn't reach their ends.
Inputs may be any that keep to these rules, and one draw needn't show every extreme that they name: `segments`: along each sequence segment numbers never fall; each number is one document of at most 800 consecutive positions.
All inputs are finite; a program needn't handle non-finite values.
Results may differ from the reference program's by a relative error of at most 0.023.
Values may be sent and summed in bfloat16 or wider, within the bound.
No kernel may reach another device: no remote copies, remote signals or barrier semaphores. Data moves between devices by JAX's collectives and lax.ppermute only.
A program may use at most 256 MiB of HBM per device.

```python
import math
import jax
import jax.numpy as jnp
import numpy as np
from jax import lax

D = 1152
HEADS = 4
HEAD_DIM = 256
FF = 6912
WINDOW = 512
LENGTH = 1024
MICRO = 2
SEQS = 4


def shard_levels(own_key, shape, shards, low, largest):
    factor_of = 1.0
    for dim, blocks in shards:
        heights = jax.random.uniform(jax.random.fold_in(jax.random.fold_in(own_key, 6), dim), (blocks,), jnp.float32, low / len(shards), largest / len(shards))
        factor_of = factor_of * jnp.repeat(jnp.exp(heights), shape[dim] // blocks).reshape((-1,) + (1,) * (len(shape) - 1 - dim))
    return factor_of


def profile(number_of, total, limit, skew):
    portions = [(1 << 20) // math.isqrt(standing ** skew) + 1 for standing in range(2, number_of + 1)]
    spare, holding = total - limit - (number_of - 1), [1] * (number_of - 1)
    while spare > 0:
        movable = [i for i in range(number_of - 1) if holding[i] < limit]
        whole, budget = sum([portions[i] for i in movable]), spare
        for i in movable:
            extra = min(limit - holding[i], max(1, budget * portions[i] // whole), spare)
            holding[i] = holding[i] + extra
            spare = spare - extra
    return np.array([limit] + holding)


def ragged(stream_key, count, total, limit, lean):
    if count == 2:
        one = jax.random.randint(stream_key, (), max(1, total - limit), min(limit, total - 1) + 1)
        return jnp.stack([one, total - one])
    lengths = jnp.asarray(profile(count, total, limit, lean), jnp.int32)
    pairs = (count - 1) // 2
    source_of, receiver = lengths[1:1 + 2 * pairs:2], lengths[2:2 + 2 * pairs:2]
    room = jnp.minimum(source_of - 1, limit - receiver)
    shifted = jax.random.randint(jax.random.fold_in(stream_key, 1), (pairs,), 0, 1 << 20) % (room + 1)
    lengths = lengths.at[1:1 + 2 * pairs:2].set(source_of - shifted).at[2:2 + 2 * pairs:2].set(receiver + shifted)
    return lengths[jax.random.permutation(jax.random.fold_in(stream_key, 2), count)]


def bell_draw(stream_key, dims, scale, bound, cuts=(), held_as=jnp.bfloat16):
    values = scale * jax.random.normal(stream_key, dims, jnp.float32)
    if cuts:
        values = values * shard_levels(stream_key, dims, cuts, -0.22, 0.18)
    return jnp.clip(values, -bound, bound).astype(held_as)


def setup_inputs(seed: int = 0) -> dict:
    arg_keys = jax.random.split(jax.random.key(seed), 17)
    tokens = bell_draw(arg_keys[0], (MICRO, SEQS, LENGTH, D), 1.0, 6.0, ((1, 4), (2, 4)))
    segments = jax.vmap(lambda own: jnp.searchsorted(jnp.cumsum(ragged(own, LENGTH // 128 + 2, LENGTH, LENGTH * 25 // 32, 1)), jnp.arange(LENGTH), side="right"))(jax.random.split(arg_keys[1], MICRO * SEQS)).reshape((MICRO, SEQS, LENGTH)).astype(jnp.int32)
    cotangent = bell_draw(arg_keys[2], (MICRO, SEQS, LENGTH, D), 1.0, 6.0, ((1, 4), (2, 4)))
    norm_input = jnp.clip(1.0 + 0.15 * jax.random.normal(arg_keys[3], (D,), jnp.float32), 0.25, 1.75).astype(jnp.bfloat16)
    query_weight = bell_draw(arg_keys[4], (D, HEADS * HEAD_DIM), D ** -0.5, 0.1875, ((0, 16), (1, 2)))
    key_weight = bell_draw(arg_keys[5], (D, HEAD_DIM), D ** -0.5, 0.1875, ((0, 16),))
    value_weight = bell_draw(arg_keys[6], (D, HEAD_DIM), D ** -0.5, 0.1875, ((0, 16),))
    norm_query = jnp.clip(1.0 + 0.15 * jax.random.normal(arg_keys[7], (HEAD_DIM,), jnp.float32), 0.25, 1.75).astype(jnp.bfloat16)
    norm_key = jnp.clip(1.0 + 0.15 * jax.random.normal(arg_keys[8], (HEAD_DIM,), jnp.float32), 0.25, 1.75).astype(jnp.bfloat16)
    out_weight = bell_draw(arg_keys[9], (HEADS * HEAD_DIM, D), (HEADS * HEAD_DIM) ** -0.5, 0.1875, ((0, 2), (1, 16)))
    norm_attention = jnp.clip(1.0 + 0.15 * jax.random.normal(arg_keys[10], (D,), jnp.float32), 0.25, 1.75).astype(jnp.bfloat16)
    norm_feed = jnp.clip(1.0 + 0.15 * jax.random.normal(arg_keys[11], (D,), jnp.float32), 0.25, 1.75).astype(jnp.bfloat16)
    gate_weight = bell_draw(arg_keys[12], (D, FF), D ** -0.5, 0.1875, ((0, 16), (1, 2)))
    up_weight = bell_draw(arg_keys[13], (D, FF), D ** -0.5, 0.1875, ((0, 16), (1, 2)))
    down_weight = bell_draw(arg_keys[14], (FF, D), FF ** -0.5, 0.078125, ((0, 2), (1, 16)))
    norm_feed_out = jnp.clip(1.0 + 0.15 * jax.random.normal(arg_keys[15], (D,), jnp.float32), 0.25, 1.75).astype(jnp.bfloat16)
    return dict(tokens=tokens, segments=segments, cotangent=cotangent, norm_input=norm_input, query_weight=query_weight, key_weight=key_weight, value_weight=value_weight, norm_query=norm_query, norm_key=norm_key, out_weight=out_weight, norm_attention=norm_attention, norm_feed=norm_feed, gate_weight=gate_weight, up_weight=up_weight, down_weight=down_weight, norm_feed_out=norm_feed_out)


EPSILON = 1e-06
ROPE_BASE = 10000.0
SCORE_SCALE = 0.0625
MASKED = -1e+30
EXACT = lax.Precision.HIGHEST

@jax.custom_vjp
def low(v):
    return lax.optimization_barrier(v.astype(jnp.bfloat16)).astype(jnp.float32)

@jax.custom_vjp
def low_back(v):
    return v

def low_keep(v):
    return (low(v), None)

def low_pass(kept, grad):
    return (grad,)

def back_keep(v):
    return (v, None)

def back_low(kept, grad):
    return (low(grad),)
low.defvjp(low_keep, low_pass)
low_back.defvjp(back_keep, back_low)

def normed(values, gain):
    return values * lax.rsqrt(lax.optimization_barrier(jnp.mean(values * values, axis=-1, keepdims=True)) + EPSILON) * gain

def turned(values, cosines, sines):
    middle = values.shape[-1] // 2
    first_half = values[..., :middle]
    second_half = values[..., middle:]
    return jnp.concatenate([first_half * cosines - second_half * sines, second_half * cosines + first_half * sines], axis=-1)

def rotations(offsets, depth):
    middle = depth // 2
    inverse = ROPE_BASE ** (-2.0 * jnp.arange(middle, dtype=jnp.float32) / depth)
    angle_grid = offsets[..., None] * inverse
    return (jnp.cos(angle_grid), jnp.sin(angle_grid))

def feed_inner(gate_act, up_act):
    return jax.nn.gelu(gate_act, approximate=True) * up_act

def doc_starts(segment_ids):
    span_len = segment_ids.shape[-1]
    places = jnp.arange(span_len, dtype=jnp.int32)
    edges = jnp.concatenate([jnp.ones(segment_ids.shape[:-1] + (1,), dtype=jnp.bool_), segment_ids[..., 1:] != segment_ids[..., :-1]], axis=-1)
    return lax.cummax(jnp.where(edges, places, 0), axis=segment_ids.ndim - 1)

def attend_one(item):
    query_rot, key_rot, value_low, starts_row = item
    span_len = key_rot.shape[0]
    raw_scores = jnp.einsum('lhe,me->hlm', query_rot, key_rot, precision=EXACT)
    scaled_scores = low_back(raw_scores) * SCORE_SCALE
    rows_at = jnp.arange(span_len, dtype=jnp.int32)[:, None]
    cols_at = jnp.arange(span_len, dtype=jnp.int32)[None, :]
    allowed = (cols_at <= rows_at) & (rows_at - cols_at < WINDOW) & (cols_at >= starts_row[:, None])
    soft_weights = jax.nn.softmax(jnp.where(allowed, scaled_scores, MASKED), axis=-1)
    mixed_heads = jnp.einsum('hlm,me->lhe', low(soft_weights), value_low, precision=EXACT)
    return low(low_back(mixed_heads))

def layer(inputs, starts, params):
    gain_input, query_proj, key_proj, value_proj, gain_query, gain_key, out_proj, gain_attention, gain_feed, gate_proj, up_proj, down_proj, gain_feed_out = params
    batch_size, span_len, width = inputs.shape
    offsets = (jnp.arange(span_len, dtype=jnp.int32)[None, :] - starts).astype(jnp.float32)
    cosines, sines = rotations(offsets, HEAD_DIM)
    hidden_one = low(normed(inputs, gain_input))
    query_full = low_back(jnp.einsum('bld,de->ble', hidden_one, query_proj, precision=EXACT))
    query_full = query_full.reshape(batch_size, span_len, HEADS, HEAD_DIM)
    key_full = low_back(jnp.einsum('bld,de->ble', hidden_one, key_proj, precision=EXACT))
    value_low = low(low_back(jnp.einsum('bld,de->ble', hidden_one, value_proj, precision=EXACT)))
    query_rot = low(turned(normed(query_full, gain_query), cosines[:, :, None, :], sines[:, :, None, :]))
    key_rot = low(turned(normed(key_full, gain_key), cosines, sines))
    mixed = lax.map(jax.checkpoint(attend_one), (query_rot, key_rot, value_low, starts))
    mixed = mixed.reshape(batch_size, span_len, HEADS * HEAD_DIM)
    attention = low_back(jnp.einsum('ble,ed->bld', mixed, out_proj, precision=EXACT))
    middle = inputs + normed(attention, gain_attention)
    hidden_two = low(normed(middle, gain_feed))
    gate_act = low_back(jnp.einsum('bld,du->blu', hidden_two, gate_proj, precision=EXACT))
    up_act = low_back(jnp.einsum('bld,du->blu', hidden_two, up_proj, precision=EXACT))
    hidden_units = low(feed_inner(gate_act, up_act))
    feed = low_back(jnp.einsum('blu,ud->bld', hidden_units, down_proj, precision=EXACT))
    return middle + normed(feed, gain_feed_out)

def reference(tokens, segments, cotangent, norm_input, query_weight, key_weight, value_weight, norm_query, norm_key, out_weight, norm_attention, norm_feed, gate_weight, up_weight, down_weight, norm_feed_out):
    params = tuple((item.astype(jnp.float32) for item in (norm_input, query_weight, key_weight, value_weight, norm_query, norm_key, out_weight, norm_attention, norm_feed, gate_weight, up_weight, down_weight, norm_feed_out)))
    group_size = math.gcd(SEQS, max(1, 4096 // LENGTH))
    group_count = SEQS // group_size
    totals = tuple((jnp.zeros(item.shape, jnp.float32) for item in params))
    outputs = []
    input_grads = []
    for micro_index in range(MICRO):
        inputs = tokens[micro_index].astype(jnp.float32).reshape(group_count, group_size, LENGTH, D)
        starts = doc_starts(segments[micro_index]).reshape(group_count, group_size, LENGTH)
        cot_all = cotangent[micro_index].astype(jnp.float32).reshape(group_count, group_size, LENGTH, D)

        def one_group(running, item):
            group_in, group_starts, group_cot = item

            def forward(values, weights):
                return layer(values, group_starts, weights)
            result, pull = jax.vjp(forward, group_in, params)
            d_inputs, d_params = pull(group_cot)
            return (tuple((left + right for left, right in zip(running, d_params))), (result, d_inputs))
        totals, (result, d_inputs) = lax.scan(one_group, totals, (inputs, starts, cot_all))
        outputs.append(result.reshape(SEQS, LENGTH, D))
        input_grads.append(d_inputs.reshape(SEQS, LENGTH, D))
    layer_output = jnp.stack(outputs).astype(jnp.bfloat16)
    input_grad = jnp.stack(input_grads)
    return (layer_output, input_grad, totals[0], totals[1], totals[2], totals[3], totals[4], totals[5], totals[6], totals[7], totals[8], totals[9], totals[10], totals[11], totals[12])
```

```python
import jax
import jax.numpy as jnp
from jax import lax
from jax.sharding import PartitionSpec as P

HEAD_DIM = 256
WINDOW = 512

EPSILON = 1e-06
ROPE_BASE = 10000.0
SCORE_SCALE = 0.0625
MASKED = -1e30

F32 = jnp.float32
BF16 = jnp.bfloat16
GROUPS = ((0, 1),)


def dot(spec, left, right):
    return jnp.einsum(spec, left, right, preferred_element_type=F32)


def normed(values, gain):
    return values * lax.rsqrt(jnp.mean(values * values, axis=-1, keepdims=True) + EPSILON) * gain


def turned(values, cosines, sines):
    middle = values.shape[-1] // 2
    first_half = values[..., :middle]
    second_half = values[..., middle:]
    return jnp.concatenate(
        [first_half * cosines - second_half * sines, second_half * cosines + first_half * sines],
        axis=-1,
    )


def rotations(offsets, depth):
    middle = depth // 2
    inverse = ROPE_BASE ** (-2.0 * jnp.arange(middle, dtype=F32) / depth)
    angle_grid = offsets[..., None] * inverse
    return (jnp.cos(angle_grid), jnp.sin(angle_grid))


def rope_normed(values, gain, cosines, sines):
    return turned(normed(values, gain), cosines, sines)


def feed_inner(gate_act, up_act):
    return jax.nn.gelu(gate_act, approximate=True) * up_act


def swap(value):
    return lax.ppermute(value, "tp", [(0, 1), (1, 0)])


def cross(value, axis, step):
    if step == 0:
        return value
    return lax.ppermute(value, axis, [(i, i ^ step) for i in range(lax.axis_size(axis))])


def shift(value, step):
    count = lax.axis_size("ctx")
    pairs = [(i, i + step) for i in range(count) if 0 <= i + step < count]
    return lax.ppermute(value, "ctx", pairs)


def gather_axis(value, axis):
    count, mine = lax.axis_size(axis), lax.axis_index(axis)
    whole = jnp.zeros((count,) + value.shape, value.dtype)
    for step in range(count):
        whole = lax.dynamic_update_index_in_dim(whole, cross(value, axis, step), mine ^ step, 0)
    return whole


def scatter_axis(value, axis):
    count, mine = lax.axis_size(axis), lax.axis_index(axis)
    total = lax.dynamic_index_in_dim(value, mine, 0, keepdims=False).astype(F32)
    for step in range(1, count):
        piece = lax.dynamic_index_in_dim(value, mine ^ step, 0, keepdims=False)
        total = total + cross(piece.astype(BF16), axis, step).astype(F32)
    return total


def trade_axis(value, axis):
    count, mine = lax.axis_size(axis), lax.axis_index(axis)
    whole = value
    for step in range(1, count):
        piece = lax.dynamic_index_in_dim(value, mine ^ step, 0, keepdims=False)
        whole = lax.dynamic_update_index_in_dim(whole, cross(piece, axis, step), mine ^ step, 0)
    return whole


def gather_rows(value):
    return jnp.swapaxes(gather_axis(gather_axis(value, "ctx"), "fsdp"), 0, 0)


def scatter_rows(value):
    return scatter_axis(scatter_axis(value, "fsdp").astype(BF16), "ctx")


def spread(rows):
    mine = [cross(rows, "fsdp", step) for step in range(lax.axis_size("fsdp"))]
    return jnp.concatenate(mine + [swap(piece) for piece in mine], axis=0)


def collect(part):
    count = lax.axis_size("fsdp")
    half = part.shape[0] // 2
    own = part[:half].astype(F32) + swap(part[half:]).astype(F32)
    size = half // count
    total = own[:size]
    for step in range(1, count):
        piece = own[step * size : (step + 1) * size].astype(BF16)
        total = total + cross(piece, "fsdp", step).astype(F32)
    return total


def local(
    tokens,
    segments,
    cotangent,
    norm_input,
    query_weight,
    key_weight,
    value_weight,
    norm_query,
    norm_key,
    out_weight,
    norm_attention,
    norm_feed,
    gate_weight,
    up_weight,
    down_weight,
    norm_feed_out,
):
    micros, seqs, block_len, width = tokens.shape
    planes = lax.axis_size("fsdp")
    depths = lax.axis_size("ctx")
    ctx_place = lax.axis_index("ctx")
    tp_place = lax.axis_index("tp")
    first_core = tp_place == 0
    half_len = block_len // lax.axis_size("tp")
    back_blocks = -(-WINDOW // block_len)
    rows_in = norm_input.shape[0]
    heads_half = query_weight.shape[1] // HEAD_DIM
    q_cols = query_weight.shape[1]
    units = gate_weight.shape[1] // planes

    gains_packed = jnp.concatenate(
        [norm_input, norm_attention, norm_feed, norm_feed_out, norm_query, norm_key]
    )[None]
    small = norm_query.shape[0]
    gains_all = gather_rows(gains_packed).reshape(planes * depths, -1).astype(F32)
    cuts = [0, rows_in, 2 * rows_in, 3 * rows_in, 4 * rows_in, 4 * rows_in + small]
    ends = cuts[1:] + [4 * rows_in + 2 * small]
    gain_input, gain_attention, gain_feed, gain_feed_out, gain_query, gain_key = (
        gains_all[:, lo:hi].reshape(-1) for lo, hi in zip(cuts, ends)
    )

    kv_shard = jnp.where(first_core, key_weight, value_weight)
    kv_own = gather_rows(kv_shard).reshape(width, HEAD_DIM)
    q_own = gather_rows(query_weight).reshape(width, q_cols)
    out_own = gather_rows(out_weight.T).reshape(width, q_cols)
    kv_cat = jnp.concatenate([kv_own, swap(kv_own)], axis=1)
    q_cat = jnp.concatenate([q_own, swap(q_own)], axis=1)
    out_cat = jnp.concatenate([out_own, swap(out_own)], axis=1)

    def plane_weight(shard):
        parts = jnp.swapaxes(shard.reshape(rows_in, planes, units), 0, 1)
        traded = trade_axis(parts, "fsdp")
        return lax.all_gather(traded, "ctx", axis=1, tiled=True).reshape(width, units)

    gate_w = plane_weight(gate_weight)
    up_w = plane_weight(up_weight)
    down_w = plane_weight(down_weight.T)

    segments_all = lax.all_gather(segments, "ctx", axis=2, tiled=True)
    half_at = tp_place * half_len
    seg_half = lax.dynamic_slice_in_dim(segments, half_at, half_len, 2)
    starts = jnp.sum(
        (segments_all[:, :, None, :] < seg_half[:, :, :, None]).astype(jnp.int32), axis=-1
    )
    token_place = ctx_place * block_len + half_at + jnp.arange(half_len, dtype=jnp.int32)
    cosines, sines = rotations((token_place - starts).astype(F32), HEAD_DIM)
    within = jnp.arange(half_len, dtype=jnp.int32)
    key_place = jnp.concatenate(
        [
            (ctx_place - back) * block_len + side * half_len + within
            for side in (tp_place, 1 - tp_place)
            for back in range(back_blocks + 1)
        ]
    )

    x_halves = lax.dynamic_slice_in_dim(tokens, half_at, half_len, 2)
    dy_halves = lax.dynamic_slice_in_dim(cotangent, half_at, half_len, 2)

    saved = []
    outputs = []
    for group in GROUPS:
        lo, hi = group[0], group[-1] + 1
        batch = (hi - lo) * seqs

        def pick(value):
            return value[lo:hi].reshape((batch,) + value.shape[2:])

        x = pick(x_halves).astype(F32)
        cos, sin, begin = pick(cosines), pick(sines), pick(starts)
        cos_heads, sin_heads = cos[:, :, None, :], sin[:, :, None, :]
        h1 = normed(x, gain_input).astype(BF16)
        kv = dot("bld,de->ble", h1, kv_cat)
        kv_left, kv_right = kv[..., :HEAD_DIM], kv[..., HEAD_DIM:]
        key_full = jnp.where(first_core, kv_left, kv_right)
        value_full = jnp.where(first_core, kv_right, kv_left)
        key_rot = rope_normed(key_full, gain_key, cos, sin).astype(BF16)
        pair = jnp.concatenate([key_rot, value_full.astype(BF16)], axis=-1)
        mine = jnp.concatenate(
            [pair] + [shift(pair, back) for back in range(1, back_blocks + 1)], axis=1
        )
        seen = jnp.concatenate([mine, swap(mine)], axis=1)
        keys, values = seen[..., :HEAD_DIM], seen[..., HEAD_DIM:]
        query_full = dot("bld,de->ble", h1, q_cat).reshape(
            batch, half_len, 2 * heads_half, HEAD_DIM
        )
        query_rot = rope_normed(query_full, gain_query, cos_heads, sin_heads).astype(BF16)
        allowed = (
            (key_place[None, None, :] <= token_place[None, :, None])
            & (token_place[None, :, None] - key_place[None, None, :] < WINDOW)
            & (key_place[None, None, :] >= begin[:, :, None])
        )
        raw = dot("blhe,bke->bhlk", query_rot, keys)
        scores = jnp.where(allowed[:, None], raw * SCORE_SCALE, MASKED)
        row_max = jnp.max(scores, axis=-1, keepdims=True)
        lifted = jnp.exp(scores - row_max)
        prob = lifted / jnp.sum(lifted, axis=-1, keepdims=True)
        prob_low = prob.astype(BF16)
        mixed = dot("bhlk,bke->blhe", prob_low, values).astype(BF16)
        mixed = mixed.reshape(batch, half_len, 2 * q_cols)
        attention = dot("ble,de->bld", mixed, out_cat)
        middle = x + normed(attention, gain_attention)
        h2 = normed(middle, gain_feed).astype(BF16).reshape(batch * half_len, width)
        h2_all = spread(h2)
        gate_act = dot("td,du->tu", h2_all, gate_w)
        up_act = dot("td,du->tu", h2_all, up_w)
        hidden = feed_inner(gate_act, up_act).astype(BF16)
        feed = collect(dot("tu,du->td", hidden, down_w).astype(BF16))
        feed = feed.reshape(batch, half_len, width)
        layer_out = (middle + normed(feed, gain_feed_out)).astype(BF16)
        outputs.append(layer_out.reshape(hi - lo, seqs, half_len, width))
        saved.append(
            (x, cos, sin, h1, key_full, query_full, query_rot, keys, values, prob, prob_low)
            + (mixed, attention, middle, h2_all, gate_act, up_act, hidden, feed)
        )

    input_grads = []
    grads = None
    for group, kept in zip(GROUPS, saved):
        lo, hi = group[0], group[-1] + 1
        batch = (hi - lo) * seqs
        (x, cos, sin, h1, key_full, query_full, query_rot, keys, values, prob, prob_low) = kept[:11]
        (mixed, attention, middle, h2_all, gate_act, up_act, hidden, feed) = kept[11:]
        cos_heads, sin_heads = cos[:, :, None, :], sin[:, :, None, :]
        dy = dy_halves[lo:hi].reshape(batch, half_len, width).astype(F32)
        d_feed, d_gain_feed_out = jax.vjp(normed, feed, gain_feed_out)[1](dy)
        d_feed_all = spread(d_feed.astype(BF16).reshape(batch * half_len, width))
        grad_down = dot("td,tu->du", d_feed_all, hidden)
        d_hidden = dot("td,du->tu", d_feed_all, down_w)
        d_gate, d_up = jax.vjp(feed_inner, gate_act, up_act)[1](d_hidden)
        d_gate, d_up = d_gate.astype(BF16), d_up.astype(BF16)
        d_h2 = collect(
            (dot("tu,du->td", d_gate, gate_w) + dot("tu,du->td", d_up, up_w)).astype(BF16)
        ).reshape(batch, half_len, width)
        grad_gate = dot("td,tu->du", h2_all, d_gate)
        grad_up = dot("td,tu->du", h2_all, d_up)
        d_mid_norm, d_gain_feed = jax.vjp(normed, middle, gain_feed)[1](d_h2)
        d_middle = dy + d_mid_norm
        d_attention, d_gain_attention = jax.vjp(normed, attention, gain_attention)[1](d_middle)
        d_attention = d_attention.astype(BF16)
        grad_out = dot("bld,ble->de", d_attention, mixed)
        d_mixed = dot("bld,de->ble", d_attention, out_cat).astype(BF16)
        d_mixed = d_mixed.reshape(batch, half_len, 2 * heads_half, HEAD_DIM)
        d_prob = dot("blhe,bke->bhlk", d_mixed, values)
        row_delta = jnp.sum(prob * d_prob, axis=-1, keepdims=True)
        d_raw = (prob * (d_prob - row_delta) * SCORE_SCALE).astype(BF16)
        d_query_rot = dot("bhlk,bke->blhe", d_raw, keys)
        d_keys = dot("bhlk,blhe->bke", d_raw, query_rot)
        d_values = dot("bhlk,blhe->bke", prob_low, d_mixed)
        d_pair = jnp.concatenate([d_keys, d_values], axis=-1)
        side = (back_blocks + 1) * half_len
        d_mine = d_pair[:, :side] + swap(d_pair[:, side:].astype(BF16)).astype(F32)
        d_kv = d_mine[:, :half_len]
        for back in range(1, back_blocks + 1):
            piece = d_mine[:, back * half_len : (back + 1) * half_len].astype(BF16)
            d_kv = d_kv + shift(piece, -back).astype(F32)

        def rotate_query(value, gain):
            return rope_normed(value, gain, cos_heads, sin_heads)

        def rotate_key(value, gain):
            return rope_normed(value, gain, cos, sin)

        d_query, d_gain_query = jax.vjp(rotate_query, query_full, gain_query)[1](d_query_rot)
        d_query = d_query.astype(BF16).reshape(batch, half_len, 2 * q_cols)
        d_key, d_gain_key = jax.vjp(rotate_key, key_full, gain_key)[1](d_kv[..., :HEAD_DIM])
        d_key = d_key.astype(BF16)
        d_value = d_kv[..., HEAD_DIM:].astype(BF16)
        d_kv_low = jnp.concatenate(
            [jnp.where(first_core, d_key, d_value), jnp.where(first_core, d_value, d_key)], axis=-1
        )
        grad_query = dot("bld,ble->de", h1, d_query)
        grad_kv = dot("bld,ble->de", h1, d_kv_low)
        d_h1 = dot("ble,de->bld", d_query, q_cat) + dot("ble,de->bld", d_kv_low, kv_cat)
        d_input_norm, d_gain_input = jax.vjp(normed, x, gain_input)[1](d_h1)
        input_grads.append((d_middle + d_input_norm).reshape(hi - lo, seqs, half_len, width))
        gain_grads = (d_gain_input, d_gain_attention, d_gain_feed, d_gain_feed_out)
        gain_grads = gain_grads + (d_gain_query, d_gain_key)
        now = (grad_down, grad_gate, grad_up, grad_out, grad_query, grad_kv) + gain_grads
        grads = now if grads is None else tuple(a + b for a, b in zip(grads, now))

    grad_down, grad_gate, grad_up, grad_out, grad_query, grad_kv = grads[:6]
    gain_grads = grads[6:]

    def plane_grad(grad):
        shaped = jnp.swapaxes(grad.astype(BF16).reshape(planes, depths, rows_in, units), 0, 1)
        part = lax.psum_scatter(
            shaped.reshape(depths * planes, rows_in, units), "ctx", scatter_dimension=0, tiled=True
        )
        return jnp.swapaxes(trade_axis(part, "fsdp"), 0, 1).reshape(rows_in, planes * units)

    out_down = plane_grad(grad_down).astype(F32).T
    out_gate = plane_grad(grad_gate).astype(F32)
    out_up = plane_grad(grad_up).astype(F32)

    def core_grad(grad):
        half = grad.shape[1] // 2
        own = grad[:, :half] + swap(grad[:, half:].astype(BF16)).astype(F32)
        return scatter_rows(own.astype(BF16).reshape(planes, depths, rows_in, half))

    out_out = core_grad(grad_out).T
    out_query = core_grad(grad_query)
    out_kv = core_grad(grad_kv)
    kv_other = swap(out_kv)
    out_key = jnp.where(first_core, out_kv, kv_other)
    out_value = jnp.where(first_core, kv_other, out_kv)

    gains_sum = jnp.concatenate(
        [grad.reshape(planes, depths, 1, -1) for grad in gain_grads], axis=-1
    )
    gains_sum = gains_sum + swap(gains_sum)
    gains_out = scatter_axis(scatter_axis(gains_sum, "fsdp"), "ctx")[0]
    pieces = [gains_out[lo:hi] for lo, hi in zip(cuts, ends)]

    return (
        jnp.concatenate(outputs, axis=0),
        jnp.concatenate(input_grads, axis=0),
        pieces[0],
        out_query,
        out_key,
        out_value,
        pieces[4],
        pieces[5],
        out_out,
        pieces[1],
        pieces[2],
        out_gate,
        out_up,
        out_down,
        pieces[3],
    )


def solution(mesh):
    both = ("fsdp", "ctx")
    return jax.shard_map(
        local,
        mesh=mesh,
        in_specs=(
            P(None, "fsdp", "ctx", None),
            P(None, "fsdp", "ctx"),
            P(None, "fsdp", "ctx", None),
            P(both),
            P(both, "tp"),
            P(both, None),
            P(both, None),
            P(both),
            P(both),
            P("tp", both),
            P(both),
            P(both),
            P(both, "tp"),
            P(both, "tp"),
            P("tp", both),
            P(both),
        ),
        out_specs=(
            P(None, "fsdp", ("ctx", "tp"), None),
            P(None, "fsdp", ("ctx", "tp"), None),
            P(both),
            P(both, "tp"),
            P(both, None),
            P(both, None),
            P(both),
            P(both),
            P("tp", both),
            P(both),
            P(both),
            P(both, "tp"),
            P(both, "tp"),
            P("tp", both),
            P(both),
        ),
        check_vma=False,
    )
```

```python
import jax
import jax.numpy as jnp
from jax import lax
from jax.sharding import PartitionSpec as P

HEAD_DIM = 256
WINDOW = 512

EPSILON = 1e-06
ROPE_BASE = 10000.0
SCORE_SCALE = 0.0625
MASKED = -1e30

SEGMENT_NUMBERS = 10

F32 = jnp.float32
BF16 = jnp.bfloat16
GROUPS = ((0, 1),)


def dot(spec, left, right):
    return jnp.einsum(spec, left, right, preferred_element_type=F32)


def normed(values, gain):
    return values * lax.rsqrt(jnp.mean(values * values, axis=-1, keepdims=True) + EPSILON) * gain


def turned(values, cosines, sines):
    middle = values.shape[-1] // 2
    first_half = values[..., :middle]
    second_half = values[..., middle:]
    return jnp.concatenate(
        [first_half * cosines - second_half * sines, second_half * cosines + first_half * sines],
        axis=-1,
    )


def rotations(offsets, depth):
    middle = depth // 2
    inverse = ROPE_BASE ** (-2.0 * jnp.arange(middle, dtype=F32) / depth)
    angle_grid = offsets[..., None] * inverse
    return (jnp.cos(angle_grid), jnp.sin(angle_grid))


def rope_normed(values, gain, cosines, sines):
    return turned(normed(values, gain), cosines, sines)


def feed_inner(gate_act, up_act):
    return jax.nn.gelu(gate_act, approximate=True) * up_act


def swap(value):
    return lax.ppermute(value, "tp", [(0, 1), (1, 0)])


BOTH = ("fsdp", "ctx")


def cross(value, mask):
    count = lax.axis_size("fsdp") * lax.axis_size("ctx")
    return lax.ppermute(value, BOTH, [(i, i ^ mask) for i in range(count)])


def shift(value, step):
    count = lax.axis_size("ctx")
    pairs = [(i, i + step) for i in range(count) if 0 <= i + step < count]
    return lax.ppermute(value, "ctx", pairs)


def together(*values):
    return lax.optimization_barrier(values)


def placed(own, other, bit, dim):
    first = jnp.where(bit == 0, own, other)
    second = jnp.where(bit == 0, other, own)
    return jnp.concatenate([first, second], axis=dim)


def parted(value, bit, dim):
    zero = lax.index_in_dim(value, 0, axis=dim, keepdims=False)
    one = lax.index_in_dim(value, 1, axis=dim, keepdims=False)
    return jnp.where(bit == 0, zero, one), jnp.where(bit == 0, one, zero)


def copies_to(value, axis):
    count = lax.axis_size(axis)
    return lax.all_to_all(jnp.broadcast_to(value[None], (count,) + value.shape), axis, 0, 0)


def gather_rows(value):
    return copies_to(copies_to(value, "ctx"), "fsdp")


def sum_of(parts, axis):
    return jnp.sum(lax.all_to_all(parts.astype(BF16), axis, 0, 0).astype(F32), axis=0)


def scatter_rows(value):
    return sum_of(sum_of(value, "fsdp"), "ctx")


def near_groups():
    planes, depths = lax.axis_size("fsdp"), lax.axis_size("ctx")
    return [
        [(f + x) * depths + c + z for x in (0, 1) for z in (0, 1)]
        for f in range(0, planes, 2)
        for c in range(0, depths, 2)
    ]


def trade(value):
    return lax.all_to_all(value, BOTH, 0, 0, axis_index_groups=near_groups())


def trade_apart(value):
    depths = lax.axis_size("ctx")
    x_bit, z_bit = lax.axis_index("fsdp") & 1, lax.axis_index("ctx") & 1
    low, high = parted(value.reshape((2, 2) + value.shape[1:]), x_bit, 0)
    (p0, p1), (p2, p3) = parted(low, z_bit, 0), parted(high, z_bit, 0)
    p1, p2, p3 = cross(p1, 1), cross(p2, depths), cross(p3, depths | 1)
    low = placed(p0[None], p1[None], z_bit, 0)
    high = placed(p2[None], p3[None], z_bit, 0)
    return placed(low[None], high[None], x_bit, 0).reshape(value.shape)


def far_bits():
    planes, depths = lax.axis_size("fsdp"), lax.axis_size("ctx")
    f_place, c_place = lax.axis_index("fsdp"), lax.axis_index("ctx")
    f_count, c_count = (planes - 1).bit_length(), (depths - 1).bit_length()
    c_bits = [(1 << k, (c_place >> k) & 1) for k in range(c_count - 1, 0, -1)]
    f_bits = [(depths << k, (f_place >> k) & 1) for k in range(f_count - 1, 0, -1)]
    return c_bits, f_bits


def gather_depth(value):
    c_bits, _ = far_bits()
    for mask, bit in c_bits[::-1]:
        value = placed(value, cross(value, mask), bit, 1)
    return value


def gather_plane(value):
    _, f_bits = far_bits()
    for mask, bit in f_bits[::-1]:
        value = placed(value, cross(value, mask), bit, 0)
    return value


def scatter_plane(value):
    _, f_bits = far_bits()
    for mask, bit in f_bits:
        halves = value.reshape((2, value.shape[0] // 2) + value.shape[1:])
        mine, other = parted(halves, bit, 0)
        value = (mine.astype(F32) + cross(other, mask).astype(F32)).astype(BF16)
    return value


def scatter_depth(value):
    c_bits, _ = far_bits()
    for mask, bit in c_bits:
        halves = value.reshape((2, 2, value.shape[1] // 2) + value.shape[2:])
        mine, other = parted(halves, bit, 1)
        value = (mine.astype(F32) + cross(other, mask).astype(F32)).astype(BF16)
    return value


def spread_start(rows):
    mine = trade(jnp.broadcast_to(rows[None], (4,) + rows.shape))
    return mine.reshape((-1,) + rows.shape[1:])


def spread(rows):
    mine = spread_start(rows)
    return jnp.concatenate([mine, swap(mine)], axis=0)


def collect_start(part):
    half = part.shape[0] // 2
    own = part[:half].astype(F32) + swap(part[half:]).astype(F32)
    return own.astype(BF16).reshape(4, half // 4, part.shape[1])


def collect(part):
    return jnp.sum(trade(collect_start(part)).astype(F32), axis=0)


def local(
    tokens,
    segments,
    cotangent,
    norm_input,
    query_weight,
    key_weight,
    value_weight,
    norm_query,
    norm_key,
    out_weight,
    norm_attention,
    norm_feed,
    gate_weight,
    up_weight,
    down_weight,
    norm_feed_out,
):
    micros, seqs, block_len, width = tokens.shape
    planes = lax.axis_size("fsdp")
    depths = lax.axis_size("ctx")
    chunks = planes * depths
    ctx_place = lax.axis_index("ctx")
    tp_place = lax.axis_index("tp")
    first_core = tp_place == 0
    half_len = block_len // lax.axis_size("tp")
    back_blocks = -(-WINDOW // block_len)
    rows_in = norm_input.shape[0]
    small = norm_query.shape[0]
    heads_half = query_weight.shape[1] // HEAD_DIM
    q_cols = query_weight.shape[1]
    units = -(-gate_weight.shape[1] // (4 * 128)) * 128
    spare = 4 * units - gate_weight.shape[1]
    numbers = jnp.arange(SEGMENT_NUMBERS, dtype=jnp.int32)
    counts = jnp.sum((segments[..., None] == numbers).astype(F32), axis=2).astype(BF16)
    kv_shard = jnp.where(first_core, key_weight, value_weight)
    gain_row = jnp.concatenate(
        [norm_input, norm_attention, norm_feed, norm_feed_out, norm_query, norm_key]
    )
    first_cols = q_cols + HEAD_DIM
    gain_row = jnp.pad(gain_row, (0, first_cols - gain_row.shape[0]))
    count_row = counts.reshape(-1)
    count_row = jnp.pad(count_row, (0, 7 * first_cols - count_row.shape[0]))
    first_pack = jnp.concatenate([query_weight, kv_shard], axis=1)
    rows_more = jnp.concatenate([gain_row, count_row]).reshape(8, first_cols)
    first_pack = jnp.concatenate([first_pack, rows_more], axis=0)
    first_pack = jnp.broadcast_to(first_pack[None], (depths,) + first_pack.shape)
    first_pack, gate_weight, up_weight, down_weight, out_weight = together(
        first_pack, gate_weight, up_weight, down_weight, out_weight
    )
    first_pack = lax.all_to_all(first_pack, "ctx", 0, 0)

    feed_parts = jnp.stack([gate_weight, up_weight, down_weight.T], axis=0)
    feed_parts = jnp.pad(feed_parts, ((0, 0), (0, 0), (0, spare)))
    feed_parts = feed_parts.reshape(3, rows_in, 4, units).transpose(2, 0, 1, 3)
    feed_parts = trade_apart(feed_parts)
    first_pack, feed_parts = together(first_pack, feed_parts)
    counts_all = first_pack[:, rows_in + 1, : counts.size].astype(F32)
    counts_all = jnp.sum(counts_all, axis=0).reshape(counts.shape)

    feed_parts = feed_parts.reshape(2, 2, 3, rows_in, units)
    gate_near, up_near, down_near = (feed_parts[:, :, which] for which in range(3))
    gate_deep = gather_depth(gate_near)
    first_pack = copies_to(first_pack, "fsdp")
    first_pack, gate_deep, up_near, down_near, out_pack = together(
        first_pack, gate_deep, up_near, down_near, out_weight.T
    )

    first_pack = first_pack.reshape(chunks, rows_in + 8, first_cols)
    gains_all = first_pack[:, rows_in].astype(F32)
    first_own = first_pack[:, :rows_in].reshape(width, first_cols)
    first_other = swap(first_own)
    cuts = [0, rows_in, 2 * rows_in, 3 * rows_in, 4 * rows_in, 4 * rows_in + small]
    ends = cuts[1:] + [4 * rows_in + 2 * small]
    gain_input, gain_attention, gain_feed, gain_feed_out, gain_query, gain_key = (
        gains_all[:, lo:hi].reshape(-1) for lo, hi in zip(cuts, ends)
    )
    out_pack = copies_to(out_pack, "ctx")
    up_deep = gather_depth(up_near)
    gate_w = gather_plane(gate_deep).reshape(width, units)

    half_at = tp_place * half_len
    seg_half = lax.dynamic_slice_in_dim(segments, half_at, half_len, 2)
    earlier = numbers < seg_half[..., None]
    starts = jnp.sum(jnp.where(earlier, counts_all[:, :, None, :], 0.0), axis=-1)
    starts = starts.astype(jnp.int32)
    token_place = ctx_place * block_len + half_at + jnp.arange(half_len, dtype=jnp.int32)
    cosines, sines = rotations((token_place - starts).astype(F32), HEAD_DIM)
    within = jnp.arange(half_len, dtype=jnp.int32)
    key_place = jnp.concatenate(
        [
            (ctx_place - back) * block_len + side * half_len + within
            for side in (tp_place, 1 - tp_place)
            for back in range(back_blocks + 1)
        ]
    )

    x_halves = lax.dynamic_slice_in_dim(tokens, half_at, half_len, 2)
    dy_halves = lax.dynamic_slice_in_dim(cotangent, half_at, half_len, 2)

    saved = []
    outputs = []
    for group in GROUPS:
        lo, hi = group[0], group[-1] + 1
        batch = (hi - lo) * seqs

        def pick(value):
            return value[lo:hi].reshape((batch,) + value.shape[2:])

        x = pick(x_halves).astype(F32)
        cos, sin, begin = pick(cosines), pick(sines), pick(starts)
        cos_heads, sin_heads = cos[:, :, None, :], sin[:, :, None, :]
        h1 = normed(x, gain_input).astype(BF16)
        left = dot("bld,de->ble", h1, first_own)
        right = dot("bld,de->ble", h1, first_other)
        kv_left, kv_right = left[..., q_cols:], right[..., q_cols:]
        key_full = jnp.where(first_core, kv_left, kv_right)
        value_full = jnp.where(first_core, kv_right, kv_left)
        key_rot = rope_normed(key_full, gain_key, cos, sin).astype(BF16)
        pair = jnp.concatenate([key_rot, value_full.astype(BF16)], axis=-1)
        pair, left, right, up_deep, gate_w, out_pack = together(
            pair, left, right, up_deep, gate_w, out_pack
        )
        up_w = gather_plane(up_deep).reshape(width, units)
        out_own = copies_to(out_pack, "fsdp").reshape(width, q_cols)
        mine = jnp.concatenate(
            [pair] + [shift(pair, back) for back in range(1, back_blocks + 1)], axis=1
        )
        seen = jnp.concatenate([mine, swap(mine)], axis=1)
        keys, values = seen[..., :HEAD_DIM], seen[..., HEAD_DIM:]
        query_full = jnp.concatenate([left[..., :q_cols], right[..., :q_cols]], axis=-1)
        query_full = query_full.reshape(batch, half_len, 2 * heads_half, HEAD_DIM)
        query_rot = rope_normed(query_full, gain_query, cos_heads, sin_heads).astype(BF16)
        query_rot, keys, values, up_w, out_own, down_near = together(
            query_rot, keys, values, up_w, out_own, down_near
        )
        out_other = swap(out_own)
        down_deep = gather_depth(down_near)
        allowed = (
            (key_place[None, None, :] <= token_place[None, :, None])
            & (token_place[None, :, None] - key_place[None, None, :] < WINDOW)
            & (key_place[None, None, :] >= begin[:, :, None])
        )
        raw = dot("blhe,bke->bhlk", query_rot, keys)
        scores = jnp.where(allowed[:, None], raw * SCORE_SCALE, MASKED)
        row_max = jnp.max(scores, axis=-1, keepdims=True)
        lifted = jnp.exp(scores - row_max)
        prob = lifted / jnp.sum(lifted, axis=-1, keepdims=True)
        prob_low = prob.astype(BF16)
        mixed = dot("bhlk,bke->blhe", prob_low, values).astype(BF16)
        mixed = mixed.reshape(batch, half_len, 2 * q_cols)
        attention = dot("ble,de->bld", mixed[..., :q_cols], out_own)
        attention = attention + dot("ble,de->bld", mixed[..., q_cols:], out_other)
        middle = x + normed(attention, gain_attention)
        h2 = normed(middle, gain_feed).astype(BF16).reshape(batch * half_len, width)
        h2, down_deep = together(h2, down_deep)
        down_w = gather_plane(down_deep).reshape(width, units)
        h2_mine, down_w = together(spread_start(h2), down_w)
        h2_all = jnp.concatenate([h2_mine, swap(h2_mine)], axis=0)
        gate_act = dot("td,du->tu", h2_all, gate_w)
        up_act = dot("td,du->tu", h2_all, up_w)
        hidden = feed_inner(gate_act, up_act).astype(BF16)
        feed = collect(dot("tu,du->td", hidden, down_w).astype(BF16))
        feed = feed.reshape(batch, half_len, width)
        layer_out = (middle + normed(feed, gain_feed_out)).astype(BF16)
        outputs.append(layer_out.reshape(hi - lo, seqs, half_len, width))
        saved.append(
            (x, cos, sin, h1, key_full, query_full, query_rot, keys, values, prob, prob_low)
            + (mixed, attention, middle, h2_all, gate_act, up_act, hidden, feed)
        )

    input_grads = []
    grads = None
    for group, kept in zip(GROUPS, saved):
        lo, hi = group[0], group[-1] + 1
        batch = (hi - lo) * seqs
        (x, cos, sin, h1, key_full, query_full, query_rot, keys, values, prob, prob_low) = kept[:11]
        (mixed, attention, middle, h2_all, gate_act, up_act, hidden, feed) = kept[11:]
        cos_heads, sin_heads = cos[:, :, None, :], sin[:, :, None, :]
        dy = dy_halves[lo:hi].reshape(batch, half_len, width).astype(F32)
        d_feed, d_gain_feed_out = jax.vjp(normed, feed, gain_feed_out)[1](dy)
        d_feed_all = spread(d_feed.astype(BF16).reshape(batch * half_len, width))
        grad_down = dot("td,tu->du", d_feed_all, hidden).astype(BF16)
        d_feed_all, grad_down = together(d_feed_all, grad_down)
        down_plane = scatter_plane(grad_down.reshape(planes, depths, rows_in, units))
        d_hidden = dot("td,du->tu", d_feed_all, down_w)
        d_gate, d_up = jax.vjp(feed_inner, gate_act, up_act)[1](d_hidden)
        d_gate, d_up = d_gate.astype(BF16), d_up.astype(BF16)
        d_h2_part = dot("tu,du->td", d_gate, gate_w) + dot("tu,du->td", d_up, up_w)
        d_h2_part = d_h2_part.astype(BF16)
        d_h2_part, down_plane, d_gate, d_up = together(d_h2_part, down_plane, d_gate, d_up)
        d_h2_part = collect_start(d_h2_part)
        grad_gate = dot("td,tu->du", h2_all, d_gate).astype(BF16)
        d_h2_part, grad_gate, d_up = together(d_h2_part, grad_gate, d_up)
        d_h2_parts = trade(d_h2_part)
        gate_plane = scatter_plane(grad_gate.reshape(planes, depths, rows_in, units))
        grad_up = dot("td,tu->du", h2_all, d_up).astype(BF16)
        d_h2_parts, gate_plane, grad_up, down_plane = together(
            d_h2_parts, gate_plane, grad_up, down_plane
        )
        up_plane = scatter_plane(grad_up.reshape(planes, depths, rows_in, units))
        down_near = scatter_depth(down_plane)
        d_h2 = jnp.sum(d_h2_parts.astype(F32), axis=0).reshape(batch, half_len, width)
        d_mid_norm, d_gain_feed = jax.vjp(normed, middle, gain_feed)[1](d_h2)
        d_middle = dy + d_mid_norm
        d_attention, d_gain_attention = jax.vjp(normed, attention, gain_attention)[1](d_middle)
        d_attention = d_attention.astype(BF16)
        d_mixed = jnp.concatenate(
            [dot("bld,de->ble", d_attention, half) for half in (out_own, out_other)], axis=-1
        ).astype(BF16)
        d_mixed = d_mixed.reshape(batch, half_len, 2 * heads_half, HEAD_DIM)
        d_prob = dot("blhe,bke->bhlk", d_mixed, values)
        row_delta = jnp.sum(prob * d_prob, axis=-1, keepdims=True)
        d_raw = (prob * (d_prob - row_delta) * SCORE_SCALE).astype(BF16)
        d_raw, prob_low, up_plane, down_near, gate_plane = together(
            d_raw, prob_low, up_plane, down_near, gate_plane
        )
        gate_near = scatter_depth(gate_plane)
        d_query_rot = dot("bhlk,bke->blhe", d_raw, keys)
        d_keys = dot("bhlk,blhe->bke", d_raw, query_rot)
        d_values = dot("bhlk,blhe->bke", prob_low, d_mixed)
        d_pair = jnp.concatenate([d_keys, d_values], axis=-1)
        out_right = dot("bld,ble->de", d_attention, mixed[..., q_cols:]).astype(BF16)
        d_pair, gate_near, up_plane, out_right = together(d_pair, gate_near, up_plane, out_right)
        out_sum = dot("bld,ble->de", d_attention, mixed[..., :q_cols])
        out_sum = (out_sum + swap(out_right).astype(F32)).astype(BF16)
        out_sum = sum_of(out_sum.reshape(planes, depths, rows_in, q_cols), "fsdp")
        side = (back_blocks + 1) * half_len
        d_mine = d_pair[:, :side] + swap(d_pair[:, side:].astype(BF16)).astype(F32)
        d_kv = d_mine[:, :half_len]
        for back in range(1, back_blocks + 1):
            piece = d_mine[:, back * half_len : (back + 1) * half_len].astype(BF16)
            d_kv = d_kv + shift(piece, -back).astype(F32)
        d_kv, out_sum, up_plane = together(d_kv, out_sum, up_plane)
        out_sum = sum_of(out_sum, "ctx")
        up_near = scatter_depth(up_plane)

        def rotate_query(value, gain):
            return rope_normed(value, gain, cos_heads, sin_heads)

        def rotate_key(value, gain):
            return rope_normed(value, gain, cos, sin)

        d_query, d_gain_query = jax.vjp(rotate_query, query_full, gain_query)[1](d_query_rot)
        d_query = d_query.astype(BF16).reshape(batch, half_len, 2 * q_cols)
        d_key, d_gain_key = jax.vjp(rotate_key, key_full, gain_key)[1](d_kv[..., :HEAD_DIM])
        d_key = d_key.astype(BF16)
        d_value = d_kv[..., HEAD_DIM:].astype(BF16)
        d_left = jnp.concatenate(
            [d_query[..., :q_cols], jnp.where(first_core, d_key, d_value)], axis=-1
        )
        d_right = jnp.concatenate(
            [d_query[..., q_cols:], jnp.where(first_core, d_value, d_key)], axis=-1
        )
        first_left = dot("bld,ble->de", h1, d_left)
        first_right = dot("bld,ble->de", h1, d_right)
        d_h1 = dot("ble,de->bld", d_left, first_own) + dot("ble,de->bld", d_right, first_other)
        d_input_norm, d_gain_input = jax.vjp(normed, x, gain_input)[1](d_h1)
        d_x = d_middle + d_input_norm
        input_grads.append(d_x.reshape(hi - lo, seqs, half_len, width))
        gain_grads = (d_gain_input, d_gain_attention, d_gain_feed, d_gain_feed_out)
        gain_grads = gain_grads + (d_gain_query, d_gain_key)
        now = (down_near, gate_near, up_near, out_sum, first_left, first_right)
        now = now + gain_grads
        grads = now if grads is None else tuple(a + b for a, b in zip(grads, now))

    down_near, gate_near, up_near, out_sum, first_left, first_right = grads[:6]
    gain_grads = grads[6:]

    gain_sums = jnp.concatenate([grad.reshape(chunks, -1) for grad in gain_grads], axis=-1)
    gain_sums = jnp.pad(gain_sums, ((0, 0), (0, first_cols - gain_sums.shape[1])))
    gain_sums = jnp.pad(gain_sums[:, None], ((0, 0), (0, 7), (0, 0)))
    first_left, first_right = (
        jnp.concatenate([grad.reshape(chunks, rows_in, first_cols), gain_sums], axis=1)
        for grad in (first_left, first_right)
    )
    last = (first_left + swap(first_right.astype(BF16)).astype(F32)).astype(BF16)
    last = sum_of(last.reshape((planes, depths) + last.shape[1:]), "fsdp")
    last, gate_near, up_near, down_near = together(last, gate_near, up_near, down_near)
    last = sum_of(last, "ctx")
    feed_grads = jnp.stack([gate_near, up_near, down_near], axis=2)
    feed_grads = trade_apart(feed_grads.reshape(4, 3, rows_in, units))
    feed_grads = feed_grads.astype(F32).transpose(1, 2, 0, 3)
    feed_grads = feed_grads.reshape(3, rows_in, 4 * units)[:, :, : 4 * units - spare]
    out_gate, out_up, out_down = feed_grads[0], feed_grads[1], feed_grads[2].T
    out_out = out_sum.T
    out_query = last[:rows_in, :q_cols]
    out_kv = last[:rows_in, q_cols:]
    gains_out = last[rows_in]
    kv_other = swap(out_kv)
    out_key = jnp.where(first_core, out_kv, kv_other)
    out_value = jnp.where(first_core, kv_other, out_kv)
    pieces = [gains_out[lo:hi] for lo, hi in zip(cuts, ends)]

    return (
        jnp.concatenate(outputs, axis=0),
        jnp.concatenate(input_grads, axis=0),
        pieces[0],
        out_query,
        out_key,
        out_value,
        pieces[4],
        pieces[5],
        out_out,
        pieces[1],
        pieces[2],
        out_gate,
        out_up,
        out_down,
        pieces[3],
    )


def solution(mesh):
    both = ("fsdp", "ctx")
    return jax.shard_map(
        local,
        mesh=mesh,
        in_specs=(
            P(None, "fsdp", "ctx", None),
            P(None, "fsdp", "ctx"),
            P(None, "fsdp", "ctx", None),
            P(both),
            P(both, "tp"),
            P(both, None),
            P(both, None),
            P(both),
            P(both),
            P("tp", both),
            P(both),
            P(both),
            P(both, "tp"),
            P(both, "tp"),
            P("tp", both),
            P(both),
        ),
        out_specs=(
            P(None, "fsdp", ("ctx", "tp"), None),
            P(None, "fsdp", ("ctx", "tp"), None),
            P(both),
            P(both, "tp"),
            P(both, None),
            P(both, None),
            P(both),
            P(both),
            P("tp", both),
            P(both),
            P(both),
            P(both, "tp"),
            P(both, "tp"),
            P("tp", both),
            P(both),
        ),
        check_vma=False,
    )
```

```python
import jax
import jax.numpy as jnp
from jax import lax
from jax.experimental import pallas as pl
from jax.experimental.pallas import tpu as pltpu
from jax.sharding import PartitionSpec as P

HEAD_DIM = 256
WINDOW = 512

EPSILON = 1e-06
ROPE_BASE = 10000.0
SCORE_SCALE = 0.0625
MASKED = -1e30

SEGMENT_NUMBERS = 10

F32 = jnp.float32
BF16 = jnp.bfloat16


def dot(spec, left, right):
    return jnp.einsum(spec, left, right, preferred_element_type=F32)


def normed(values, gain):
    return values * lax.rsqrt(jnp.mean(values * values, axis=-1, keepdims=True) + EPSILON) * gain


def rotations(offsets, depth):
    middle = depth // 2
    inverse = ROPE_BASE ** (-2.0 * jnp.arange(middle, dtype=F32) / depth)
    angle_grid = offsets[..., None] * inverse
    return (jnp.cos(angle_grid), jnp.sin(angle_grid))


GELU_SCALE = 0.7978845608028654
GELU_CUBE = 0.044715


def feed_forward(rows, gate_w, up_w, down_w):
    z = dot("td,du->tu", rows, gate_w)
    up = dot("td,du->tu", rows, up_w)
    square = z * z
    t = jnp.tanh(GELU_SCALE * z * (1.0 + GELU_CUBE * square))
    half_one = 0.5 * (1.0 + t)
    gelu = z * half_one
    slope = half_one + 0.5 * z * (1.0 - t * t) * GELU_SCALE * (1.0 + 3.0 * GELU_CUBE * square)
    hidden = (gelu * up).astype(BF16)
    part = dot("tu,du->td", hidden, down_w).astype(BF16)
    return hidden, gelu.astype(BF16), (up * slope).astype(BF16), part


def contract(left, right, left_dim, right_dim):
    dims = (((left_dim,), (right_dim,)), ((), ()))
    return lax.dot_general(left, right, dims, preferred_element_type=F32)


def normed_back(values, gain, grad):
    scale = lax.rsqrt(jnp.mean(values * values, axis=-1, keepdims=True) + EPSILON)
    inner = gain * grad
    along = jnp.mean(values * inner, axis=-1, keepdims=True)
    d_values = scale * inner - values * (scale * scale * scale) * along
    return d_values, jnp.sum(grad * values * scale, axis=0, keepdims=True)


def turned(values, cosines, sines):
    middle = values.shape[-1] // 2
    first, second = values[:, :middle], values[:, middle:]
    return jnp.concatenate(
        [first * cosines - second * sines, second * cosines + first * sines], axis=-1
    )


def turned_back(values, cosines, sines):
    return turned(values, cosines, -sines)


def head(at):
    return slice(at * HEAD_DIM, (at + 1) * HEAD_DIM)


def project_kernel(core, x, own, other, gain_in, gain_q, gain_k, cosines, sines, *outs):
    h1, raw, query_rot, key_full, pair = outs
    cos, sin = cosines[...], sines[...]
    low = normed(x[...].astype(F32), gain_in[...]).astype(BF16)
    h1[...] = low
    q_cols = own.shape[1] - HEAD_DIM
    left, right = contract(low, own[...], 1, 0), contract(low, other[...], 1, 0)
    first = core[0] == 0
    key = jnp.where(first, left[:, q_cols:], right[:, q_cols:])
    value = jnp.where(first, right[:, q_cols:], left[:, q_cols:])
    key_full[...] = key
    pair[:, :HEAD_DIM] = turned(normed(key, gain_k[...]), cos, sin).astype(BF16)
    pair[:, HEAD_DIM:] = value.astype(BF16)
    raw[:, :q_cols] = left[:, :q_cols]
    raw[:, q_cols:] = right[:, :q_cols]
    for at in range(raw.shape[1] // HEAD_DIM):
        turn = turned(normed(raw[:, head(at)], gain_q[...]), cos, sin)
        query_rot[:, head(at)] = turn.astype(BF16)


def allowed_pairs(tokens_at, keys_at, starts):
    t, u, begin = tokens_at[...], keys_at[...], starts[...]
    return (u <= t) & (t - u < WINDOW) & (u >= begin)


def probabilities(query, keys, allowed):
    scores = jnp.where(allowed, contract(query, keys, 1, 1) * SCORE_SCALE, MASKED)
    lifted = jnp.exp(scores - jnp.max(scores, axis=-1, keepdims=True))
    return lifted / jnp.sum(lifted, axis=-1, keepdims=True)


def attend_kernel(tokens_at, keys_at, starts, query_rot, seen, x, own, other, gain_a, gain_f, *outs):
    mixed, attention, middle, h2 = outs
    allowed = allowed_pairs(tokens_at, keys_at, starts)
    keys, values = seen[0, :, :HEAD_DIM], seen[0, :, HEAD_DIM:]
    for at in range(query_rot.shape[1] // HEAD_DIM):
        prob = probabilities(query_rot[:, head(at)], keys, allowed).astype(BF16)
        mixed[:, head(at)] = contract(prob, values, 1, 0).astype(BF16)
    q_cols = own.shape[1]
    result = contract(mixed[:, :q_cols], own[...], 1, 1)
    result = result + contract(mixed[:, q_cols:], other[...], 1, 1)
    attention[...] = result
    mid = x[...].astype(F32) + normed(result, gain_a[...])
    middle[...] = mid
    h2[...] = normed(mid, gain_f[...]).astype(BF16)


def attend_back_kernel(tokens_at, keys_at, starts, query_rot, seen, own, other, *rest):
    gain_a, gain_f, gain_q, cosines, sines, parts, middle, attention, dy, raw = rest[:10]
    d_middle, d_attention, d_query, d_near, d_far, d_gains, d_gain_q, d_mixed = rest[10:]

    @pl.when(pl.program_id(0) == 0)
    def _():
        d_gains[...] = jnp.zeros_like(d_gains)
        d_gain_q[...] = jnp.zeros_like(d_gain_q)

    d_h2 = parts[0].astype(F32)
    for at in range(1, parts.shape[0]):
        d_h2 = d_h2 + parts[at].astype(F32)
    d_mid, d_gain_f = normed_back(middle[...], gain_f[...], d_h2)
    d_mid = d_mid + dy[...].astype(F32)
    d_middle[...] = d_mid
    d_att, d_gain_a = normed_back(attention[...], gain_a[...], d_mid)
    d_gains[0:1, :] += d_gain_f
    d_gains[1:2, :] += d_gain_a
    d_att = d_att.astype(BF16)
    d_attention[...] = d_att
    q_cols = own.shape[1]
    d_mixed[:, :q_cols] = contract(d_att, own[...], 1, 0).astype(BF16)
    d_mixed[:, q_cols:] = contract(d_att, other[...], 1, 0).astype(BF16)
    allowed = allowed_pairs(tokens_at, keys_at, starts)
    keys, values = seen[0, :, :HEAD_DIM], seen[0, :, HEAD_DIM:]
    d_keys = jnp.zeros(keys.shape, F32)
    d_values = jnp.zeros(keys.shape, F32)
    for at in range(query_rot.shape[1] // HEAD_DIM):
        query, d_mix = query_rot[:, head(at)], d_mixed[:, head(at)]
        prob = probabilities(query, keys, allowed)
        d_prob = contract(d_mix, values, 1, 1)
        delta = jnp.sum(prob * d_prob, axis=-1, keepdims=True)
        d_raw = (prob * (d_prob - delta) * SCORE_SCALE).astype(BF16)
        d_keys = d_keys + contract(d_raw, query, 0, 0)
        d_values = d_values + contract(prob.astype(BF16), d_mix, 0, 0)
        d_rot = turned_back(contract(d_raw, keys, 1, 0), cosines[...], sines[...])
        d_full, d_gain = normed_back(raw[:, head(at)], gain_q[...], d_rot)
        d_query[:, head(at)] = d_full.astype(BF16)
        d_gain_q[0:1, :] += d_gain
    side = keys.shape[0] // 2
    d_near[0, :, :HEAD_DIM] = d_keys[:side]
    d_near[0, :, HEAD_DIM:] = d_values[:side]
    d_far[0, :, :HEAD_DIM] = d_keys[side:].astype(BF16)
    d_far[0, :, HEAD_DIM:] = d_values[side:].astype(BF16)


def project_back_kernel(core, d_kv, key_full, d_query, h1, x, own, other, *rest):
    gain_in, gain_k, cosines, sines, d_middle = rest[:5]
    input_grad, kv_left, kv_right, d_gain_in, d_gain_k = rest[5:]
    d_rot = turned_back(d_kv[:, :HEAD_DIM], cosines[...], sines[...])
    d_key, d_gain = normed_back(key_full[...], gain_k[...], d_rot)
    d_gain_k[...] = jnp.broadcast_to(d_gain, d_gain_k.shape)
    d_key, d_value = d_key.astype(BF16).astype(F32), d_kv[:, HEAD_DIM:]
    first = core[0] == 0
    d_left = jnp.where(first, d_key, d_value).astype(BF16)
    d_right = jnp.where(first, d_value, d_key).astype(BF16)
    low = h1[...]
    kv_left[...] = contract(low, d_left, 0, 0)
    kv_right[...] = contract(low, d_right, 0, 0)
    q_cols = own.shape[1] - HEAD_DIM
    d_h1 = contract(d_query[:, :q_cols], own[:, :q_cols], 1, 1)
    d_h1 = d_h1 + contract(d_query[:, q_cols:], other[:, :q_cols], 1, 1)
    d_h1 = d_h1 + contract(d_left, own[:, q_cols:], 1, 1)
    d_h1 = d_h1 + contract(d_right, other[:, q_cols:], 1, 1)
    d_x, d_gain = normed_back(x[...].astype(F32), gain_in[...], d_h1)
    input_grad[...] = d_middle[...] + d_x
    d_gain_in[...] = jnp.broadcast_to(d_gain, d_gain_in.shape)


def feed_norm_kernel(gain, parts, middle, dy, layer_out, d_feed, d_gain):
    feed = parts[0].astype(F32)
    for at in range(1, parts.shape[0]):
        feed = feed + parts[at].astype(F32)
    layer_out[...] = (middle[...] + normed(feed, gain[...])).astype(BF16)
    d_values, d_row = normed_back(feed, gain[...], dy[...].astype(F32))
    d_feed[...] = d_values.astype(BF16)
    d_gain[...] = jnp.broadcast_to(d_row, d_gain.shape)


def run(kernel, outs, *values, grid=None, in_specs=None, out_specs=None, scratch=()):
    more = {}
    if grid is not None:
        more = dict(grid=grid, in_specs=in_specs, out_specs=out_specs)
    elif in_specs is not None:
        more = dict(in_specs=in_specs)
    return pl.pallas_call(
        kernel,
        out_shape=[jax.ShapeDtypeStruct(shape, dtype) for shape, dtype in outs],
        scratch_shapes=list(scratch),
        compiler_params=pltpu.CompilerParams(vmem_limit_bytes=48 * 1024 * 1024),
        cost_estimate=pl.CostEstimate(flops=1, bytes_accessed=1, transcendentals=0),
        **more,
    )(*values)


def in_vmem(count):
    return [pl.BlockSpec(memory_space=pltpu.VMEM)] * count


def rows_spec(rows, width):
    return pl.BlockSpec((rows, width), lambda i: (i, 0))


def same_spec(*shape):
    return pl.BlockSpec(shape, lambda i: (0,) * len(shape))


def swap(value):
    return lax.ppermute(value, "tp", [(0, 1), (1, 0)])


BOTH = ("fsdp", "ctx")


def cross(value, mask):
    count = lax.axis_size("fsdp") * lax.axis_size("ctx")
    return lax.ppermute(value, BOTH, [(i, i ^ mask) for i in range(count)])


def shift(value, step):
    count = lax.axis_size("ctx")
    pairs = [(i, i + step) for i in range(count) if 0 <= i + step < count]
    return lax.ppermute(value, "ctx", pairs)


def together(*values):
    return lax.optimization_barrier(values)


def placed(own, other, bit, dim):
    first = jnp.where(bit == 0, own, other)
    second = jnp.where(bit == 0, other, own)
    return jnp.concatenate([first, second], axis=dim)


def parted(value, bit, dim):
    zero = lax.index_in_dim(value, 0, axis=dim, keepdims=False)
    one = lax.index_in_dim(value, 1, axis=dim, keepdims=False)
    return jnp.where(bit == 0, zero, one), jnp.where(bit == 0, one, zero)


def copies_to(value, axis):
    count = lax.axis_size(axis)
    return lax.all_to_all(jnp.broadcast_to(value[None], (count,) + value.shape), axis, 0, 0)


def gather_rows(value):
    return copies_to(copies_to(value, "ctx"), "fsdp")


def sum_of(parts, axis):
    return jnp.sum(lax.all_to_all(parts.astype(BF16), axis, 0, 0).astype(F32), axis=0)


def scatter_rows(value):
    return sum_of(sum_of(value, "fsdp"), "ctx")


def near_groups():
    planes, depths = lax.axis_size("fsdp"), lax.axis_size("ctx")
    return [
        [(f + x) * depths + c + z for x in (0, 1) for z in (0, 1)]
        for f in range(0, planes, 2)
        for c in range(0, depths, 2)
    ]


def trade(value):
    return lax.all_to_all(value, BOTH, 0, 0, axis_index_groups=near_groups())


def trade_apart(value):
    depths = lax.axis_size("ctx")
    x_bit, z_bit = lax.axis_index("fsdp") & 1, lax.axis_index("ctx") & 1
    low, high = parted(value.reshape((2, 2) + value.shape[1:]), x_bit, 0)
    (p0, p1), (p2, p3) = parted(low, z_bit, 0), parted(high, z_bit, 0)
    p1, p2, p3 = cross(p1, 1), cross(p2, depths), cross(p3, depths | 1)
    low = placed(p0[None], p1[None], z_bit, 0)
    high = placed(p2[None], p3[None], z_bit, 0)
    return placed(low[None], high[None], x_bit, 0).reshape(value.shape)


def far_bits():
    planes, depths = lax.axis_size("fsdp"), lax.axis_size("ctx")
    f_place, c_place = lax.axis_index("fsdp"), lax.axis_index("ctx")
    f_count, c_count = (planes - 1).bit_length(), (depths - 1).bit_length()
    c_bits = [(1 << k, (c_place >> k) & 1) for k in range(c_count - 1, 0, -1)]
    f_bits = [(depths << k, (f_place >> k) & 1) for k in range(f_count - 1, 0, -1)]
    return c_bits, f_bits


def gather_depth(value):
    c_bits, _ = far_bits()
    for mask, bit in c_bits[::-1]:
        value = placed(value, cross(value, mask), bit, 1)
    return value


def gather_plane(value):
    _, f_bits = far_bits()
    for mask, bit in f_bits[::-1]:
        value = placed(value, cross(value, mask), bit, 0)
    return value


def scatter_plane(value):
    _, f_bits = far_bits()
    for mask, bit in f_bits:
        halves = value.reshape((2, value.shape[0] // 2) + value.shape[1:])
        mine, other = parted(halves, bit, 0)
        value = (mine.astype(F32) + cross(other, mask).astype(F32)).astype(BF16)
    return value


def scatter_depth(value):
    c_bits, _ = far_bits()
    for mask, bit in c_bits:
        halves = value.reshape((2, 2, value.shape[1] // 2) + value.shape[2:])
        mine, other = parted(halves, bit, 1)
        value = (mine.astype(F32) + cross(other, mask).astype(F32)).astype(BF16)
    return value


def spread_start(rows):
    mine = trade(jnp.broadcast_to(rows[None], (4,) + rows.shape))
    return mine.reshape((-1,) + rows.shape[1:])


def spread(rows):
    mine = spread_start(rows)
    return jnp.concatenate([mine, swap(mine)], axis=0)


def collect_start(part):
    half = part.shape[0] // 2
    own = part[:half].astype(F32) + swap(part[half:]).astype(F32)
    return own.astype(BF16).reshape(4, half // 4, part.shape[1])


def local(
    tokens,
    segments,
    cotangent,
    norm_input,
    query_weight,
    key_weight,
    value_weight,
    norm_query,
    norm_key,
    out_weight,
    norm_attention,
    norm_feed,
    gate_weight,
    up_weight,
    down_weight,
    norm_feed_out,
):
    micros, seqs, block_len, width = tokens.shape
    planes = lax.axis_size("fsdp")
    depths = lax.axis_size("ctx")
    chunks = planes * depths
    ctx_place = lax.axis_index("ctx")
    tp_place = lax.axis_index("tp")
    first_core = tp_place == 0
    half_len = block_len // lax.axis_size("tp")
    back_blocks = -(-WINDOW // block_len)
    rows_in = norm_input.shape[0]
    small = norm_query.shape[0]
    heads_half = query_weight.shape[1] // HEAD_DIM
    q_cols = query_weight.shape[1]
    units = -(-gate_weight.shape[1] // (4 * 128)) * 128
    spare = 4 * units - gate_weight.shape[1]
    numbers = jnp.arange(SEGMENT_NUMBERS, dtype=jnp.int32)
    counts = jnp.sum((segments[..., None] == numbers).astype(F32), axis=2).astype(BF16)
    kv_shard = jnp.where(first_core, key_weight, value_weight)
    gains = (norm_input, norm_attention, norm_feed, norm_feed_out, norm_query, norm_key)
    gain_sizes = [gain.shape[0] for gain in gains]
    first_cols = q_cols + HEAD_DIM

    def row(value):
        return jnp.pad(value[None], ((0, 0), (0, first_cols - value.shape[0])))

    more = [row(gain) for gain in gains] + [row(counts.reshape(-1))]
    more = more + [jnp.zeros((1, first_cols), BF16)]
    first_pack = jnp.concatenate([query_weight, kv_shard], axis=1)
    first_pack = jnp.concatenate([first_pack] + more, axis=0)
    first_pack = jnp.broadcast_to(first_pack[None], (depths,) + first_pack.shape)
    first_pack, gate_weight, up_weight, down_weight, out_weight = together(
        first_pack, gate_weight, up_weight, down_weight, out_weight
    )
    first_pack = lax.all_to_all(first_pack, "ctx", 0, 0)

    feed_parts = jnp.stack([gate_weight, up_weight, down_weight.T], axis=0)
    feed_parts = jnp.pad(feed_parts, ((0, 0), (0, 0), (0, spare)))
    feed_parts = feed_parts.reshape(3, rows_in, 4, units).transpose(2, 0, 1, 3)
    feed_parts = trade_apart(feed_parts)
    first_pack, feed_parts = together(first_pack, feed_parts)
    counts_all = first_pack[:, rows_in + len(gains), : counts.size].astype(F32)
    counts_all = jnp.sum(counts_all, axis=0).reshape(counts.shape)

    feed_parts = feed_parts.reshape(2, 2, 3, rows_in, units)
    gate_near, up_near, down_near = (feed_parts[:, :, which] for which in range(3))
    gate_deep = gather_depth(gate_near)
    first_pack = copies_to(first_pack, "fsdp")
    first_pack, gate_deep, up_near, down_near, out_pack = together(
        first_pack, gate_deep, up_near, down_near, out_weight.T
    )

    first_pack = first_pack.reshape(chunks, rows_in + 8, first_cols)
    first_own = first_pack[:, :rows_in].reshape(width, first_cols)
    first_other = swap(first_own)
    gain_input, gain_attention, gain_feed, gain_feed_out, gain_query, gain_key = (
        first_pack[:, rows_in + at, :size].astype(F32).reshape(-1)
        for at, size in enumerate(gain_sizes)
    )
    out_pack = copies_to(out_pack, "ctx")
    up_deep = gather_depth(up_near)
    gate_w = gather_plane(gate_deep).reshape(width, units)

    half_at = tp_place * half_len
    seg_half = lax.dynamic_slice_in_dim(segments, half_at, half_len, 2)
    earlier = numbers < seg_half[..., None]
    starts = jnp.sum(jnp.where(earlier, counts_all[:, :, None, :], 0.0), axis=-1)
    starts = starts.astype(jnp.int32)
    token_place = ctx_place * block_len + half_at + jnp.arange(half_len, dtype=jnp.int32)
    cosines, sines = rotations((token_place - starts).astype(F32), HEAD_DIM)
    within = jnp.arange(half_len, dtype=jnp.int32)
    key_place = jnp.concatenate(
        [
            (ctx_place - back) * block_len + side * half_len + within
            for side in (tp_place, 1 - tp_place)
            for back in range(back_blocks + 1)
        ]
    )

    batch = micros * seqs
    rows = batch * half_len
    x_low = lax.dynamic_slice_in_dim(tokens, half_at, half_len, 2).reshape(rows, width)
    dy_low = lax.dynamic_slice_in_dim(cotangent, half_at, half_len, 2).reshape(rows, width)
    cos, sin = cosines.reshape(rows, -1), sines.reshape(rows, -1)
    starts = starts.reshape(rows, 1)
    core = tp_place.reshape(1)
    gains_wide = [
        gain[None]
        for gain in (gain_input, gain_attention, gain_feed, gain_feed_out, gain_query, gain_key)
    ]
    g_in, g_att, g_feed, g_out, g_query, g_key = gains_wide
    smem = [pl.BlockSpec(memory_space=pltpu.SMEM)]
    wide, cols_all = (rows, width), 2 * q_cols

    h1, query_raw, query_rot, key_full, pair = run(
        project_kernel,
        [(wide, BF16), ((rows, cols_all), F32), ((rows, cols_all), BF16)]
        + [((rows, HEAD_DIM), F32), ((rows, 2 * HEAD_DIM), BF16)],
        core, x_low, first_own, first_other, g_in, g_query, g_key, cos, sin,
        in_specs=smem + in_vmem(8),
    )
    pair, up_deep, gate_w, out_pack, down_near = together(
        pair, up_deep, gate_w, out_pack, down_near
    )
    down_deep = gather_depth(down_near)
    up_w = gather_plane(up_deep).reshape(width, units)
    out_own = copies_to(out_pack, "fsdp").reshape(width, q_cols)
    pair = pair.reshape(batch, half_len, 2 * HEAD_DIM)
    mine = jnp.concatenate(
        [pair] + [shift(pair, back) for back in range(1, back_blocks + 1)], axis=1
    )
    seen = jnp.concatenate([mine, swap(mine)], axis=1)
    seen, up_w, out_own, down_deep = together(seen, up_w, out_own, down_deep)
    out_other = swap(out_own)
    down_w = gather_plane(down_deep).reshape(width, units)
    span = seen.shape[1]
    token_rows, key_cols = token_place[:, None], key_place[None]
    place_specs = [same_spec(half_len, 1), same_spec(1, span), rows_spec(half_len, 1)]
    seen_spec = pl.BlockSpec((1, span, 2 * HEAD_DIM), lambda i: (i, 0, 0))
    row_spec, col_spec = rows_spec(half_len, width), rows_spec(half_len, cols_all)
    out_specs = [same_spec(width, q_cols)] * 2
    mixed, attention, middle, h2 = run(
        attend_kernel,
        [((rows, cols_all), BF16), (wide, F32), (wide, F32), (wide, BF16)],
        token_rows, key_cols, starts, query_rot, seen, x_low, out_own, out_other, g_att, g_feed,
        grid=(batch,),
        in_specs=place_specs
        + [col_spec, seen_spec, row_spec]
        + out_specs
        + [same_spec(1, width)] * 2,
        out_specs=[col_spec] + [row_spec] * 3,
    )

    h2_mine, down_w = together(spread_start(h2), down_w)
    h2_all = jnp.concatenate([h2_mine, swap(h2_mine)], axis=0)
    hidden, by_up, by_gate, part = feed_forward(h2_all, gate_w, up_w, down_w)
    feed_parts = trade(collect_start(part))
    layer_out, d_feed, d_gain_out = run(
        feed_norm_kernel,
        [(wide, BF16), (wide, BF16), ((8, width), F32)],
        g_out, feed_parts, middle, dy_low,
    )
    d_feed_all = spread(d_feed)
    grad_down = dot("td,tu->du", d_feed_all, hidden).astype(BF16)
    d_feed_all, grad_down = together(d_feed_all, grad_down)
    down_plane = scatter_plane(grad_down.reshape(planes, depths, rows_in, units))
    d_hidden = dot("td,du->tu", d_feed_all, down_w)
    d_gate = (d_hidden * by_gate.astype(F32)).astype(BF16)
    d_up = (d_hidden * by_up.astype(F32)).astype(BF16)
    grad_gate = dot("td,tu->du", h2_all, d_gate).astype(BF16)
    d_gate, d_up, grad_gate, down_plane = together(d_gate, d_up, grad_gate, down_plane)
    gate_plane = scatter_plane(grad_gate.reshape(planes, depths, rows_in, units))
    down_near = scatter_depth(down_plane)
    grad_up = dot("td,tu->du", h2_all, d_up).astype(BF16)
    d_h2_part = dot("tu,du->td", d_gate, gate_w) + dot("tu,du->td", d_up, up_w)
    d_h2_part, grad_up, gate_plane, down_near = together(
        d_h2_part.astype(BF16), grad_up, gate_plane, down_near
    )
    d_h2_part = collect_start(d_h2_part)
    gate_near = scatter_depth(gate_plane)
    up_plane = scatter_plane(grad_up.reshape(planes, depths, rows_in, units))
    d_h2_parts = trade(d_h2_part)
    d_h2_parts, gate_near, up_plane = together(d_h2_parts, gate_near, up_plane)
    up_near = scatter_depth(up_plane)

    side = span // 2
    near_spec = pl.BlockSpec((1, side, 2 * HEAD_DIM), lambda i: (i, 0, 0))
    turn_spec = rows_spec(half_len, HEAD_DIM // 2)
    d_middle, d_attention, d_query, d_near, d_far, d_gains, d_gain_query = run(
        attend_back_kernel,
        [(wide, F32), (wide, BF16), ((rows, cols_all), BF16)]
        + [((batch, side, 2 * HEAD_DIM), F32), ((batch, side, 2 * HEAD_DIM), BF16)]
        + [((8, width), F32), ((8, HEAD_DIM), F32)],
        token_rows, key_cols, starts, query_rot, seen, out_own, out_other,
        g_att, g_feed, g_query, cos, sin, d_h2_parts, middle, attention, dy_low, query_raw,
        grid=(batch,),
        in_specs=place_specs
        + [col_spec, seen_spec]
        + out_specs
        + [same_spec(1, width)] * 2
        + [same_spec(1, HEAD_DIM), turn_spec, turn_spec]
        + [pl.BlockSpec((4, half_len, width), lambda i: (0, i, 0))]
        + [row_spec] * 3
        + [col_spec],
        out_specs=[row_spec, row_spec, col_spec, near_spec, near_spec]
        + [same_spec(8, width), same_spec(8, HEAD_DIM)],
        scratch=[pltpu.VMEM((half_len, cols_all), BF16)],
    )
    d_near, d_far, d_query, d_attention, up_near = together(
        d_near, d_far, d_query, d_attention, up_near
    )
    feed_grads = jnp.stack([gate_near, up_near, down_near], axis=2)
    feed_grads = trade_apart(feed_grads.reshape(4, 3, rows_in, units))
    d_mine = d_near + swap(d_far).astype(F32)
    both_left = jnp.concatenate(
        [dot("td,te->de", d_attention, mixed[:, :q_cols])]
        + [dot("td,te->de", h1, d_query[:, :q_cols])],
        axis=1,
    )
    both_right = jnp.concatenate(
        [dot("td,te->de", d_attention, mixed[:, q_cols:]).astype(BF16)]
        + [dot("td,te->de", h1, d_query[:, q_cols:]).astype(BF16)],
        axis=1,
    )
    both = (both_left + swap(both_right).astype(F32)).astype(BF16)
    both = sum_of(both.reshape(planes, depths, rows_in, cols_all), "fsdp")
    d_kv = d_mine[:, :half_len]
    for back in range(1, back_blocks + 1):
        piece = d_mine[:, back * half_len : (back + 1) * half_len].astype(BF16)
        d_kv = d_kv + shift(piece, -back).astype(F32)
    d_kv, both, feed_grads = together(d_kv, both, feed_grads)
    both = sum_of(both, "ctx")
    input_grad, kv_left, kv_right, d_gain_in, d_gain_key = run(
        project_back_kernel,
        [(wide, F32), ((width, HEAD_DIM), F32), ((width, HEAD_DIM), F32)]
        + [((8, width), F32), ((8, HEAD_DIM), F32)],
        core, d_kv.reshape(rows, 2 * HEAD_DIM), key_full, d_query, h1, x_low,
        first_own, first_other, g_in, g_key, cos, sin, d_middle,
        in_specs=smem + in_vmem(12),
    )
    kv_left, kv_right, both = together(kv_left, kv_right, both)
    gain_grads = (d_gain_in[0], d_gains[1], d_gains[0], d_gain_out[0])
    gain_grads = gain_grads + (d_gain_query[0], d_gain_key[0])

    gain_sums = [
        jnp.pad(grad.reshape(chunks, 1, -1), ((0, 0), (0, 0), (0, HEAD_DIM - size)))
        for grad, size in zip(gain_grads, gain_sizes)
    ]
    gain_sums = gain_sums + [jnp.zeros((chunks, 8 - len(gains), HEAD_DIM), F32)]
    kv_left, kv_right = (
        jnp.concatenate([grad.reshape(chunks, rows_in, HEAD_DIM)] + gain_sums, axis=1)
        for grad in (kv_left, kv_right)
    )
    last = (kv_left + swap(kv_right.astype(BF16)).astype(F32)).astype(BF16)
    out_out, out_query = both[:, :q_cols].T, both[:, q_cols:]
    last = sum_of(sum_of(last.reshape((planes, depths) + last.shape[1:]), "fsdp"), "ctx")
    feed_grads = feed_grads.astype(F32).transpose(1, 2, 0, 3)
    feed_grads = feed_grads.reshape(3, rows_in, 4 * units)[:, :, : 4 * units - spare]
    out_gate, out_up, out_down = feed_grads[0], feed_grads[1], feed_grads[2].T
    out_kv = last[:rows_in]
    kv_other = swap(out_kv)
    out_key = jnp.where(first_core, out_kv, kv_other)
    out_value = jnp.where(first_core, kv_other, out_kv)
    pieces = [last[rows_in + at, :size] for at, size in enumerate(gain_sizes)]

    return (
        layer_out.reshape(micros, seqs, half_len, width),
        input_grad.reshape(micros, seqs, half_len, width),
        pieces[0],
        out_query,
        out_key,
        out_value,
        pieces[4],
        pieces[5],
        out_out,
        pieces[1],
        pieces[2],
        out_gate,
        out_up,
        out_down,
        pieces[3],
    )


def solution(mesh):
    both = ("fsdp", "ctx")
    return jax.shard_map(
        local,
        mesh=mesh,
        in_specs=(
            P(None, "fsdp", "ctx", None),
            P(None, "fsdp", "ctx"),
            P(None, "fsdp", "ctx", None),
            P(both),
            P(both, "tp"),
            P(both, None),
            P(both, None),
            P(both),
            P(both),
            P("tp", both),
            P(both),
            P(both),
            P(both, "tp"),
            P(both, "tp"),
            P("tp", both),
            P(both),
        ),
        out_specs=(
            P(None, "fsdp", ("ctx", "tp"), None),
            P(None, "fsdp", ("ctx", "tp"), None),
            P(both),
            P(both, "tp"),
            P(both, None),
            P(both, None),
            P(both),
            P(both),
            P("tp", both),
            P(both),
            P(both),
            P(both, "tp"),
            P(both, "tp"),
            P("tp", both),
            P(both),
        ),
        check_vma=False,
    )
```

```python
import jax
import jax.numpy as jnp
from jax import lax
from jax.experimental import pallas as pl
from jax.experimental.pallas import tpu as pltpu
from jax.sharding import PartitionSpec as P

HEAD_DIM = 256
WINDOW = 512

EPSILON = 1e-06
ROPE_BASE = 10000.0
SCORE_SCALE = 0.0625
MASKED = -1e30

SEGMENT_NUMBERS = 10

F32 = jnp.float32
BF16 = jnp.bfloat16


def dot(spec, left, right):
    return jnp.einsum(spec, left, right, preferred_element_type=F32)


def normed(values, gain):
    return values * lax.rsqrt(jnp.mean(values * values, axis=-1, keepdims=True) + EPSILON) * gain


def rotations(offsets, depth):
    middle = depth // 2
    inverse = ROPE_BASE ** (-2.0 * jnp.arange(middle, dtype=F32) / depth)
    angle_grid = offsets[..., None] * inverse
    return (jnp.cos(angle_grid), jnp.sin(angle_grid))


GELU_SCALE = 0.7978845608028654
GELU_CUBE = 0.044715


def feed_forward(rows, gate_w, up_w, down_w):
    z = dot("td,du->tu", rows, gate_w)
    up = dot("td,du->tu", rows, up_w)
    square = z * z
    t = jnp.tanh(GELU_SCALE * z * (1.0 + GELU_CUBE * square))
    half_one = 0.5 * (1.0 + t)
    gelu = z * half_one
    slope = half_one + 0.5 * z * (1.0 - t * t) * GELU_SCALE * (1.0 + 3.0 * GELU_CUBE * square)
    hidden = (gelu * up).astype(BF16)
    part = dot("tu,du->td", hidden, down_w).astype(BF16)
    return hidden, gelu.astype(BF16), (up * slope).astype(BF16), part


def contract(left, right, left_dim, right_dim):
    dims = (((left_dim,), (right_dim,)), ((), ()))
    return lax.dot_general(left, right, dims, preferred_element_type=F32)


def normed_back(values, gain, grad):
    scale = lax.rsqrt(jnp.mean(values * values, axis=-1, keepdims=True) + EPSILON)
    inner = gain * grad
    along = jnp.mean(values * inner, axis=-1, keepdims=True)
    d_values = scale * inner - values * (scale * scale * scale) * along
    return d_values, jnp.sum(grad * values * scale, axis=0, keepdims=True)


def turned(values, cosines, sines):
    middle = values.shape[-1] // 2
    first, second = values[:, :middle], values[:, middle:]
    return jnp.concatenate(
        [first * cosines - second * sines, second * cosines + first * sines], axis=-1
    )


def turned_back(values, cosines, sines):
    return turned(values, cosines, -sines)


def head(at):
    return slice(at * HEAD_DIM, (at + 1) * HEAD_DIM)


def project_kernel(core, x, own, other, gain_in, gain_q, gain_k, cosines, sines, *outs):
    h1, raw, query_rot, key_full, pair = outs
    cos, sin = cosines[...], sines[...]
    low = normed(x[...].astype(F32), gain_in[...]).astype(BF16)
    h1[...] = low
    q_cols = own.shape[1] - HEAD_DIM
    left, right = contract(low, own[...], 1, 0), contract(low, other[...], 1, 0)
    first = core[0] == 0
    key = jnp.where(first, left[:, q_cols:], right[:, q_cols:])
    value = jnp.where(first, right[:, q_cols:], left[:, q_cols:])
    key_full[...] = key
    pair[:, :HEAD_DIM] = turned(normed(key, gain_k[...]), cos, sin).astype(BF16)
    pair[:, HEAD_DIM:] = value.astype(BF16)
    raw[:, :q_cols] = left[:, :q_cols]
    raw[:, q_cols:] = right[:, :q_cols]
    for at in range(raw.shape[1] // HEAD_DIM):
        turn = turned(normed(raw[:, head(at)], gain_q[...]), cos, sin)
        query_rot[:, head(at)] = turn.astype(BF16)


def allowed_pairs(tokens_at, keys_at, starts):
    t, u, begin = tokens_at[...], keys_at[...], starts[...]
    return (u <= t) & (t - u < WINDOW) & (u >= begin)


def probabilities(query, keys, allowed):
    scores = jnp.where(allowed, contract(query, keys, 1, 1) * SCORE_SCALE, MASKED)
    lifted = jnp.exp(scores - jnp.max(scores, axis=-1, keepdims=True))
    return lifted / jnp.sum(lifted, axis=-1, keepdims=True)


def attend_kernel(tokens_at, keys_at, starts, query_rot, seen, x, own, other, gain_a, gain_f, *outs):
    mixed, attention, middle, h2 = outs
    allowed = allowed_pairs(tokens_at, keys_at, starts)
    keys, values = seen[0, :, :HEAD_DIM], seen[0, :, HEAD_DIM:]
    for at in range(query_rot.shape[1] // HEAD_DIM):
        prob = probabilities(query_rot[:, head(at)], keys, allowed).astype(BF16)
        mixed[:, head(at)] = contract(prob, values, 1, 0).astype(BF16)
    q_cols = own.shape[1]
    result = contract(mixed[:, :q_cols], own[...], 1, 1)
    result = result + contract(mixed[:, q_cols:], other[...], 1, 1)
    attention[...] = result
    mid = x[...].astype(F32) + normed(result, gain_a[...])
    middle[...] = mid
    h2[...] = normed(mid, gain_f[...]).astype(BF16)


def attend_back_kernel(tokens_at, keys_at, starts, query_rot, seen, own, other, *rest):
    gain_a, gain_f, gain_q, cosines, sines, parts, middle, attention, dy, raw = rest[:10]
    d_middle, d_attention, d_query, d_near, d_far, d_gains, d_gain_q, d_mixed = rest[10:]

    @pl.when(pl.program_id(0) == 0)
    def _():
        d_gains[...] = jnp.zeros_like(d_gains)
        d_gain_q[...] = jnp.zeros_like(d_gain_q)

    d_h2 = parts[0].astype(F32)
    for at in range(1, parts.shape[0]):
        d_h2 = d_h2 + parts[at].astype(F32)
    d_mid, d_gain_f = normed_back(middle[...], gain_f[...], d_h2)
    d_mid = d_mid + dy[...].astype(F32)
    d_middle[...] = d_mid
    d_att, d_gain_a = normed_back(attention[...], gain_a[...], d_mid)
    d_gains[0:1, :] += d_gain_f
    d_gains[1:2, :] += d_gain_a
    d_att = d_att.astype(BF16)
    d_attention[...] = d_att
    q_cols = own.shape[1]
    d_mixed[:, :q_cols] = contract(d_att, own[...], 1, 0).astype(BF16)
    d_mixed[:, q_cols:] = contract(d_att, other[...], 1, 0).astype(BF16)
    allowed = allowed_pairs(tokens_at, keys_at, starts)
    keys, values = seen[0, :, :HEAD_DIM], seen[0, :, HEAD_DIM:]
    d_keys = jnp.zeros(keys.shape, F32)
    d_values = jnp.zeros(keys.shape, F32)
    for at in range(query_rot.shape[1] // HEAD_DIM):
        query, d_mix = query_rot[:, head(at)], d_mixed[:, head(at)]
        prob = probabilities(query, keys, allowed)
        d_prob = contract(d_mix, values, 1, 1)
        delta = jnp.sum(prob * d_prob, axis=-1, keepdims=True)
        d_raw = (prob * (d_prob - delta) * SCORE_SCALE).astype(BF16)
        d_keys = d_keys + contract(d_raw, query, 0, 0)
        d_values = d_values + contract(prob.astype(BF16), d_mix, 0, 0)
        d_rot = turned_back(contract(d_raw, keys, 1, 0), cosines[...], sines[...])
        d_full, d_gain = normed_back(raw[:, head(at)], gain_q[...], d_rot)
        d_query[:, head(at)] = d_full.astype(BF16)
        d_gain_q[0:1, :] += d_gain
    side = keys.shape[0] // 2
    d_near[0, :, :HEAD_DIM] = d_keys[:side]
    d_near[0, :, HEAD_DIM:] = d_values[:side]
    d_far[0, :, :HEAD_DIM] = d_keys[side:].astype(BF16)
    d_far[0, :, HEAD_DIM:] = d_values[side:].astype(BF16)


def project_back_kernel(core, d_kv, key_full, d_query, h1, x, own, other, *rest):
    gain_in, gain_k, cosines, sines, d_middle = rest[:5]
    input_grad, kv_left, kv_right, d_gain_in, d_gain_k = rest[5:]
    d_rot = turned_back(d_kv[:, :HEAD_DIM], cosines[...], sines[...])
    d_key, d_gain = normed_back(key_full[...], gain_k[...], d_rot)
    d_gain_k[...] = jnp.broadcast_to(d_gain, d_gain_k.shape)
    d_key, d_value = d_key.astype(BF16).astype(F32), d_kv[:, HEAD_DIM:]
    first = core[0] == 0
    d_left = jnp.where(first, d_key, d_value).astype(BF16)
    d_right = jnp.where(first, d_value, d_key).astype(BF16)
    low = h1[...]
    kv_left[...] = contract(low, d_left, 0, 0)
    kv_right[...] = contract(low, d_right, 0, 0)
    q_cols = own.shape[1] - HEAD_DIM
    d_h1 = contract(d_query[:, :q_cols], own[:, :q_cols], 1, 1)
    d_h1 = d_h1 + contract(d_query[:, q_cols:], other[:, :q_cols], 1, 1)
    d_h1 = d_h1 + contract(d_left, own[:, q_cols:], 1, 1)
    d_h1 = d_h1 + contract(d_right, other[:, q_cols:], 1, 1)
    d_x, d_gain = normed_back(x[...].astype(F32), gain_in[...], d_h1)
    input_grad[...] = d_middle[...] + d_x
    d_gain_in[...] = jnp.broadcast_to(d_gain, d_gain_in.shape)


def feed_norm_kernel(gain, parts, middle, dy, layer_out, d_feed, d_gain):
    feed = parts[0].astype(F32)
    for at in range(1, parts.shape[0]):
        feed = feed + parts[at].astype(F32)
    layer_out[...] = (middle[...] + normed(feed, gain[...])).astype(BF16)
    d_values, d_row = normed_back(feed, gain[...], dy[...].astype(F32))
    d_feed[...] = d_values.astype(BF16)
    d_gain[...] = jnp.broadcast_to(d_row, d_gain.shape)


def shares_kernel(share, gate, up, down, *outs):
    units = outs[0].shape[2]
    for mine in range(len(outs)):

        @pl.when(share[0] == mine)
        def _():
            for step, out in enumerate(outs):
                start = (mine ^ step) * units
                stop = min(start + units, gate.shape[1])
                for at, weight in enumerate((gate, up, down)):
                    part = weight[:, start:stop]
                    if stop - start < units:
                        blank = jnp.zeros((part.shape[0], start + units - stop), part.dtype)
                        part = jnp.concatenate([part, blank], axis=1)
                    out[at] = part


def run(kernel, outs, *values, grid=None, in_specs=None, out_specs=None, scratch=()):
    more = {}
    if grid is not None:
        more = dict(grid=grid, in_specs=in_specs, out_specs=out_specs)
    elif in_specs is not None:
        more = dict(in_specs=in_specs)
    return pl.pallas_call(
        kernel,
        out_shape=[jax.ShapeDtypeStruct(shape, dtype) for shape, dtype in outs],
        scratch_shapes=list(scratch),
        compiler_params=pltpu.CompilerParams(vmem_limit_bytes=48 * 1024 * 1024),
        cost_estimate=pl.CostEstimate(flops=1, bytes_accessed=1, transcendentals=0),
        **more,
    )(*values)


def in_vmem(count):
    return [pl.BlockSpec(memory_space=pltpu.VMEM)] * count


def rows_spec(rows, width):
    return pl.BlockSpec((rows, width), lambda i: (i, 0))


def same_spec(*shape):
    return pl.BlockSpec(shape, lambda i: (0,) * len(shape))


def swap(value):
    return lax.ppermute(value, "tp", [(0, 1), (1, 0)])


BOTH = ("fsdp", "ctx")


def cross(value, mask):
    count = lax.axis_size("fsdp") * lax.axis_size("ctx")
    return lax.ppermute(value, BOTH, [(i, i ^ mask) for i in range(count)])


def shift(value, step):
    count = lax.axis_size("ctx")
    pairs = [(i, i + step) for i in range(count) if 0 <= i + step < count]
    return lax.ppermute(value, "ctx", pairs)


def together(*values):
    return lax.optimization_barrier(values)


def placed(own, other, bit, dim):
    first = jnp.where(bit == 0, own, other)
    second = jnp.where(bit == 0, other, own)
    return jnp.concatenate([first, second], axis=dim)


def parted(value, bit, dim):
    zero = lax.index_in_dim(value, 0, axis=dim, keepdims=False)
    one = lax.index_in_dim(value, 1, axis=dim, keepdims=False)
    return jnp.where(bit == 0, zero, one), jnp.where(bit == 0, one, zero)


def copies_to(value, axis):
    count = lax.axis_size(axis)
    return lax.all_to_all(jnp.broadcast_to(value[None], (count,) + value.shape), axis, 0, 0)


def gather_rows(value):
    return copies_to(copies_to(value, "ctx"), "fsdp")


def sum_of(parts, axis):
    return jnp.sum(lax.all_to_all(parts.astype(BF16), axis, 0, 0).astype(F32), axis=0)


def scatter_rows(value):
    return sum_of(sum_of(value, "fsdp"), "ctx")


def near_groups():
    planes, depths = lax.axis_size("fsdp"), lax.axis_size("ctx")
    return [
        [(f + x) * depths + c + z for x in (0, 1) for z in (0, 1)]
        for f in range(0, planes, 2)
        for c in range(0, depths, 2)
    ]


def trade(value):
    return lax.all_to_all(value, BOTH, 0, 0, axis_index_groups=near_groups())


def trade_apart(value):
    x_bit, z_bit = lax.axis_index("fsdp") & 1, lax.axis_index("ctx") & 1
    low, high = parted(value.reshape((2, 2) + value.shape[1:]), x_bit, 0)
    (p0, p1), (p2, p3) = parted(low, z_bit, 0), parted(high, z_bit, 0)
    return trade_parts(p0, p1, p2, p3)


def trade_parts(p0, p1, p2, p3):
    depths = lax.axis_size("ctx")
    x_bit, z_bit = lax.axis_index("fsdp") & 1, lax.axis_index("ctx") & 1
    p1, p2, p3 = cross(p1, 1), cross(p2, depths), cross(p3, depths | 1)
    low = placed(p0[None], p1[None], z_bit, 0)
    high = placed(p2[None], p3[None], z_bit, 0)
    return placed(low[None], high[None], x_bit, 0).reshape((4,) + p0.shape)


def far_bits():
    planes, depths = lax.axis_size("fsdp"), lax.axis_size("ctx")
    f_place, c_place = lax.axis_index("fsdp"), lax.axis_index("ctx")
    f_count, c_count = (planes - 1).bit_length(), (depths - 1).bit_length()
    c_bits = [(1 << k, (c_place >> k) & 1) for k in range(c_count - 1, 0, -1)]
    f_bits = [(depths << k, (f_place >> k) & 1) for k in range(f_count - 1, 0, -1)]
    return c_bits, f_bits


def gather_depth(value):
    c_bits, _ = far_bits()
    for mask, bit in c_bits[::-1]:
        value = placed(value, cross(value, mask), bit, 1)
    return value


def gather_plane(value):
    _, f_bits = far_bits()
    for mask, bit in f_bits[::-1]:
        value = placed(value, cross(value, mask), bit, 0)
    return value


def scatter_plane(value):
    _, f_bits = far_bits()
    for mask, bit in f_bits:
        halves = value.reshape((2, value.shape[0] // 2) + value.shape[1:])
        mine, other = parted(halves, bit, 0)
        value = (mine.astype(F32) + cross(other, mask).astype(F32)).astype(BF16)
    return value


def scatter_depth(value):
    c_bits, _ = far_bits()
    for mask, bit in c_bits:
        halves = value.reshape((2, 2, value.shape[1] // 2) + value.shape[2:])
        mine, other = parted(halves, bit, 1)
        value = (mine.astype(F32) + cross(other, mask).astype(F32)).astype(BF16)
    return value


def spread_start(rows):
    mine = trade(jnp.broadcast_to(rows[None], (4,) + rows.shape))
    return mine.reshape((-1,) + rows.shape[1:])


def spread(rows):
    mine = spread_start(rows)
    return jnp.concatenate([mine, swap(mine)], axis=0)


def collect_start(part):
    half = part.shape[0] // 2
    own = part[:half].astype(F32) + swap(part[half:]).astype(F32)
    return own.astype(BF16).reshape(4, half // 4, part.shape[1])


def local(
    tokens,
    segments,
    cotangent,
    norm_input,
    query_weight,
    key_weight,
    value_weight,
    norm_query,
    norm_key,
    out_weight,
    norm_attention,
    norm_feed,
    gate_weight,
    up_weight,
    down_weight,
    norm_feed_out,
):
    micros, seqs, block_len, width = tokens.shape
    planes = lax.axis_size("fsdp")
    depths = lax.axis_size("ctx")
    chunks = planes * depths
    ctx_place = lax.axis_index("ctx")
    tp_place = lax.axis_index("tp")
    first_core = tp_place == 0
    half_len = block_len // lax.axis_size("tp")
    back_blocks = -(-WINDOW // block_len)
    rows_in = norm_input.shape[0]
    small = norm_query.shape[0]
    heads_half = query_weight.shape[1] // HEAD_DIM
    q_cols = query_weight.shape[1]
    units = -(-gate_weight.shape[1] // (4 * 128)) * 128
    spare = 4 * units - gate_weight.shape[1]
    numbers = jnp.arange(SEGMENT_NUMBERS, dtype=jnp.int32)
    counts = jnp.sum((segments[..., None] == numbers).astype(F32), axis=2).astype(BF16)
    kv_shard = jnp.where(first_core, key_weight, value_weight)
    gains = (norm_input, norm_attention, norm_feed, norm_feed_out, norm_query, norm_key)
    gain_sizes = [gain.shape[0] for gain in gains]
    first_cols = q_cols + HEAD_DIM

    def row(*values):
        values = jnp.stack(values)
        return jnp.pad(values, ((0, 0), (0, first_cols - values.shape[1])))

    more = [row(*gains[:4]), row(*gains[4:]), row(counts.reshape(-1))]
    more = more + [jnp.zeros((1, first_cols), BF16)]
    first_pack = jnp.concatenate([query_weight, kv_shard], axis=1)
    first_pack = jnp.concatenate([first_pack] + more, axis=0)
    first_pack = jnp.broadcast_to(first_pack[None], (depths,) + first_pack.shape)
    first_pack, gate_weight, up_weight, down_weight, out_weight = together(
        first_pack, gate_weight, up_weight, down_weight, out_weight
    )
    first_pack = lax.all_to_all(first_pack, "ctx", 0, 0)

    share = ((lax.axis_index("fsdp") & 1) * 2 + (ctx_place & 1)).reshape(1)
    shares = run(
        shares_kernel,
        [((3, rows_in, units), BF16)] * 4,
        share, gate_weight, up_weight, down_weight.T,
        in_specs=[pl.BlockSpec(memory_space=pltpu.SMEM)] + in_vmem(3),
    )
    feed_parts = trade_parts(*shares)
    first_pack, feed_parts = together(first_pack, feed_parts)
    counts_all = first_pack[:, rows_in + len(gains), : counts.size].astype(F32)
    counts_all = jnp.sum(counts_all, axis=0).reshape(counts.shape)

    feed_parts = feed_parts.reshape(2, 2, 3, rows_in, units)
    gate_near, up_near, down_near = (feed_parts[:, :, which] for which in range(3))
    gate_deep = gather_depth(gate_near)
    first_pack = copies_to(first_pack, "fsdp")
    first_pack, gate_deep, up_near, down_near, out_pack = together(
        first_pack, gate_deep, up_near, down_near, out_weight.T
    )

    first_pack = first_pack.reshape(chunks, rows_in + 8, first_cols)
    first_own = first_pack[:, :rows_in].reshape(width, first_cols)
    first_other = swap(first_own)
    gain_input, gain_attention, gain_feed, gain_feed_out, gain_query, gain_key = (
        first_pack[:, rows_in + at, :size].astype(F32).reshape(-1)
        for at, size in enumerate(gain_sizes)
    )
    out_pack = copies_to(out_pack, "ctx")
    up_deep = gather_depth(up_near)
    gate_w = gather_plane(gate_deep).reshape(width, units)

    half_at = tp_place * half_len
    seg_half = lax.dynamic_slice_in_dim(segments, half_at, half_len, 2)
    earlier = numbers < seg_half[..., None]
    starts = jnp.sum(jnp.where(earlier, counts_all[:, :, None, :], 0.0), axis=-1)
    starts = starts.astype(jnp.int32)
    token_place = ctx_place * block_len + half_at + jnp.arange(half_len, dtype=jnp.int32)
    cosines, sines = rotations((token_place - starts).astype(F32), HEAD_DIM)
    within = jnp.arange(half_len, dtype=jnp.int32)
    key_place = jnp.concatenate(
        [
            (ctx_place - back) * block_len + side * half_len + within
            for side in (tp_place, 1 - tp_place)
            for back in range(back_blocks + 1)
        ]
    )

    batch = micros * seqs
    rows = batch * half_len
    x_low = lax.dynamic_slice_in_dim(tokens, half_at, half_len, 2).reshape(rows, width)
    dy_low = lax.dynamic_slice_in_dim(cotangent, half_at, half_len, 2).reshape(rows, width)
    cos, sin = cosines.reshape(rows, -1), sines.reshape(rows, -1)
    starts = starts.reshape(rows, 1)
    core = tp_place.reshape(1)
    gains_wide = [
        gain[None]
        for gain in (gain_input, gain_attention, gain_feed, gain_feed_out, gain_query, gain_key)
    ]
    g_in, g_att, g_feed, g_out, g_query, g_key = gains_wide
    smem = [pl.BlockSpec(memory_space=pltpu.SMEM)]
    wide, cols_all = (rows, width), 2 * q_cols

    h1, query_raw, query_rot, key_full, pair = run(
        project_kernel,
        [(wide, BF16), ((rows, cols_all), F32), ((rows, cols_all), BF16)]
        + [((rows, HEAD_DIM), F32), ((rows, 2 * HEAD_DIM), BF16)],
        core, x_low, first_own, first_other, g_in, g_query, g_key, cos, sin,
        in_specs=smem + in_vmem(8),
    )
    pair, up_deep, gate_w, out_pack, down_near = together(
        pair, up_deep, gate_w, out_pack, down_near
    )
    down_deep = gather_depth(down_near)
    up_w = gather_plane(up_deep).reshape(width, units)
    out_own = copies_to(out_pack, "fsdp").reshape(width, q_cols)
    pair = pair.reshape(batch, half_len, 2 * HEAD_DIM)
    mine = jnp.concatenate(
        [pair] + [shift(pair, back) for back in range(1, back_blocks + 1)], axis=1
    )
    seen = jnp.concatenate([mine, swap(mine)], axis=1)
    seen, up_w, out_own, down_deep = together(seen, up_w, out_own, down_deep)
    out_other = swap(out_own)
    down_w = gather_plane(down_deep).reshape(width, units)
    span = seen.shape[1]
    token_rows, key_cols = token_place[:, None], key_place[None]
    place_specs = [same_spec(half_len, 1), same_spec(1, span), rows_spec(half_len, 1)]
    seen_spec = pl.BlockSpec((1, span, 2 * HEAD_DIM), lambda i: (i, 0, 0))
    row_spec, col_spec = rows_spec(half_len, width), rows_spec(half_len, cols_all)
    out_specs = [same_spec(width, q_cols)] * 2
    mixed, attention, middle, h2 = run(
        attend_kernel,
        [((rows, cols_all), BF16), (wide, F32), (wide, F32), (wide, BF16)],
        token_rows, key_cols, starts, query_rot, seen, x_low, out_own, out_other, g_att, g_feed,
        grid=(batch,),
        in_specs=place_specs
        + [col_spec, seen_spec, row_spec]
        + out_specs
        + [same_spec(1, width)] * 2,
        out_specs=[col_spec] + [row_spec] * 3,
    )

    h2_mine, down_w = together(spread_start(h2), down_w)
    h2_all = jnp.concatenate([h2_mine, swap(h2_mine)], axis=0)
    hidden, by_up, by_gate, part = feed_forward(h2_all, gate_w, up_w, down_w)
    feed_parts = trade(collect_start(part))
    layer_out, d_feed, d_gain_out = run(
        feed_norm_kernel,
        [(wide, BF16), (wide, BF16), ((8, width), F32)],
        g_out, feed_parts, middle, dy_low,
    )
    d_feed_all = spread(d_feed)
    grad_down = dot("td,tu->du", d_feed_all, hidden).astype(BF16)
    d_feed_all, grad_down = together(d_feed_all, grad_down)
    down_plane = scatter_plane(grad_down.reshape(planes, depths, rows_in, units))
    d_hidden = dot("td,du->tu", d_feed_all, down_w)
    d_gate = (d_hidden * by_gate.astype(F32)).astype(BF16)
    d_up = (d_hidden * by_up.astype(F32)).astype(BF16)
    d_h2_part = dot("tu,du->td", d_gate, gate_w) + dot("tu,du->td", d_up, up_w)
    d_h2_part, d_gate, d_up, down_plane = together(
        d_h2_part.astype(BF16), d_gate, d_up, down_plane
    )
    down_near = scatter_depth(down_plane)
    d_h2_parts = trade(collect_start(d_h2_part))
    grad_gate = dot("td,tu->du", h2_all, d_gate).astype(BF16)
    gate_plane = scatter_plane(grad_gate.reshape(planes, depths, rows_in, units))
    grad_up = dot("td,tu->du", h2_all, d_up).astype(BF16)
    d_h2_parts, down_near, gate_plane, grad_up = together(
        d_h2_parts, down_near, gate_plane, grad_up
    )
    gate_near = scatter_depth(gate_plane)
    up_plane = scatter_plane(grad_up.reshape(planes, depths, rows_in, units))

    side = span // 2
    near_spec = pl.BlockSpec((1, side, 2 * HEAD_DIM), lambda i: (i, 0, 0))
    turn_spec = rows_spec(half_len, HEAD_DIM // 2)
    d_middle, d_attention, d_query, d_near, d_far, d_gains, d_gain_query = run(
        attend_back_kernel,
        [(wide, F32), (wide, BF16), ((rows, cols_all), BF16)]
        + [((batch, side, 2 * HEAD_DIM), F32), ((batch, side, 2 * HEAD_DIM), BF16)]
        + [((8, width), F32), ((8, HEAD_DIM), F32)],
        token_rows, key_cols, starts, query_rot, seen, out_own, out_other,
        g_att, g_feed, g_query, cos, sin, d_h2_parts, middle, attention, dy_low, query_raw,
        grid=(batch,),
        in_specs=place_specs
        + [col_spec, seen_spec]
        + out_specs
        + [same_spec(1, width)] * 2
        + [same_spec(1, HEAD_DIM), turn_spec, turn_spec]
        + [pl.BlockSpec((4, half_len, width), lambda i: (0, i, 0))]
        + [row_spec] * 3
        + [col_spec],
        out_specs=[row_spec, row_spec, col_spec, near_spec, near_spec]
        + [same_spec(8, width), same_spec(8, HEAD_DIM)],
        scratch=[pltpu.VMEM((half_len, cols_all), BF16)],
    )
    d_near, d_far, d_query, d_attention, gate_near, up_plane = together(
        d_near, d_far, d_query, d_attention, gate_near, up_plane
    )
    d_mine = d_near + swap(d_far).astype(F32)
    both_left = jnp.concatenate(
        [dot("td,te->de", d_attention, mixed[:, :q_cols])]
        + [dot("td,te->de", h1, d_query[:, :q_cols])],
        axis=1,
    )
    both_right = jnp.concatenate(
        [dot("td,te->de", d_attention, mixed[:, q_cols:]).astype(BF16)]
        + [dot("td,te->de", h1, d_query[:, q_cols:]).astype(BF16)],
        axis=1,
    )
    both = swap(both_right)
    d_mine, both = together(d_mine, both)
    both = both_left + both.astype(F32)
    both = sum_of(both.reshape(planes, depths, rows_in, cols_all), "fsdp")
    d_kv = d_mine[:, :half_len]
    for back in range(1, back_blocks + 1):
        piece = d_mine[:, back * half_len : (back + 1) * half_len].astype(BF16)
        d_kv = d_kv + shift(piece, -back).astype(F32)
    d_kv, up_plane = together(d_kv, up_plane)
    up_near = scatter_depth(up_plane)
    input_grad, kv_left, kv_right, d_gain_in, d_gain_key = run(
        project_back_kernel,
        [(wide, F32), ((width, HEAD_DIM), F32), ((width, HEAD_DIM), F32)]
        + [((8, width), F32), ((8, HEAD_DIM), F32)],
        core, d_kv.reshape(rows, 2 * HEAD_DIM), key_full, d_query, h1, x_low,
        first_own, first_other, g_in, g_key, cos, sin, d_middle,
        in_specs=smem + in_vmem(12),
    )
    gain_grads = (d_gain_in[0], d_gains[1], d_gains[0], d_gain_out[0])
    gain_grads = gain_grads + (d_gain_query[0], d_gain_key[0])

    gain_sums = [
        jnp.pad(grad.reshape(chunks, 1, -1), ((0, 0), (0, 0), (0, HEAD_DIM - size)))
        for grad, size in zip(gain_grads, gain_sizes)
    ]
    gain_sums = gain_sums + [jnp.zeros((chunks, 8 - len(gains), HEAD_DIM), F32)]
    kv_left, kv_right = (
        jnp.concatenate([grad.reshape(chunks, rows_in, HEAD_DIM)] + gain_sums, axis=1)
        for grad in (kv_left, kv_right)
    )
    last = (kv_left + swap(kv_right.astype(BF16)).astype(F32)).astype(BF16)
    last, both, up_near = together(last, both, up_near)
    last = sum_of(last.reshape((planes, depths) + last.shape[1:]), "fsdp")
    last, gate_near, up_near, down_near = together(last, gate_near, up_near, down_near)
    feed_grads = jnp.stack([gate_near, up_near, down_near], axis=2)
    feed_grads = trade_apart(feed_grads.reshape(4, 3, rows_in, units))
    both = jnp.pad(both, ((0, 0), (0, last.shape[1] - rows_in), (0, 0)))
    last = sum_of(jnp.concatenate([both, last], axis=-1), "ctx")
    both, last = last[:rows_in, :cols_all], last[:, cols_all:]
    out_out, out_query = both[:, :q_cols].T, both[:, q_cols:]
    feed_grads = feed_grads.astype(F32).transpose(1, 2, 0, 3)
    feed_grads = feed_grads.reshape(3, rows_in, 4 * units)[:, :, : 4 * units - spare]
    out_gate, out_up, out_down = feed_grads[0], feed_grads[1], feed_grads[2].T
    out_kv = last[:rows_in]
    kv_other = swap(out_kv)
    out_key = jnp.where(first_core, out_kv, kv_other)
    out_value = jnp.where(first_core, kv_other, out_kv)
    pieces = [last[rows_in + at, :size] for at, size in enumerate(gain_sizes)]

    return (
        layer_out.reshape(micros, seqs, half_len, width),
        input_grad.reshape(micros, seqs, half_len, width),
        pieces[0],
        out_query,
        out_key,
        out_value,
        pieces[4],
        pieces[5],
        out_out,
        pieces[1],
        pieces[2],
        out_gate,
        out_up,
        out_down,
        pieces[3],
    )


def solution(mesh):
    both = ("fsdp", "ctx")
    return jax.shard_map(
        local,
        mesh=mesh,
        in_specs=(
            P(None, "fsdp", "ctx", None),
            P(None, "fsdp", "ctx"),
            P(None, "fsdp", "ctx", None),
            P(both),
            P(both, "tp"),
            P(both, None),
            P(both, None),
            P(both),
            P(both),
            P("tp", both),
            P(both),
            P(both),
            P(both, "tp"),
            P(both, "tp"),
            P("tp", both),
            P(both),
        ),
        out_specs=(
            P(None, "fsdp", ("ctx", "tp"), None),
            P(None, "fsdp", ("ctx", "tp"), None),
            P(both),
            P(both, "tp"),
            P(both, None),
            P(both, None),
            P(both),
            P(both),
            P("tp", both),
            P(both),
            P(both),
            P(both, "tp"),
            P(both, "tp"),
            P("tp", both),
            P(both),
        ),
        check_vma=False,
    )
```

```python
import jax
import jax.numpy as jnp
from jax import lax
from jax.experimental import pallas as pl
from jax.experimental.pallas import tpu as pltpu
from jax.sharding import PartitionSpec as P

HEAD_DIM = 256
WINDOW = 512

EPSILON = 1e-06
ROPE_BASE = 10000.0
SCORE_SCALE = 0.0625
MASKED = -1e30

SEGMENT_NUMBERS = 10

F32 = jnp.float32
BF16 = jnp.bfloat16


def dot(spec, left, right):
    return jnp.einsum(spec, left, right, preferred_element_type=F32)


def normed(values, gain):
    return values * lax.rsqrt(jnp.mean(values * values, axis=-1, keepdims=True) + EPSILON) * gain


def rotations(offsets, depth):
    middle = depth // 2
    inverse = ROPE_BASE ** (-2.0 * jnp.arange(middle, dtype=F32) / depth)
    angle_grid = offsets[..., None] * inverse
    return (jnp.cos(angle_grid), jnp.sin(angle_grid))


GELU_SCALE = 0.7978845608028654
GELU_CUBE = 0.044715


def feed_forward(rows, gate_w, up_w, down_w):
    z = dot("td,du->tu", rows, gate_w)
    up = dot("td,du->tu", rows, up_w)
    square = z * z
    t = jnp.tanh(GELU_SCALE * z * (1.0 + GELU_CUBE * square))
    half_one = 0.5 * (1.0 + t)
    gelu = z * half_one
    slope = half_one + 0.5 * z * (1.0 - t * t) * GELU_SCALE * (1.0 + 3.0 * GELU_CUBE * square)
    hidden = (gelu * up).astype(BF16)
    part = dot("tu,du->td", hidden, down_w).astype(BF16)
    return hidden, gelu.astype(BF16), (up * slope).astype(BF16), part


def contract(left, right, left_dim, right_dim):
    dims = (((left_dim,), (right_dim,)), ((), ()))
    return lax.dot_general(left, right, dims, preferred_element_type=F32)


def normed_back(values, gain, grad):
    scale = lax.rsqrt(jnp.mean(values * values, axis=-1, keepdims=True) + EPSILON)
    inner = gain * grad
    along = jnp.mean(values * inner, axis=-1, keepdims=True)
    d_values = scale * inner - values * (scale * scale * scale) * along
    return d_values, jnp.sum(grad * values * scale, axis=0, keepdims=True)


def turned(values, cosines, sines):
    middle = values.shape[-1] // 2
    first, second = values[:, :middle], values[:, middle:]
    return jnp.concatenate(
        [first * cosines - second * sines, second * cosines + first * sines], axis=-1
    )


def turned_back(values, cosines, sines):
    return turned(values, cosines, -sines)


def head(at):
    return slice(at * HEAD_DIM, (at + 1) * HEAD_DIM)


def project_kernel(core, x, own, other, gain_in, gain_q, gain_k, cosines, sines, *outs):
    h1, raw, query_rot, key_full, pair = outs
    cos, sin = cosines[...], sines[...]
    low = normed(x[...].astype(F32), gain_in[...]).astype(BF16)
    h1[...] = low
    q_cols = own.shape[1] - HEAD_DIM
    left, right = contract(low, own[...], 1, 0), contract(low, other[...], 1, 0)
    first = core[0] == 0
    key = jnp.where(first, left[:, q_cols:], right[:, q_cols:])
    value = jnp.where(first, right[:, q_cols:], left[:, q_cols:])
    key_full[...] = key
    pair[:, :HEAD_DIM] = turned(normed(key, gain_k[...]), cos, sin).astype(BF16)
    pair[:, HEAD_DIM:] = value.astype(BF16)
    raw[:, :q_cols] = left[:, :q_cols]
    raw[:, q_cols:] = right[:, :q_cols]
    for at in range(raw.shape[1] // HEAD_DIM):
        turn = turned(normed(raw[:, head(at)], gain_q[...]), cos, sin)
        query_rot[:, head(at)] = turn.astype(BF16)


def allowed_pairs(tokens_at, keys_at, starts):
    t, u, begin = tokens_at[...], keys_at[...], starts[...]
    return (u <= t) & (t - u < WINDOW) & (u >= begin)


def probabilities(query, keys, allowed):
    scores = jnp.where(allowed, contract(query, keys, 1, 1) * SCORE_SCALE, MASKED)
    lifted = jnp.exp(scores - jnp.max(scores, axis=-1, keepdims=True))
    return lifted / jnp.sum(lifted, axis=-1, keepdims=True)


def attend_kernel(tokens_at, keys_at, starts, query_rot, seen, x, own, other, gain_a, gain_f, *outs):
    mixed, attention, middle, h2 = outs
    allowed = allowed_pairs(tokens_at, keys_at, starts)
    keys, values = seen[0, :, :HEAD_DIM], seen[0, :, HEAD_DIM:]
    for at in range(query_rot.shape[1] // HEAD_DIM):
        prob = probabilities(query_rot[:, head(at)], keys, allowed).astype(BF16)
        mixed[:, head(at)] = contract(prob, values, 1, 0).astype(BF16)
    q_cols = own.shape[1]
    result = contract(mixed[:, :q_cols], own[...], 1, 1)
    result = result + contract(mixed[:, q_cols:], other[...], 1, 1)
    attention[...] = result
    mid = x[...].astype(F32) + normed(result, gain_a[...])
    middle[...] = mid
    h2[...] = normed(mid, gain_f[...]).astype(BF16)


def attend_back_kernel(tokens_at, keys_at, starts, query_rot, seen, own, other, *rest):
    gain_a, gain_f, gain_q, cosines, sines, parts, middle, attention, dy, raw = rest[:10]
    d_middle, d_attention, d_query, d_near, d_far, d_gains, d_gain_q, d_mixed = rest[10:]

    @pl.when(pl.program_id(0) == 0)
    def _():
        d_gains[...] = jnp.zeros_like(d_gains)
        d_gain_q[...] = jnp.zeros_like(d_gain_q)

    d_h2 = parts[0].astype(F32)
    for at in range(1, parts.shape[0]):
        d_h2 = d_h2 + parts[at].astype(F32)
    d_mid, d_gain_f = normed_back(middle[...], gain_f[...], d_h2)
    d_mid = d_mid + dy[...].astype(F32)
    d_middle[...] = d_mid
    d_att, d_gain_a = normed_back(attention[...], gain_a[...], d_mid)
    d_gains[0:1, :] += d_gain_f
    d_gains[1:2, :] += d_gain_a
    d_att = d_att.astype(BF16)
    d_attention[...] = d_att
    q_cols = own.shape[1]
    d_mixed[:, :q_cols] = contract(d_att, own[...], 1, 0).astype(BF16)
    d_mixed[:, q_cols:] = contract(d_att, other[...], 1, 0).astype(BF16)
    allowed = allowed_pairs(tokens_at, keys_at, starts)
    keys, values = seen[0, :, :HEAD_DIM], seen[0, :, HEAD_DIM:]
    d_keys = jnp.zeros(keys.shape, F32)
    d_values = jnp.zeros(keys.shape, F32)
    for at in range(query_rot.shape[1] // HEAD_DIM):
        query, d_mix = query_rot[:, head(at)], d_mixed[:, head(at)]
        prob = probabilities(query, keys, allowed)
        d_prob = contract(d_mix, values, 1, 1)
        delta = jnp.sum(prob * d_prob, axis=-1, keepdims=True)
        d_raw = (prob * (d_prob - delta) * SCORE_SCALE).astype(BF16)
        d_keys = d_keys + contract(d_raw, query, 0, 0)
        d_values = d_values + contract(prob.astype(BF16), d_mix, 0, 0)
        d_rot = turned_back(contract(d_raw, keys, 1, 0), cosines[...], sines[...])
        d_full, d_gain = normed_back(raw[:, head(at)], gain_q[...], d_rot)
        d_query[:, head(at)] = d_full.astype(BF16)
        d_gain_q[0:1, :] += d_gain
    side = keys.shape[0] // 2
    d_near[0, :, :HEAD_DIM] = d_keys[:side]
    d_near[0, :, HEAD_DIM:] = d_values[:side]
    d_far[0, :, :HEAD_DIM] = d_keys[side:].astype(BF16)
    d_far[0, :, HEAD_DIM:] = d_values[side:].astype(BF16)


def project_back_kernel(core, d_kv, key_full, d_query, h1, x, own, other, *rest):
    gain_in, gain_k, cosines, sines, d_middle = rest[:5]
    input_grad, kv_left, kv_right, d_gain_in, d_gain_k = rest[5:]
    d_rot = turned_back(d_kv[:, :HEAD_DIM], cosines[...], sines[...])
    d_key, d_gain = normed_back(key_full[...], gain_k[...], d_rot)
    d_gain_k[...] = jnp.broadcast_to(d_gain, d_gain_k.shape)
    d_key, d_value = d_key.astype(BF16).astype(F32), d_kv[:, HEAD_DIM:]
    first = core[0] == 0
    d_left = jnp.where(first, d_key, d_value).astype(BF16)
    d_right = jnp.where(first, d_value, d_key).astype(BF16)
    low = h1[...]
    kv_left[...] = contract(low, d_left, 0, 0)
    kv_right[...] = contract(low, d_right, 0, 0)
    q_cols = own.shape[1] - HEAD_DIM
    d_h1 = contract(d_query[:, :q_cols], own[:, :q_cols], 1, 1)
    d_h1 = d_h1 + contract(d_query[:, q_cols:], other[:, :q_cols], 1, 1)
    d_h1 = d_h1 + contract(d_left, own[:, q_cols:], 1, 1)
    d_h1 = d_h1 + contract(d_right, other[:, q_cols:], 1, 1)
    d_x, d_gain = normed_back(x[...].astype(F32), gain_in[...], d_h1)
    input_grad[...] = d_middle[...] + d_x
    d_gain_in[...] = jnp.broadcast_to(d_gain, d_gain_in.shape)


def feed_norm_kernel(gain, parts, middle, dy, layer_out, d_feed, d_gain):
    feed = parts[0].astype(F32)
    for at in range(1, parts.shape[0]):
        feed = feed + parts[at].astype(F32)
    layer_out[...] = (middle[...] + normed(feed, gain[...])).astype(BF16)
    d_values, d_row = normed_back(feed, gain[...], dy[...].astype(F32))
    d_feed[...] = d_values.astype(BF16)
    d_gain[...] = jnp.broadcast_to(d_row, d_gain.shape)


def shares_kernel(share, gate, up, down, *outs):
    units = outs[0].shape[2]
    for mine in range(len(outs)):

        @pl.when(share[0] == mine)
        def _():
            for step, out in enumerate(outs):
                start = (mine ^ step) * units
                stop = min(start + units, gate.shape[1])
                for at, weight in enumerate((gate, up, down)):
                    part = weight[:, start:stop]
                    if stop - start < units:
                        blank = jnp.zeros((part.shape[0], start + units - stop), part.dtype)
                        part = jnp.concatenate([part, blank], axis=1)
                    out[at] = part


def run(kernel, outs, *values, grid=None, in_specs=None, out_specs=None, scratch=()):
    more = {}
    if grid is not None:
        more = dict(grid=grid, in_specs=in_specs, out_specs=out_specs)
    elif in_specs is not None:
        more = dict(in_specs=in_specs)
    return pl.pallas_call(
        kernel,
        out_shape=[jax.ShapeDtypeStruct(shape, dtype) for shape, dtype in outs],
        scratch_shapes=list(scratch),
        compiler_params=pltpu.CompilerParams(vmem_limit_bytes=48 * 1024 * 1024),
        cost_estimate=pl.CostEstimate(flops=1, bytes_accessed=1, transcendentals=0),
        **more,
    )(*values)


def in_vmem(count):
    return [pl.BlockSpec(memory_space=pltpu.VMEM)] * count


def rows_spec(rows, width):
    return pl.BlockSpec((rows, width), lambda i: (i, 0))


def same_spec(*shape):
    return pl.BlockSpec(shape, lambda i: (0,) * len(shape))


def swap(value):
    return lax.ppermute(value, "tp", [(0, 1), (1, 0)])


BOTH = ("fsdp", "ctx")


def cross(value, mask):
    count = lax.axis_size("fsdp") * lax.axis_size("ctx")
    return lax.ppermute(value, BOTH, [(i, i ^ mask) for i in range(count)])


def shift(value, step):
    count = lax.axis_size("ctx")
    pairs = [(i, i + step) for i in range(count) if 0 <= i + step < count]
    return lax.ppermute(value, "ctx", pairs)


def together(*values):
    return lax.optimization_barrier(values)


def placed(own, other, bit, dim):
    first = jnp.where(bit == 0, own, other)
    second = jnp.where(bit == 0, other, own)
    return jnp.concatenate([first, second], axis=dim)


def parted(value, bit, dim):
    zero = lax.index_in_dim(value, 0, axis=dim, keepdims=False)
    one = lax.index_in_dim(value, 1, axis=dim, keepdims=False)
    return jnp.where(bit == 0, zero, one), jnp.where(bit == 0, one, zero)


def copies_to(value, axis):
    count = lax.axis_size(axis)
    return lax.all_to_all(jnp.broadcast_to(value[None], (count,) + value.shape), axis, 0, 0)


def gather_rows(value):
    return copies_to(copies_to(value, "ctx"), "fsdp")


def sum_of(parts, axis):
    return jnp.sum(lax.all_to_all(parts.astype(BF16), axis, 0, 0).astype(F32), axis=0)


def scatter_rows(value):
    return sum_of(sum_of(value, "fsdp"), "ctx")


def near_groups():
    planes, depths = lax.axis_size("fsdp"), lax.axis_size("ctx")
    return [
        [(f + x) * depths + c + z for x in (0, 1) for z in (0, 1)]
        for f in range(0, planes, 2)
        for c in range(0, depths, 2)
    ]


def trade(value):
    return lax.all_to_all(value, BOTH, 0, 0, axis_index_groups=near_groups())


def trade_apart(value):
    x_bit, z_bit = lax.axis_index("fsdp") & 1, lax.axis_index("ctx") & 1
    low, high = parted(value.reshape((2, 2) + value.shape[1:]), x_bit, 0)
    (p0, p1), (p2, p3) = parted(low, z_bit, 0), parted(high, z_bit, 0)
    return trade_parts(p0, p1, p2, p3)


def trade_parts(p0, p1, p2, p3):
    depths = lax.axis_size("ctx")
    x_bit, z_bit = lax.axis_index("fsdp") & 1, lax.axis_index("ctx") & 1
    p1, p2, p3 = cross(p1, 1), cross(p2, depths), cross(p3, depths | 1)
    low = placed(p0[None], p1[None], z_bit, 0)
    high = placed(p2[None], p3[None], z_bit, 0)
    return placed(low[None], high[None], x_bit, 0).reshape((4,) + p0.shape)


def far_bits():
    planes, depths = lax.axis_size("fsdp"), lax.axis_size("ctx")
    f_place, c_place = lax.axis_index("fsdp"), lax.axis_index("ctx")
    f_count, c_count = (planes - 1).bit_length(), (depths - 1).bit_length()
    c_bits = [(1 << k, (c_place >> k) & 1) for k in range(c_count - 1, 0, -1)]
    f_bits = [(depths << k, (f_place >> k) & 1) for k in range(f_count - 1, 0, -1)]
    return c_bits, f_bits


def gather_depth(value):
    c_bits, _ = far_bits()
    for mask, bit in c_bits[::-1]:
        value = placed(value, cross(value, mask), bit, 1)
    return value


def gather_plane(value):
    _, f_bits = far_bits()
    for mask, bit in f_bits[::-1]:
        value = placed(value, cross(value, mask), bit, 0)
    return value


def scatter_plane(value):
    _, f_bits = far_bits()
    for mask, bit in f_bits:
        halves = value.reshape((2, value.shape[0] // 2) + value.shape[1:])
        mine, other = parted(halves, bit, 0)
        value = (mine.astype(F32) + cross(other, mask).astype(F32)).astype(BF16)
    return value


def scatter_depth(value):
    c_bits, _ = far_bits()
    for mask, bit in c_bits:
        halves = value.reshape((2, 2, value.shape[1] // 2) + value.shape[2:])
        mine, other = parted(halves, bit, 1)
        value = (mine.astype(F32) + cross(other, mask).astype(F32)).astype(BF16)
    return value


def spread_start(rows):
    mine = trade(jnp.broadcast_to(rows[None], (4,) + rows.shape))
    return mine.reshape((-1,) + rows.shape[1:])


def spread(rows):
    mine = spread_start(rows)
    return jnp.concatenate([mine, swap(mine)], axis=0)


def collect_start(part):
    half = part.shape[0] // 2
    own = part[:half].astype(F32) + swap(part[half:]).astype(F32)
    return own.astype(BF16).reshape(4, half // 4, part.shape[1])


def local(
    tokens,
    segments,
    cotangent,
    norm_input,
    query_weight,
    key_weight,
    value_weight,
    norm_query,
    norm_key,
    out_weight,
    norm_attention,
    norm_feed,
    gate_weight,
    up_weight,
    down_weight,
    norm_feed_out,
):
    micros, seqs, block_len, width = tokens.shape
    planes = lax.axis_size("fsdp")
    depths = lax.axis_size("ctx")
    chunks = planes * depths
    ctx_place = lax.axis_index("ctx")
    tp_place = lax.axis_index("tp")
    first_core = tp_place == 0
    half_len = block_len // lax.axis_size("tp")
    back_blocks = -(-WINDOW // block_len)
    rows_in = norm_input.shape[0]
    small = norm_query.shape[0]
    heads_half = query_weight.shape[1] // HEAD_DIM
    q_cols = query_weight.shape[1]
    units = -(-gate_weight.shape[1] // (4 * 128)) * 128
    spare = 4 * units - gate_weight.shape[1]
    numbers = jnp.arange(SEGMENT_NUMBERS, dtype=jnp.int32)
    counts = jnp.sum((segments[..., None] == numbers).astype(F32), axis=2).astype(BF16)
    kv_shard = jnp.where(first_core, key_weight, value_weight)
    gains = (norm_input, norm_attention, norm_feed, norm_feed_out, norm_query, norm_key)
    gain_sizes = [gain.shape[0] for gain in gains]
    first_cols = q_cols + HEAD_DIM

    def row(*values):
        values = jnp.stack(values)
        return jnp.pad(values, ((0, 0), (0, first_cols - values.shape[1])))

    more = [row(*gains[:4]), row(*gains[4:]), row(counts.reshape(-1))]
    more = more + [jnp.zeros((1, first_cols), BF16)]
    first_pack = jnp.concatenate([query_weight, kv_shard], axis=1)
    first_pack = jnp.concatenate([first_pack] + more, axis=0)
    first_pack = jnp.broadcast_to(first_pack[None], (depths,) + first_pack.shape)
    first_pack, gate_weight, up_weight, down_weight = together(
        first_pack, gate_weight, up_weight, down_weight
    )
    out_pack = copies_to(out_weight.T, "ctx")
    first_pack, out_pack = together(first_pack, out_pack)
    first_pack = lax.all_to_all(first_pack, "ctx", 0, 0)

    share = ((lax.axis_index("fsdp") & 1) * 2 + (ctx_place & 1)).reshape(1)
    shares = run(
        shares_kernel,
        [((3, rows_in, units), BF16)] * 4,
        share, gate_weight, up_weight, down_weight.T,
        in_specs=[pl.BlockSpec(memory_space=pltpu.SMEM)] + in_vmem(3),
    )
    feed_parts = trade_parts(*shares)
    first_pack, feed_parts = together(first_pack, feed_parts)
    counts_all = first_pack[:, rows_in + len(gains), : counts.size].astype(F32)
    counts_all = jnp.sum(counts_all, axis=0).reshape(counts.shape)

    feed_parts = feed_parts.reshape(2, 2, 3, rows_in, units)
    gate_near, up_near, down_near = (feed_parts[:, :, which] for which in range(3))
    gate_deep = gather_depth(gate_near)
    first_pack = copies_to(first_pack, "fsdp")
    first_pack, gate_deep, up_near, down_near, out_pack = together(
        first_pack, gate_deep, up_near, down_near, out_pack
    )

    first_pack = first_pack.reshape(chunks, rows_in + 8, first_cols)
    first_own = first_pack[:, :rows_in].reshape(width, first_cols)
    first_other = swap(first_own)
    gain_input, gain_attention, gain_feed, gain_feed_out, gain_query, gain_key = (
        first_pack[:, rows_in + at, :size].astype(F32).reshape(-1)
        for at, size in enumerate(gain_sizes)
    )
    up_deep = gather_depth(up_near)
    gate_w = gather_plane(gate_deep).reshape(width, units)

    half_at = tp_place * half_len
    seg_half = lax.dynamic_slice_in_dim(segments, half_at, half_len, 2)
    earlier = numbers < seg_half[..., None]
    starts = jnp.sum(jnp.where(earlier, counts_all[:, :, None, :], 0.0), axis=-1)
    starts = starts.astype(jnp.int32)
    token_place = ctx_place * block_len + half_at + jnp.arange(half_len, dtype=jnp.int32)
    cosines, sines = rotations((token_place - starts).astype(F32), HEAD_DIM)
    within = jnp.arange(half_len, dtype=jnp.int32)
    key_place = jnp.concatenate(
        [
            (ctx_place - back) * block_len + side * half_len + within
            for side in (tp_place, 1 - tp_place)
            for back in range(back_blocks + 1)
        ]
    )

    batch = micros * seqs
    rows = batch * half_len
    x_low = lax.dynamic_slice_in_dim(tokens, half_at, half_len, 2).reshape(rows, width)
    dy_low = lax.dynamic_slice_in_dim(cotangent, half_at, half_len, 2).reshape(rows, width)
    cos, sin = cosines.reshape(rows, -1), sines.reshape(rows, -1)
    starts = starts.reshape(rows, 1)
    core = tp_place.reshape(1)
    gains_wide = [
        gain[None]
        for gain in (gain_input, gain_attention, gain_feed, gain_feed_out, gain_query, gain_key)
    ]
    g_in, g_att, g_feed, g_out, g_query, g_key = gains_wide
    smem = [pl.BlockSpec(memory_space=pltpu.SMEM)]
    wide, cols_all = (rows, width), 2 * q_cols

    h1, query_raw, query_rot, key_full, pair = run(
        project_kernel,
        [(wide, BF16), ((rows, cols_all), F32), ((rows, cols_all), BF16)]
        + [((rows, HEAD_DIM), F32), ((rows, 2 * HEAD_DIM), BF16)],
        core, x_low, first_own, first_other, g_in, g_query, g_key, cos, sin,
        in_specs=smem + in_vmem(8),
    )
    up_deep, gate_w, out_pack, down_near = together(up_deep, gate_w, out_pack, down_near)
    down_deep = gather_depth(down_near)
    up_w = gather_plane(up_deep).reshape(width, units)
    out_own = copies_to(out_pack, "fsdp").reshape(width, q_cols)
    pair = pair.reshape(batch, half_len, 2 * HEAD_DIM)
    mine = jnp.concatenate(
        [pair] + [shift(pair, back) for back in range(1, back_blocks + 1)], axis=1
    )
    seen = jnp.concatenate([mine, swap(mine)], axis=1)
    seen, up_w, out_own, down_deep = together(seen, up_w, out_own, down_deep)
    out_other = swap(out_own)
    down_w = gather_plane(down_deep).reshape(width, units)
    span = seen.shape[1]
    token_rows, key_cols = token_place[:, None], key_place[None]
    place_specs = [same_spec(half_len, 1), same_spec(1, span), rows_spec(half_len, 1)]
    seen_spec = pl.BlockSpec((1, span, 2 * HEAD_DIM), lambda i: (i, 0, 0))
    row_spec, col_spec = rows_spec(half_len, width), rows_spec(half_len, cols_all)
    out_specs = [same_spec(width, q_cols)] * 2
    mixed, attention, middle, h2 = run(
        attend_kernel,
        [((rows, cols_all), BF16), (wide, F32), (wide, F32), (wide, BF16)],
        token_rows, key_cols, starts, query_rot, seen, x_low, out_own, out_other, g_att, g_feed,
        grid=(batch,),
        in_specs=place_specs
        + [col_spec, seen_spec, row_spec]
        + out_specs
        + [same_spec(1, width)] * 2,
        out_specs=[col_spec] + [row_spec] * 3,
    )

    h2_mine, down_w = together(spread_start(h2), down_w)
    h2_all = jnp.concatenate([h2_mine, swap(h2_mine)], axis=0)
    hidden, by_up, by_gate, part = feed_forward(h2_all, gate_w, up_w, down_w)
    feed_parts = trade(collect_start(part))
    layer_out, d_feed, d_gain_out = run(
        feed_norm_kernel,
        [(wide, BF16), (wide, BF16), ((8, width), F32)],
        g_out, feed_parts, middle, dy_low,
    )
    d_feed_all = spread(d_feed)
    grad_down = dot("td,tu->du", d_feed_all, hidden).astype(BF16)
    d_feed_all, grad_down = together(d_feed_all, grad_down)
    down_plane = scatter_plane(grad_down.reshape(planes, depths, rows_in, units))
    d_hidden = dot("td,du->tu", d_feed_all, down_w)
    d_gate = (d_hidden * by_gate.astype(F32)).astype(BF16)
    d_up = (d_hidden * by_up.astype(F32)).astype(BF16)
    d_h2_part = dot("tu,du->td", d_gate, gate_w) + dot("tu,du->td", d_up, up_w)
    d_h2_part, d_gate, d_up, down_plane = together(
        d_h2_part.astype(BF16), d_gate, d_up, down_plane
    )
    down_near = scatter_depth(down_plane)
    d_h2_parts = trade(collect_start(d_h2_part))
    grad_gate = dot("td,tu->du", h2_all, d_gate).astype(BF16)
    gate_plane = scatter_plane(grad_gate.reshape(planes, depths, rows_in, units))
    grad_up = dot("td,tu->du", h2_all, d_up).astype(BF16)
    d_h2_parts, down_near, gate_plane, grad_up = together(
        d_h2_parts, down_near, gate_plane, grad_up
    )
    gate_near = scatter_depth(gate_plane)
    up_plane = scatter_plane(grad_up.reshape(planes, depths, rows_in, units))

    side = span // 2
    near_spec = pl.BlockSpec((1, side, 2 * HEAD_DIM), lambda i: (i, 0, 0))
    turn_spec = rows_spec(half_len, HEAD_DIM // 2)
    d_middle, d_attention, d_query, d_near, d_far, d_gains, d_gain_query = run(
        attend_back_kernel,
        [(wide, F32), (wide, BF16), ((rows, cols_all), BF16)]
        + [((batch, side, 2 * HEAD_DIM), F32), ((batch, side, 2 * HEAD_DIM), BF16)]
        + [((8, width), F32), ((8, HEAD_DIM), F32)],
        token_rows, key_cols, starts, query_rot, seen, out_own, out_other,
        g_att, g_feed, g_query, cos, sin, d_h2_parts, middle, attention, dy_low, query_raw,
        grid=(batch,),
        in_specs=place_specs
        + [col_spec, seen_spec]
        + out_specs
        + [same_spec(1, width)] * 2
        + [same_spec(1, HEAD_DIM), turn_spec, turn_spec]
        + [pl.BlockSpec((4, half_len, width), lambda i: (0, i, 0))]
        + [row_spec] * 3
        + [col_spec],
        out_specs=[row_spec, row_spec, col_spec, near_spec, near_spec]
        + [same_spec(8, width), same_spec(8, HEAD_DIM)],
        scratch=[pltpu.VMEM((half_len, cols_all), BF16)],
    )
    d_near, d_far, d_query, d_attention, gate_near, up_plane = together(
        d_near, d_far, d_query, d_attention, gate_near, up_plane
    )
    d_mine = d_near + swap(d_far).astype(F32)
    both_left = jnp.concatenate(
        [dot("td,te->de", d_attention, mixed[:, :q_cols])]
        + [dot("td,te->de", h1, d_query[:, :q_cols])],
        axis=1,
    )
    both_right = jnp.concatenate(
        [dot("td,te->de", d_attention, mixed[:, q_cols:]).astype(BF16)]
        + [dot("td,te->de", h1, d_query[:, q_cols:]).astype(BF16)],
        axis=1,
    )
    both = swap(both_right)
    d_mine, both = together(d_mine, both)
    both = both_left + both.astype(F32)
    both = sum_of(both.reshape(planes, depths, rows_in, cols_all), "fsdp")
    d_kv = d_mine[:, :half_len]
    for back in range(1, back_blocks + 1):
        piece = d_mine[:, back * half_len : (back + 1) * half_len].astype(BF16)
        d_kv = d_kv + shift(piece, -back).astype(F32)
    d_kv, up_plane = together(d_kv, up_plane)
    up_near = scatter_depth(up_plane)
    input_grad, kv_left, kv_right, d_gain_in, d_gain_key = run(
        project_back_kernel,
        [(wide, F32), ((width, HEAD_DIM), F32), ((width, HEAD_DIM), F32)]
        + [((8, width), F32), ((8, HEAD_DIM), F32)],
        core, d_kv.reshape(rows, 2 * HEAD_DIM), key_full, d_query, h1, x_low,
        first_own, first_other, g_in, g_key, cos, sin, d_middle,
        in_specs=smem + in_vmem(12),
    )
    gain_grads = (d_gain_in[0], d_gains[1], d_gains[0], d_gain_out[0])
    gain_grads = gain_grads + (d_gain_query[0], d_gain_key[0])

    gain_sums = [
        jnp.pad(grad.reshape(chunks, 1, -1), ((0, 0), (0, 0), (0, HEAD_DIM - size)))
        for grad, size in zip(gain_grads, gain_sizes)
    ]
    gain_sums = gain_sums + [jnp.zeros((chunks, 8 - len(gains), HEAD_DIM), F32)]
    kv_left, kv_right = (
        jnp.concatenate([grad.reshape(chunks, rows_in, HEAD_DIM)] + gain_sums, axis=1)
        for grad in (kv_left, kv_right)
    )
    last = (kv_left + swap(kv_right.astype(BF16)).astype(F32)).astype(BF16)
    last, both, up_near = together(last, both, up_near)
    last = sum_of(last.reshape((planes, depths) + last.shape[1:]), "fsdp")
    last, gate_near, up_near, down_near = together(last, gate_near, up_near, down_near)
    feed_grads = jnp.stack([gate_near, up_near, down_near], axis=2)
    feed_grads = trade_apart(feed_grads.reshape(4, 3, rows_in, units))
    both = jnp.pad(both, ((0, 0), (0, last.shape[1] - rows_in), (0, 0)))
    last = sum_of(jnp.concatenate([both, last], axis=-1), "ctx")
    both, last = last[:rows_in, :cols_all], last[:, cols_all:]
    out_out, out_query = both[:, :q_cols].T, both[:, q_cols:]
    feed_grads = feed_grads.astype(F32).transpose(1, 2, 0, 3)
    feed_grads = feed_grads.reshape(3, rows_in, 4 * units)[:, :, : 4 * units - spare]
    out_gate, out_up, out_down = feed_grads[0], feed_grads[1], feed_grads[2].T
    out_kv = last[:rows_in]
    kv_other = swap(out_kv)
    out_key = jnp.where(first_core, out_kv, kv_other)
    out_value = jnp.where(first_core, kv_other, out_kv)
    pieces = [last[rows_in + at, :size] for at, size in enumerate(gain_sizes)]

    return (
        layer_out.reshape(micros, seqs, half_len, width),
        input_grad.reshape(micros, seqs, half_len, width),
        pieces[0],
        out_query,
        out_key,
        out_value,
        pieces[4],
        pieces[5],
        out_out,
        pieces[1],
        pieces[2],
        out_gate,
        out_up,
        out_down,
        pieces[3],
    )


def solution(mesh):
    both = ("fsdp", "ctx")
    return jax.shard_map(
        local,
        mesh=mesh,
        in_specs=(
            P(None, "fsdp", "ctx", None),
            P(None, "fsdp", "ctx"),
            P(None, "fsdp", "ctx", None),
            P(both),
            P(both, "tp"),
            P(both, None),
            P(both, None),
            P(both),
            P(both),
            P("tp", both),
            P(both),
            P(both),
            P(both, "tp"),
            P(both, "tp"),
            P("tp", both),
            P(both),
        ),
        out_specs=(
            P(None, "fsdp", ("ctx", "tp"), None),
            P(None, "fsdp", ("ctx", "tp"), None),
            P(both),
            P(both, "tp"),
            P(both, None),
            P(both, None),
            P(both),
            P(both),
            P("tp", both),
            P(both),
            P(both),
            P(both, "tp"),
            P(both, "tp"),
            P("tp", both),
            P(both),
        ),
        check_vma=False,
    )
```

```python
import jax
import jax.numpy as jnp
from jax import lax
from jax.experimental import pallas as pl
from jax.experimental.pallas import tpu as pltpu
from jax.sharding import PartitionSpec as P

HEAD_DIM = 256
WINDOW = 512

EPSILON = 1e-06
ROPE_BASE = 10000.0
SCORE_SCALE = 0.0625
MASKED = -1e30

SEGMENT_NUMBERS = 10

F32 = jnp.float32
BF16 = jnp.bfloat16


def dot(spec, left, right):
    return jnp.einsum(spec, left, right, preferred_element_type=F32)


def normed(values, gain):
    return values * lax.rsqrt(jnp.mean(values * values, axis=-1, keepdims=True) + EPSILON) * gain


def rotations(offsets, depth):
    middle = depth // 2
    inverse = ROPE_BASE ** (-2.0 * jnp.arange(middle, dtype=F32) / depth)
    angle_grid = offsets[..., None] * inverse
    return (jnp.cos(angle_grid), jnp.sin(angle_grid))


GELU_SCALE = 0.7978845608028654
GELU_CUBE = 0.044715


def feed_forward(rows, gate_w, up_w, down_w):
    z = dot("td,du->tu", rows, gate_w)
    up = dot("td,du->tu", rows, up_w)
    square = z * z
    t = jnp.tanh(GELU_SCALE * z * (1.0 + GELU_CUBE * square))
    half_one = 0.5 * (1.0 + t)
    gelu = z * half_one
    slope = half_one + 0.5 * z * (1.0 - t * t) * GELU_SCALE * (1.0 + 3.0 * GELU_CUBE * square)
    hidden = (gelu * up).astype(BF16)
    part = dot("tu,du->td", hidden, down_w).astype(BF16)
    return hidden, gelu.astype(BF16), (up * slope).astype(BF16), part


def contract(left, right, left_dim, right_dim):
    dims = (((left_dim,), (right_dim,)), ((), ()))
    return lax.dot_general(left, right, dims, preferred_element_type=F32)


def normed_back(values, gain, grad):
    scale = lax.rsqrt(jnp.mean(values * values, axis=-1, keepdims=True) + EPSILON)
    inner = gain * grad
    along = jnp.mean(values * inner, axis=-1, keepdims=True)
    d_values = scale * inner - values * (scale * scale * scale) * along
    return d_values, jnp.sum(grad * values * scale, axis=0, keepdims=True)


def turned(values, cosines, sines):
    middle = values.shape[-1] // 2
    first, second = values[:, :middle], values[:, middle:]
    return jnp.concatenate(
        [first * cosines - second * sines, second * cosines + first * sines], axis=-1
    )


def turned_back(values, cosines, sines):
    return turned(values, cosines, -sines)


def head(at):
    return slice(at * HEAD_DIM, (at + 1) * HEAD_DIM)


def project_kernel(core, x, own, other, gain_in, gain_q, gain_k, cosines, sines, *outs):
    h1, raw, query_rot, key_full, pair = outs
    cos, sin = cosines[...], sines[...]
    low = normed(x[...].astype(F32), gain_in[...]).astype(BF16)
    h1[...] = low
    q_cols = own.shape[1] - HEAD_DIM
    left, right = contract(low, own[...], 1, 0), contract(low, other[...], 1, 0)
    first = core[0] == 0
    key = jnp.where(first, left[:, q_cols:], right[:, q_cols:])
    value = jnp.where(first, right[:, q_cols:], left[:, q_cols:])
    key_full[...] = key
    pair[:, :HEAD_DIM] = turned(normed(key, gain_k[...]), cos, sin).astype(BF16)
    pair[:, HEAD_DIM:] = value.astype(BF16)
    raw[:, :q_cols] = left[:, :q_cols]
    raw[:, q_cols:] = right[:, :q_cols]
    for at in range(raw.shape[1] // HEAD_DIM):
        turn = turned(normed(raw[:, head(at)], gain_q[...]), cos, sin)
        query_rot[:, head(at)] = turn.astype(BF16)


def allowed_pairs(tokens_at, keys_at, starts):
    t, u, begin = tokens_at[...], keys_at[...], starts[...]
    return (u <= t) & (t - u < WINDOW) & (u >= begin)


def probabilities(query, keys, allowed):
    scores = jnp.where(allowed, contract(query, keys, 1, 1) * SCORE_SCALE, MASKED)
    lifted = jnp.exp(scores - jnp.max(scores, axis=-1, keepdims=True))
    return lifted / jnp.sum(lifted, axis=-1, keepdims=True)


def attend_kernel(tokens_at, keys_at, starts, query_rot, seen, x, own, other, gain_a, gain_f, *outs):
    mixed, attention, middle, h2 = outs
    allowed = allowed_pairs(tokens_at, keys_at, starts)
    keys, values = seen[0, :, :HEAD_DIM], seen[0, :, HEAD_DIM:]
    for at in range(query_rot.shape[1] // HEAD_DIM):
        prob = probabilities(query_rot[:, head(at)], keys, allowed).astype(BF16)
        mixed[:, head(at)] = contract(prob, values, 1, 0).astype(BF16)
    q_cols = own.shape[1]
    result = contract(mixed[:, :q_cols], own[...], 1, 1)
    result = result + contract(mixed[:, q_cols:], other[...], 1, 1)
    attention[...] = result
    mid = x[...].astype(F32) + normed(result, gain_a[...])
    middle[...] = mid
    h2[...] = normed(mid, gain_f[...]).astype(BF16)


def attend_back_kernel(tokens_at, keys_at, starts, query_rot, seen, own, other, *rest):
    gain_a, gain_f, gain_q, cosines, sines, parts, middle, attention, dy, raw = rest[:10]
    d_middle, d_attention, d_query, d_near, d_far, d_gains, d_gain_q, d_mixed = rest[10:]

    @pl.when(pl.program_id(0) == 0)
    def _():
        d_gains[...] = jnp.zeros_like(d_gains)
        d_gain_q[...] = jnp.zeros_like(d_gain_q)

    d_h2 = parts[0].astype(F32)
    for at in range(1, parts.shape[0]):
        d_h2 = d_h2 + parts[at].astype(F32)
    d_mid, d_gain_f = normed_back(middle[...], gain_f[...], d_h2)
    d_mid = d_mid + dy[...].astype(F32)
    d_middle[...] = d_mid
    d_att, d_gain_a = normed_back(attention[...], gain_a[...], d_mid)
    d_gains[0:1, :] += d_gain_f
    d_gains[1:2, :] += d_gain_a
    d_att = d_att.astype(BF16)
    d_attention[...] = d_att
    q_cols = own.shape[1]
    d_mixed[:, :q_cols] = contract(d_att, own[...], 1, 0).astype(BF16)
    d_mixed[:, q_cols:] = contract(d_att, other[...], 1, 0).astype(BF16)
    allowed = allowed_pairs(tokens_at, keys_at, starts)
    keys, values = seen[0, :, :HEAD_DIM], seen[0, :, HEAD_DIM:]
    d_keys = jnp.zeros(keys.shape, F32)
    d_values = jnp.zeros(keys.shape, F32)
    for at in range(query_rot.shape[1] // HEAD_DIM):
        query, d_mix = query_rot[:, head(at)], d_mixed[:, head(at)]
        prob = probabilities(query, keys, allowed)
        d_prob = contract(d_mix, values, 1, 1)
        delta = jnp.sum(prob * d_prob, axis=-1, keepdims=True)
        d_raw = (prob * (d_prob - delta) * SCORE_SCALE).astype(BF16)
        d_keys = d_keys + contract(d_raw, query, 0, 0)
        d_values = d_values + contract(prob.astype(BF16), d_mix, 0, 0)
        d_rot = turned_back(contract(d_raw, keys, 1, 0), cosines[...], sines[...])
        d_full, d_gain = normed_back(raw[:, head(at)], gain_q[...], d_rot)
        d_query[:, head(at)] = d_full.astype(BF16)
        d_gain_q[0:1, :] += d_gain
    side = keys.shape[0] // 2
    d_near[0, :, :HEAD_DIM] = d_keys[:side]
    d_near[0, :, HEAD_DIM:] = d_values[:side]
    d_far[0, :, :HEAD_DIM] = d_keys[side:].astype(BF16)
    d_far[0, :, HEAD_DIM:] = d_values[side:].astype(BF16)


def project_back_kernel(core, d_kv, key_full, d_query, h1, x, own, other, *rest):
    gain_in, gain_k, cosines, sines, d_middle = rest[:5]
    input_grad, kv_left, kv_right, d_gain_in, d_gain_k = rest[5:]
    d_rot = turned_back(d_kv[:, :HEAD_DIM], cosines[...], sines[...])
    d_key, d_gain = normed_back(key_full[...], gain_k[...], d_rot)
    d_gain_k[...] = jnp.broadcast_to(d_gain, d_gain_k.shape)
    d_key, d_value = d_key.astype(BF16).astype(F32), d_kv[:, HEAD_DIM:]
    first = core[0] == 0
    d_left = jnp.where(first, d_key, d_value).astype(BF16)
    d_right = jnp.where(first, d_value, d_key).astype(BF16)
    low = h1[...]
    kv_left[...] = contract(low, d_left, 0, 0)
    kv_right[...] = contract(low, d_right, 0, 0)
    q_cols = own.shape[1] - HEAD_DIM
    d_h1 = contract(d_query[:, :q_cols], own[:, :q_cols], 1, 1)
    d_h1 = d_h1 + contract(d_query[:, q_cols:], other[:, :q_cols], 1, 1)
    d_h1 = d_h1 + contract(d_left, own[:, q_cols:], 1, 1)
    d_h1 = d_h1 + contract(d_right, other[:, q_cols:], 1, 1)
    d_x, d_gain = normed_back(x[...].astype(F32), gain_in[...], d_h1)
    input_grad[...] = d_middle[...] + d_x
    d_gain_in[...] = jnp.broadcast_to(d_gain, d_gain_in.shape)


def feed_norm_kernel(gain, parts, middle, dy, layer_out, d_feed, d_gain):
    feed = parts[0].astype(F32)
    for at in range(1, parts.shape[0]):
        feed = feed + parts[at].astype(F32)
    layer_out[...] = (middle[...] + normed(feed, gain[...])).astype(BF16)
    d_values, d_row = normed_back(feed, gain[...], dy[...].astype(F32))
    d_feed[...] = d_values.astype(BF16)
    d_gain[...] = jnp.broadcast_to(d_row, d_gain.shape)


def shares_kernel(share, gate, up, down, *outs):
    units = outs[0].shape[2]
    for mine in range(len(outs)):

        @pl.when(share[0] == mine)
        def _():
            for step, out in enumerate(outs):
                start = (mine ^ step) * units
                stop = min(start + units, gate.shape[1])
                for at, weight in enumerate((gate, up, down)):
                    part = weight[:, start:stop]
                    if stop - start < units:
                        blank = jnp.zeros((part.shape[0], start + units - stop), part.dtype)
                        part = jnp.concatenate([part, blank], axis=1)
                    out[at] = part


def run(kernel, outs, *values, grid=None, in_specs=None, out_specs=None, scratch=()):
    more = {}
    if grid is not None:
        more = dict(grid=grid, in_specs=in_specs, out_specs=out_specs)
    elif in_specs is not None:
        more = dict(in_specs=in_specs)
    return pl.pallas_call(
        kernel,
        out_shape=[jax.ShapeDtypeStruct(shape, dtype) for shape, dtype in outs],
        scratch_shapes=list(scratch),
        compiler_params=pltpu.CompilerParams(vmem_limit_bytes=48 * 1024 * 1024),
        cost_estimate=pl.CostEstimate(flops=1, bytes_accessed=1, transcendentals=0),
        **more,
    )(*values)


def in_vmem(count):
    return [pl.BlockSpec(memory_space=pltpu.VMEM)] * count


def rows_spec(rows, width):
    return pl.BlockSpec((rows, width), lambda i: (i, 0))


def same_spec(*shape):
    return pl.BlockSpec(shape, lambda i: (0,) * len(shape))


def swap(value):
    return lax.ppermute(value, "tp", [(0, 1), (1, 0)])


BOTH = ("fsdp", "ctx")


def cross(value, mask):
    count = lax.axis_size("fsdp") * lax.axis_size("ctx")
    return lax.ppermute(value, BOTH, [(i, i ^ mask) for i in range(count)])


def shift(value, step):
    count = lax.axis_size("ctx")
    pairs = [(i, i + step) for i in range(count) if 0 <= i + step < count]
    return lax.ppermute(value, "ctx", pairs)


def together(*values):
    return lax.optimization_barrier(values)


def placed(own, other, bit, dim):
    first = jnp.where(bit == 0, own, other)
    second = jnp.where(bit == 0, other, own)
    return jnp.concatenate([first, second], axis=dim)


def parted(value, bit, dim):
    zero = lax.index_in_dim(value, 0, axis=dim, keepdims=False)
    one = lax.index_in_dim(value, 1, axis=dim, keepdims=False)
    return jnp.where(bit == 0, zero, one), jnp.where(bit == 0, one, zero)


def copies_to(value, axis):
    count = lax.axis_size(axis)
    return lax.all_to_all(jnp.broadcast_to(value[None], (count,) + value.shape), axis, 0, 0)


def gather_rows(value):
    return copies_to(copies_to(value, "ctx"), "fsdp")


def sum_of(parts, axis):
    return jnp.sum(lax.all_to_all(parts.astype(BF16), axis, 0, 0).astype(F32), axis=0)


def scatter_rows(value):
    return sum_of(sum_of(value, "fsdp"), "ctx")


def near_groups():
    planes, depths = lax.axis_size("fsdp"), lax.axis_size("ctx")
    return [
        [(f + x) * depths + c + z for x in (0, 1) for z in (0, 1)]
        for f in range(0, planes, 2)
        for c in range(0, depths, 2)
    ]


def trade(value):
    return lax.all_to_all(value, BOTH, 0, 0, axis_index_groups=near_groups())


def trade_split(value):
    x_bit, z_bit = lax.axis_index("fsdp") & 1, lax.axis_index("ctx") & 1
    low, high = parted(value.reshape((2, 2) + value.shape[1:]), x_bit, 0)
    return parted(low, z_bit, 0) + parted(high, z_bit, 0)


def trade_parts(p0, p1, p2, p3):
    depths = lax.axis_size("ctx")
    return trade_join(p0, cross(p1, 1), cross(p2, depths), cross(p3, depths | 1))


def trade_join(p0, p1, p2, p3):
    x_bit, z_bit = lax.axis_index("fsdp") & 1, lax.axis_index("ctx") & 1
    low = placed(p0[None], p1[None], z_bit, 0)
    high = placed(p2[None], p3[None], z_bit, 0)
    return placed(low[None], high[None], x_bit, 0).reshape((4,) + p0.shape)


def far_bits():
    planes, depths = lax.axis_size("fsdp"), lax.axis_size("ctx")
    f_place, c_place = lax.axis_index("fsdp"), lax.axis_index("ctx")
    f_count, c_count = (planes - 1).bit_length(), (depths - 1).bit_length()
    c_bits = [(1 << k, (c_place >> k) & 1) for k in range(c_count - 1, 0, -1)]
    f_bits = [(depths << k, (f_place >> k) & 1) for k in range(f_count - 1, 0, -1)]
    return c_bits, f_bits


def gather_depth(value):
    c_bits, _ = far_bits()
    for mask, bit in c_bits[::-1]:
        value = placed(value, cross(value, mask), bit, 1)
    return value


def gather_plane(value):
    _, f_bits = far_bits()
    for mask, bit in f_bits[::-1]:
        value = placed(value, cross(value, mask), bit, 0)
    return value


def scatter_plane(value):
    _, f_bits = far_bits()
    for mask, bit in f_bits:
        halves = value.reshape((2, value.shape[0] // 2) + value.shape[1:])
        mine, other = parted(halves, bit, 0)
        value = (mine.astype(F32) + cross(other, mask).astype(F32)).astype(BF16)
    return value


def scatter_depth(value):
    c_bits, _ = far_bits()
    for mask, bit in c_bits:
        halves = value.reshape((2, 2, value.shape[1] // 2) + value.shape[2:])
        mine, other = parted(halves, bit, 1)
        value = (mine.astype(F32) + cross(other, mask).astype(F32)).astype(BF16)
    return value


def spread_start(rows):
    mine = trade(jnp.broadcast_to(rows[None], (4,) + rows.shape))
    return mine.reshape((-1,) + rows.shape[1:])


def spread(rows):
    mine = spread_start(rows)
    return jnp.concatenate([mine, swap(mine)], axis=0)


def collect_start(part):
    half = part.shape[0] // 2
    own = part[:half].astype(F32) + swap(part[half:]).astype(F32)
    return own.astype(BF16).reshape(4, half // 4, part.shape[1])


def local(
    tokens,
    segments,
    cotangent,
    norm_input,
    query_weight,
    key_weight,
    value_weight,
    norm_query,
    norm_key,
    out_weight,
    norm_attention,
    norm_feed,
    gate_weight,
    up_weight,
    down_weight,
    norm_feed_out,
):
    micros, seqs, block_len, width = tokens.shape
    planes = lax.axis_size("fsdp")
    depths = lax.axis_size("ctx")
    chunks = planes * depths
    ctx_place = lax.axis_index("ctx")
    tp_place = lax.axis_index("tp")
    first_core = tp_place == 0
    half_len = block_len // lax.axis_size("tp")
    back_blocks = -(-WINDOW // block_len)
    rows_in = norm_input.shape[0]
    small = norm_query.shape[0]
    heads_half = query_weight.shape[1] // HEAD_DIM
    q_cols = query_weight.shape[1]
    units = -(-gate_weight.shape[1] // (4 * 128)) * 128
    spare = 4 * units - gate_weight.shape[1]
    numbers = jnp.arange(SEGMENT_NUMBERS, dtype=jnp.int32)
    counts = jnp.sum((segments[..., None] == numbers).astype(F32), axis=2).astype(BF16)
    kv_shard = jnp.where(first_core, key_weight, value_weight)
    gains = (norm_input, norm_attention, norm_feed, norm_feed_out, norm_query, norm_key)
    gain_sizes = [gain.shape[0] for gain in gains]
    first_cols = q_cols + HEAD_DIM

    def row(*values):
        values = jnp.stack(values)
        return jnp.pad(values, ((0, 0), (0, first_cols - values.shape[1])))

    more = [row(*gains[:4]), row(*gains[4:]), row(counts.reshape(-1))]
    more = more + [jnp.zeros((1, first_cols), BF16)]
    first_pack = jnp.concatenate([query_weight, kv_shard], axis=1)
    first_pack = jnp.concatenate([first_pack] + more, axis=0)
    first_pack = jnp.broadcast_to(first_pack[None], (depths,) + first_pack.shape)
    first_pack, gate_weight, up_weight, down_weight = together(
        first_pack, gate_weight, up_weight, down_weight
    )
    out_pack = copies_to(out_weight.T, "ctx")
    first_pack, out_pack = together(first_pack, out_pack)
    first_pack = lax.all_to_all(first_pack, "ctx", 0, 0)

    share = ((lax.axis_index("fsdp") & 1) * 2 + (ctx_place & 1)).reshape(1)
    shares = run(
        shares_kernel,
        [((3, rows_in, units), BF16)] * 4,
        share, gate_weight, up_weight, down_weight.T,
        in_specs=[pl.BlockSpec(memory_space=pltpu.SMEM)] + in_vmem(3),
    )
    feed_parts = trade_parts(*shares)
    first_pack, feed_parts = together(first_pack, feed_parts)
    counts_all = first_pack[:, rows_in + len(gains), : counts.size].astype(F32)
    counts_all = jnp.sum(counts_all, axis=0).reshape(counts.shape)

    feed_parts = feed_parts.reshape(2, 2, 3, rows_in, units)
    gate_near, up_near, down_near = (feed_parts[:, :, which] for which in range(3))
    gate_deep = gather_depth(gate_near)
    first_pack = copies_to(first_pack, "fsdp")
    first_pack, gate_deep, up_near, down_near, out_pack = together(
        first_pack, gate_deep, up_near, down_near, out_pack
    )

    first_pack = first_pack.reshape(chunks, rows_in + 8, first_cols)
    first_own = first_pack[:, :rows_in].reshape(width, first_cols)
    first_other = swap(first_own)
    gain_input, gain_attention, gain_feed, gain_feed_out, gain_query, gain_key = (
        first_pack[:, rows_in + at, :size].astype(F32).reshape(-1)
        for at, size in enumerate(gain_sizes)
    )
    up_deep = gather_depth(up_near)
    gate_w = gather_plane(gate_deep).reshape(width, units)

    half_at = tp_place * half_len
    seg_half = lax.dynamic_slice_in_dim(segments, half_at, half_len, 2)
    earlier = numbers < seg_half[..., None]
    starts = jnp.sum(jnp.where(earlier, counts_all[:, :, None, :], 0.0), axis=-1)
    starts = starts.astype(jnp.int32)
    token_place = ctx_place * block_len + half_at + jnp.arange(half_len, dtype=jnp.int32)
    cosines, sines = rotations((token_place - starts).astype(F32), HEAD_DIM)
    within = jnp.arange(half_len, dtype=jnp.int32)
    key_place = jnp.concatenate(
        [
            (ctx_place - back) * block_len + side * half_len + within
            for side in (tp_place, 1 - tp_place)
            for back in range(back_blocks + 1)
        ]
    )

    batch = micros * seqs
    rows = batch * half_len
    x_low = lax.dynamic_slice_in_dim(tokens, half_at, half_len, 2).reshape(rows, width)
    dy_low = lax.dynamic_slice_in_dim(cotangent, half_at, half_len, 2).reshape(rows, width)
    cos, sin = cosines.reshape(rows, -1), sines.reshape(rows, -1)
    starts = starts.reshape(rows, 1)
    core = tp_place.reshape(1)
    gains_wide = [
        gain[None]
        for gain in (gain_input, gain_attention, gain_feed, gain_feed_out, gain_query, gain_key)
    ]
    g_in, g_att, g_feed, g_out, g_query, g_key = gains_wide
    smem = [pl.BlockSpec(memory_space=pltpu.SMEM)]
    wide, cols_all = (rows, width), 2 * q_cols

    h1, query_raw, query_rot, key_full, pair = run(
        project_kernel,
        [(wide, BF16), ((rows, cols_all), F32), ((rows, cols_all), BF16)]
        + [((rows, HEAD_DIM), F32), ((rows, 2 * HEAD_DIM), BF16)],
        core, x_low, first_own, first_other, g_in, g_query, g_key, cos, sin,
        in_specs=smem + in_vmem(8),
    )
    up_deep, gate_w, out_pack, down_near = together(up_deep, gate_w, out_pack, down_near)
    down_deep = gather_depth(down_near)
    up_w = gather_plane(up_deep).reshape(width, units)
    out_own = copies_to(out_pack, "fsdp").reshape(width, q_cols)
    pair = pair.reshape(batch, half_len, 2 * HEAD_DIM)
    mine = jnp.concatenate(
        [pair] + [shift(pair, back) for back in range(1, back_blocks + 1)], axis=1
    )
    seen = jnp.concatenate([mine, swap(mine)], axis=1)
    seen, up_w, out_own, down_deep = together(seen, up_w, out_own, down_deep)
    out_other = swap(out_own)
    down_w = gather_plane(down_deep).reshape(width, units)
    span = seen.shape[1]
    token_rows, key_cols = token_place[:, None], key_place[None]
    place_specs = [same_spec(half_len, 1), same_spec(1, span), rows_spec(half_len, 1)]
    seen_spec = pl.BlockSpec((1, span, 2 * HEAD_DIM), lambda i: (i, 0, 0))
    row_spec, col_spec = rows_spec(half_len, width), rows_spec(half_len, cols_all)
    out_specs = [same_spec(width, q_cols)] * 2
    mixed, attention, middle, h2 = run(
        attend_kernel,
        [((rows, cols_all), BF16), (wide, F32), (wide, F32), (wide, BF16)],
        token_rows, key_cols, starts, query_rot, seen, x_low, out_own, out_other, g_att, g_feed,
        grid=(batch,),
        in_specs=place_specs
        + [col_spec, seen_spec, row_spec]
        + out_specs
        + [same_spec(1, width)] * 2,
        out_specs=[col_spec] + [row_spec] * 3,
    )

    h2_mine, down_w = together(spread_start(h2), down_w)
    h2_all = jnp.concatenate([h2_mine, swap(h2_mine)], axis=0)
    hidden, by_up, by_gate, part = feed_forward(h2_all, gate_w, up_w, down_w)
    feed_parts = trade(collect_start(part))
    layer_out, d_feed, d_gain_out = run(
        feed_norm_kernel,
        [(wide, BF16), (wide, BF16), ((8, width), F32)],
        g_out, feed_parts, middle, dy_low,
    )
    d_feed_all = spread(d_feed)
    grad_down = dot("td,tu->du", d_feed_all, hidden).astype(BF16)
    d_feed_all, grad_down = together(d_feed_all, grad_down)
    down_plane = scatter_plane(grad_down.reshape(planes, depths, rows_in, units))
    d_hidden = dot("td,du->tu", d_feed_all, down_w)
    d_gate = (d_hidden * by_gate.astype(F32)).astype(BF16)
    d_up = (d_hidden * by_up.astype(F32)).astype(BF16)
    d_h2_part = dot("tu,du->td", d_gate, gate_w) + dot("tu,du->td", d_up, up_w)
    d_h2_part, d_gate, d_up, down_plane = together(
        d_h2_part.astype(BF16), d_gate, d_up, down_plane
    )
    down_near = scatter_depth(down_plane)
    d_h2_parts = trade(collect_start(d_h2_part))
    grad_gate = dot("td,tu->du", h2_all, d_gate).astype(BF16)
    gate_plane = scatter_plane(grad_gate.reshape(planes, depths, rows_in, units))
    grad_up = dot("td,tu->du", h2_all, d_up).astype(BF16)
    d_h2_parts, down_near, gate_plane, grad_up = together(
        d_h2_parts, down_near, gate_plane, grad_up
    )
    gate_near = scatter_depth(gate_plane)
    up_plane = scatter_plane(grad_up.reshape(planes, depths, rows_in, units))

    side = span // 2
    near_spec = pl.BlockSpec((1, side, 2 * HEAD_DIM), lambda i: (i, 0, 0))
    turn_spec = rows_spec(half_len, HEAD_DIM // 2)
    d_middle, d_attention, d_query, d_near, d_far, d_gains, d_gain_query = run(
        attend_back_kernel,
        [(wide, F32), (wide, BF16), ((rows, cols_all), BF16)]
        + [((batch, side, 2 * HEAD_DIM), F32), ((batch, side, 2 * HEAD_DIM), BF16)]
        + [((8, width), F32), ((8, HEAD_DIM), F32)],
        token_rows, key_cols, starts, query_rot, seen, out_own, out_other,
        g_att, g_feed, g_query, cos, sin, d_h2_parts, middle, attention, dy_low, query_raw,
        grid=(batch,),
        in_specs=place_specs
        + [col_spec, seen_spec]
        + out_specs
        + [same_spec(1, width)] * 2
        + [same_spec(1, HEAD_DIM), turn_spec, turn_spec]
        + [pl.BlockSpec((4, half_len, width), lambda i: (0, i, 0))]
        + [row_spec] * 3
        + [col_spec],
        out_specs=[row_spec, row_spec, col_spec, near_spec, near_spec]
        + [same_spec(8, width), same_spec(8, HEAD_DIM)],
        scratch=[pltpu.VMEM((half_len, cols_all), BF16)],
    )
    d_near, d_far, d_query, d_attention, gate_near, up_plane = together(
        d_near, d_far, d_query, d_attention, gate_near, up_plane
    )
    d_mine = d_near + swap(d_far).astype(F32)
    both_left = jnp.concatenate(
        [dot("td,te->de", d_attention, mixed[:, :q_cols])]
        + [dot("td,te->de", h1, d_query[:, :q_cols])],
        axis=1,
    )
    both_right = jnp.concatenate(
        [dot("td,te->de", d_attention, mixed[:, q_cols:]).astype(BF16)]
        + [dot("td,te->de", h1, d_query[:, q_cols:]).astype(BF16)],
        axis=1,
    )
    both = swap(both_right)
    d_mine, both = together(d_mine, both)
    both = both_left + both.astype(F32)
    both = sum_of(both.reshape(planes, depths, rows_in, cols_all), "fsdp")
    d_kv = d_mine[:, :half_len]
    for back in range(1, back_blocks + 1):
        piece = d_mine[:, back * half_len : (back + 1) * half_len].astype(BF16)
        d_kv = d_kv + shift(piece, -back).astype(F32)
    d_kv, up_plane = together(d_kv, up_plane)
    up_near = scatter_depth(up_plane)
    input_grad, kv_left, kv_right, d_gain_in, d_gain_key = run(
        project_back_kernel,
        [(wide, F32), ((width, HEAD_DIM), F32), ((width, HEAD_DIM), F32)]
        + [((8, width), F32), ((8, HEAD_DIM), F32)],
        core, d_kv.reshape(rows, 2 * HEAD_DIM), key_full, d_query, h1, x_low,
        first_own, first_other, g_in, g_key, cos, sin, d_middle,
        in_specs=smem + in_vmem(12),
    )
    gain_grads = (d_gain_in[0], d_gains[1], d_gains[0], d_gain_out[0])
    gain_grads = gain_grads + (d_gain_query[0], d_gain_key[0])

    gain_sums = [
        jnp.pad(grad.reshape(chunks, 1, -1), ((0, 0), (0, 0), (0, HEAD_DIM - size)))
        for grad, size in zip(gain_grads, gain_sizes)
    ]
    gain_sums = gain_sums + [jnp.zeros((chunks, 8 - len(gains), HEAD_DIM), F32)]
    kv_left, kv_right = (
        jnp.concatenate([grad.reshape(chunks, rows_in, HEAD_DIM)] + gain_sums, axis=1)
        for grad in (kv_left, kv_right)
    )
    last = (kv_left + swap(kv_right.astype(BF16)).astype(F32)).astype(BF16)
    last, both, up_near = together(last, both, up_near)
    feed_grads = jnp.stack([gate_near, up_near, down_near], axis=2)
    own, near, wide, diagonal = trade_split(feed_grads.reshape(4, 3, rows_in, units))
    near = cross(near, 1)
    last = sum_of(last.reshape((planes, depths) + last.shape[1:]), "fsdp")
    last, near, wide, diagonal = together(last, near, wide, diagonal)
    wide, diagonal = cross(wide, depths), cross(diagonal, depths | 1)
    feed_grads = trade_join(own, near, wide, diagonal)
    both = jnp.pad(both, ((0, 0), (0, last.shape[1] - rows_in), (0, 0)))
    last = sum_of(jnp.concatenate([both, last], axis=-1), "ctx")
    both, last = last[:rows_in, :cols_all], last[:, cols_all:]
    out_out, out_query = both[:, :q_cols].T, both[:, q_cols:]
    feed_grads = feed_grads.astype(F32).transpose(1, 2, 0, 3)
    feed_grads = feed_grads.reshape(3, rows_in, 4 * units)[:, :, : 4 * units - spare]
    out_gate, out_up, out_down = feed_grads[0], feed_grads[1], feed_grads[2].T
    out_kv = last[:rows_in]
    kv_other = swap(out_kv)
    out_key = jnp.where(first_core, out_kv, kv_other)
    out_value = jnp.where(first_core, kv_other, out_kv)
    pieces = [last[rows_in + at, :size] for at, size in enumerate(gain_sizes)]

    return (
        layer_out.reshape(micros, seqs, half_len, width),
        input_grad.reshape(micros, seqs, half_len, width),
        pieces[0],
        out_query,
        out_key,
        out_value,
        pieces[4],
        pieces[5],
        out_out,
        pieces[1],
        pieces[2],
        out_gate,
        out_up,
        out_down,
        pieces[3],
    )


def solution(mesh):
    both = ("fsdp", "ctx")
    return jax.shard_map(
        local,
        mesh=mesh,
        in_specs=(
            P(None, "fsdp", "ctx", None),
            P(None, "fsdp", "ctx"),
            P(None, "fsdp", "ctx", None),
            P(both),
            P(both, "tp"),
            P(both, None),
            P(both, None),
            P(both),
            P(both),
            P("tp", both),
            P(both),
            P(both),
            P(both, "tp"),
            P(both, "tp"),
            P("tp", both),
            P(both),
        ),
        out_specs=(
            P(None, "fsdp", ("ctx", "tp"), None),
            P(None, "fsdp", ("ctx", "tp"), None),
            P(both),
            P(both, "tp"),
            P(both, None),
            P(both, None),
            P(both),
            P(both),
            P("tp", both),
            P(both),
            P(both),
            P(both, "tp"),
            P(both, "tp"),
            P("tp", both),
            P(both),
        ),
        check_vma=False,
    )
```

```python
import jax
import jax.numpy as jnp
from jax import lax
from jax.experimental import pallas as pl
from jax.experimental.pallas import tpu as pltpu
from jax.sharding import PartitionSpec as P

HEAD_DIM = 256
WINDOW = 512

EPSILON = 1e-06
ROPE_BASE = 10000.0
SCORE_SCALE = 0.0625
MASKED = -1e30

SEGMENT_NUMBERS = 10

F32 = jnp.float32
BF16 = jnp.bfloat16


def dot(spec, left, right):
    return jnp.einsum(spec, left, right, preferred_element_type=F32)


def normed(values, gain):
    return values * lax.rsqrt(jnp.mean(values * values, axis=-1, keepdims=True) + EPSILON) * gain


def rotations(offsets, depth):
    middle = depth // 2
    inverse = ROPE_BASE ** (-2.0 * jnp.arange(middle, dtype=F32) / depth)
    angle_grid = offsets[..., None] * inverse
    return (jnp.cos(angle_grid), jnp.sin(angle_grid))


GELU_SCALE = 0.7978845608028654
GELU_CUBE = 0.044715


def feed_forward(rows, gate_w, up_w, down_w):
    z = dot("td,du->tu", rows, gate_w)
    up = dot("td,du->tu", rows, up_w)
    square = z * z
    t = jnp.tanh(GELU_SCALE * z * (1.0 + GELU_CUBE * square))
    half_one = 0.5 * (1.0 + t)
    gelu = z * half_one
    slope = half_one + 0.5 * z * (1.0 - t * t) * GELU_SCALE * (1.0 + 3.0 * GELU_CUBE * square)
    hidden = (gelu * up).astype(BF16)
    part = dot("tu,du->td", hidden, down_w).astype(BF16)
    return hidden, gelu.astype(BF16), (up * slope).astype(BF16), part


def contract(left, right, left_dim, right_dim):
    dims = (((left_dim,), (right_dim,)), ((), ()))
    return lax.dot_general(left, right, dims, preferred_element_type=F32)


def normed_back(values, gain, grad):
    scale = lax.rsqrt(jnp.mean(values * values, axis=-1, keepdims=True) + EPSILON)
    inner = gain * grad
    along = jnp.mean(values * inner, axis=-1, keepdims=True)
    d_values = scale * inner - values * (scale * scale * scale) * along
    return d_values, jnp.sum(grad * values * scale, axis=0, keepdims=True)


def turned(values, cosines, sines):
    middle = values.shape[-1] // 2
    first, second = values[:, :middle], values[:, middle:]
    return jnp.concatenate(
        [first * cosines - second * sines, second * cosines + first * sines], axis=-1
    )


def turned_back(values, cosines, sines):
    return turned(values, cosines, -sines)


def head(at):
    return slice(at * HEAD_DIM, (at + 1) * HEAD_DIM)


def project_kernel(core, x, own, other, gain_in, gain_q, gain_k, cosines, sines, *outs):
    h1, raw, query_rot, key_full, pair = outs
    cos, sin = cosines[...], sines[...]
    low = normed(x[...].astype(F32), gain_in[...]).astype(BF16)
    h1[...] = low
    q_cols = own.shape[1] - HEAD_DIM
    left, right = contract(low, own[...], 1, 0), contract(low, other[...], 1, 0)
    first = core[0] == 0
    key = jnp.where(first, left[:, q_cols:], right[:, q_cols:])
    value = jnp.where(first, right[:, q_cols:], left[:, q_cols:])
    key_full[...] = key
    pair[:, :HEAD_DIM] = turned(normed(key, gain_k[...]), cos, sin).astype(BF16)
    pair[:, HEAD_DIM:] = value.astype(BF16)
    raw[:, :q_cols] = left[:, :q_cols]
    raw[:, q_cols:] = right[:, :q_cols]
    for at in range(raw.shape[1] // HEAD_DIM):
        turn = turned(normed(raw[:, head(at)], gain_q[...]), cos, sin)
        query_rot[:, head(at)] = turn.astype(BF16)


def allowed_pairs(tokens_at, keys_at, starts):
    t, u, begin = tokens_at[...], keys_at[...], starts[...]
    return (u <= t) & (t - u < WINDOW) & (u >= begin)


def probabilities(query, keys, allowed):
    scores = jnp.where(allowed, contract(query, keys, 1, 1) * SCORE_SCALE, MASKED)
    lifted = jnp.exp(scores - jnp.max(scores, axis=-1, keepdims=True))
    return lifted / jnp.sum(lifted, axis=-1, keepdims=True)


def attend_kernel(tokens_at, keys_at, starts, query_rot, seen, x, own, other, gain_a, gain_f, *outs):
    mixed, attention, middle, h2 = outs
    allowed = allowed_pairs(tokens_at, keys_at, starts)
    keys, values = seen[0, :, :HEAD_DIM], seen[0, :, HEAD_DIM:]
    for at in range(query_rot.shape[1] // HEAD_DIM):
        prob = probabilities(query_rot[:, head(at)], keys, allowed).astype(BF16)
        mixed[:, head(at)] = contract(prob, values, 1, 0).astype(BF16)
    q_cols = own.shape[1]
    result = contract(mixed[:, :q_cols], own[...], 1, 1)
    result = result + contract(mixed[:, q_cols:], other[...], 1, 1)
    attention[...] = result
    mid = x[...].astype(F32) + normed(result, gain_a[...])
    middle[...] = mid
    h2[...] = normed(mid, gain_f[...]).astype(BF16)


def attend_back_kernel(tokens_at, keys_at, starts, query_rot, seen, own, other, *rest):
    gain_a, gain_f, gain_q, cosines, sines, parts, middle, attention, dy, raw = rest[:10]
    d_middle, d_attention, d_query, d_near, d_far, d_gains, d_gain_q, d_mixed = rest[10:]

    @pl.when(pl.program_id(0) == 0)
    def _():
        d_gains[...] = jnp.zeros_like(d_gains)
        d_gain_q[...] = jnp.zeros_like(d_gain_q)

    d_h2 = parts[0].astype(F32)
    for at in range(1, parts.shape[0]):
        d_h2 = d_h2 + parts[at].astype(F32)
    d_mid, d_gain_f = normed_back(middle[...], gain_f[...], d_h2)
    d_mid = d_mid + dy[...].astype(F32)
    d_middle[...] = d_mid
    d_att, d_gain_a = normed_back(attention[...], gain_a[...], d_mid)
    d_gains[0:1, :] += d_gain_f
    d_gains[1:2, :] += d_gain_a
    d_att = d_att.astype(BF16)
    d_attention[...] = d_att
    q_cols = own.shape[1]
    d_mixed[:, :q_cols] = contract(d_att, own[...], 1, 0).astype(BF16)
    d_mixed[:, q_cols:] = contract(d_att, other[...], 1, 0).astype(BF16)
    allowed = allowed_pairs(tokens_at, keys_at, starts)
    keys, values = seen[0, :, :HEAD_DIM], seen[0, :, HEAD_DIM:]
    d_keys = jnp.zeros(keys.shape, F32)
    d_values = jnp.zeros(keys.shape, F32)
    for at in range(query_rot.shape[1] // HEAD_DIM):
        query, d_mix = query_rot[:, head(at)], d_mixed[:, head(at)]
        prob = probabilities(query, keys, allowed)
        d_prob = contract(d_mix, values, 1, 1)
        delta = jnp.sum(prob * d_prob, axis=-1, keepdims=True)
        d_raw = (prob * (d_prob - delta) * SCORE_SCALE).astype(BF16)
        d_keys = d_keys + contract(d_raw, query, 0, 0)
        d_values = d_values + contract(prob.astype(BF16), d_mix, 0, 0)
        d_rot = turned_back(contract(d_raw, keys, 1, 0), cosines[...], sines[...])
        d_full, d_gain = normed_back(raw[:, head(at)], gain_q[...], d_rot)
        d_query[:, head(at)] = d_full.astype(BF16)
        d_gain_q[0:1, :] += d_gain
    side = keys.shape[0] // 2
    d_near[0, :, :HEAD_DIM] = d_keys[:side]
    d_near[0, :, HEAD_DIM:] = d_values[:side]
    d_far[0, :, :HEAD_DIM] = d_keys[side:].astype(BF16)
    d_far[0, :, HEAD_DIM:] = d_values[side:].astype(BF16)


def project_back_kernel(core, d_kv, key_full, d_query, h1, x, own, other, *rest):
    gain_in, gain_k, cosines, sines, d_middle = rest[:5]
    input_grad, kv_left, kv_right, d_gain_in, d_gain_k = rest[5:]
    d_rot = turned_back(d_kv[:, :HEAD_DIM], cosines[...], sines[...])
    d_key, d_gain = normed_back(key_full[...], gain_k[...], d_rot)
    d_gain_k[...] = jnp.broadcast_to(d_gain, d_gain_k.shape)
    d_key, d_value = d_key.astype(BF16).astype(F32), d_kv[:, HEAD_DIM:]
    first = core[0] == 0
    d_left = jnp.where(first, d_key, d_value).astype(BF16)
    d_right = jnp.where(first, d_value, d_key).astype(BF16)
    low = h1[...]
    kv_left[...] = contract(low, d_left, 0, 0)
    kv_right[...] = contract(low, d_right, 0, 0).astype(BF16)
    q_cols = own.shape[1] - HEAD_DIM
    d_h1 = contract(d_query[:, :q_cols], own[:, :q_cols], 1, 1)
    d_h1 = d_h1 + contract(d_query[:, q_cols:], other[:, :q_cols], 1, 1)
    d_h1 = d_h1 + contract(d_left, own[:, q_cols:], 1, 1)
    d_h1 = d_h1 + contract(d_right, other[:, q_cols:], 1, 1)
    d_x, d_gain = normed_back(x[...].astype(F32), gain_in[...], d_h1)
    input_grad[...] = d_middle[...] + d_x
    d_gain_in[...] = jnp.broadcast_to(d_gain, d_gain_in.shape)


def feed_norm_kernel(gain, parts, middle, dy, layer_out, d_feed, d_gain):
    feed = parts[0].astype(F32)
    for at in range(1, parts.shape[0]):
        feed = feed + parts[at].astype(F32)
    layer_out[...] = (middle[...] + normed(feed, gain[...])).astype(BF16)
    d_values, d_row = normed_back(feed, gain[...], dy[...].astype(F32))
    d_feed[...] = d_values.astype(BF16)
    d_gain[...] = jnp.broadcast_to(d_row, d_gain.shape)


def shares_kernel(share, gate, up, down, *outs):
    units = outs[0].shape[2]
    for mine in range(len(outs)):

        @pl.when(share[0] == mine)
        def _():
            for step, out in enumerate(outs):
                start = (mine ^ step) * units
                stop = min(start + units, gate.shape[1])
                for at, weight in enumerate((gate, up, down)):
                    part = weight[:, start:stop]
                    if stop - start < units:
                        blank = jnp.zeros((part.shape[0], start + units - stop), part.dtype)
                        part = jnp.concatenate([part, blank], axis=1)
                    out[at] = part


def run(kernel, outs, *values, grid=None, in_specs=None, out_specs=None, scratch=()):
    more = {}
    if grid is not None:
        more = dict(grid=grid, in_specs=in_specs, out_specs=out_specs)
    elif in_specs is not None:
        more = dict(in_specs=in_specs)
    return pl.pallas_call(
        kernel,
        out_shape=[jax.ShapeDtypeStruct(shape, dtype) for shape, dtype in outs],
        scratch_shapes=list(scratch),
        compiler_params=pltpu.CompilerParams(vmem_limit_bytes=48 * 1024 * 1024),
        cost_estimate=pl.CostEstimate(flops=1, bytes_accessed=1, transcendentals=0),
        **more,
    )(*values)


def in_vmem(count):
    return [pl.BlockSpec(memory_space=pltpu.VMEM)] * count


def rows_spec(rows, width):
    return pl.BlockSpec((rows, width), lambda i: (i, 0))


def same_spec(*shape):
    return pl.BlockSpec(shape, lambda i: (0,) * len(shape))


def swap(value):
    return lax.ppermute(value, "tp", [(0, 1), (1, 0)])


BOTH = ("fsdp", "ctx")


def cross(value, mask):
    count = lax.axis_size("fsdp") * lax.axis_size("ctx")
    return lax.ppermute(value, BOTH, [(i, i ^ mask) for i in range(count)])


def shift(value, step):
    count = lax.axis_size("ctx")
    pairs = [(i, i + step) for i in range(count) if 0 <= i + step < count]
    return lax.ppermute(value, "ctx", pairs)


def together(*values):
    return lax.optimization_barrier(values)


def placed(own, other, bit, dim):
    first = jnp.where(bit == 0, own, other)
    second = jnp.where(bit == 0, other, own)
    return jnp.concatenate([first, second], axis=dim)


def parted(value, bit, dim):
    zero = lax.index_in_dim(value, 0, axis=dim, keepdims=False)
    one = lax.index_in_dim(value, 1, axis=dim, keepdims=False)
    return jnp.where(bit == 0, zero, one), jnp.where(bit == 0, one, zero)


def copies_to(value, axis):
    count = lax.axis_size(axis)
    return lax.all_to_all(jnp.broadcast_to(value[None], (count,) + value.shape), axis, 0, 0)


def gather_rows(value):
    return copies_to(copies_to(value, "ctx"), "fsdp")


def sum_of(parts, axis):
    return jnp.sum(lax.all_to_all(parts.astype(BF16), axis, 0, 0).astype(F32), axis=0)


def scatter_rows(value):
    return sum_of(sum_of(value, "fsdp"), "ctx")


def near_groups():
    planes, depths = lax.axis_size("fsdp"), lax.axis_size("ctx")
    return [
        [(f + x) * depths + c + z for x in (0, 1) for z in (0, 1)]
        for f in range(0, planes, 2)
        for c in range(0, depths, 2)
    ]


def trade(value):
    return lax.all_to_all(value, BOTH, 0, 0, axis_index_groups=near_groups())


def trade_split(value):
    x_bit, z_bit = lax.axis_index("fsdp") & 1, lax.axis_index("ctx") & 1
    low, high = parted(value.reshape((2, 2) + value.shape[1:]), x_bit, 0)
    return parted(low, z_bit, 0) + parted(high, z_bit, 0)


def trade_parts(p0, p1, p2, p3):
    depths = lax.axis_size("ctx")
    return trade_join(p0, cross(p1, 1), cross(p2, depths), cross(p3, depths | 1))


def trade_join(p0, p1, p2, p3):
    x_bit, z_bit = lax.axis_index("fsdp") & 1, lax.axis_index("ctx") & 1
    low = placed(p0[None], p1[None], z_bit, 0)
    high = placed(p2[None], p3[None], z_bit, 0)
    return placed(low[None], high[None], x_bit, 0).reshape((4,) + p0.shape)


def far_bits():
    planes, depths = lax.axis_size("fsdp"), lax.axis_size("ctx")
    f_place, c_place = lax.axis_index("fsdp"), lax.axis_index("ctx")
    f_count, c_count = (planes - 1).bit_length(), (depths - 1).bit_length()
    c_bits = [(1 << k, (c_place >> k) & 1) for k in range(c_count - 1, 0, -1)]
    f_bits = [(depths << k, (f_place >> k) & 1) for k in range(f_count - 1, 0, -1)]
    return c_bits, f_bits


def gather_depth(value):
    c_bits, _ = far_bits()
    for mask, bit in c_bits[::-1]:
        value = placed(value, cross(value, mask), bit, 1)
    return value


def gather_plane(value):
    _, f_bits = far_bits()
    for mask, bit in f_bits[::-1]:
        value = placed(value, cross(value, mask), bit, 0)
    return value


def scatter_plane(value):
    _, f_bits = far_bits()
    for mask, bit in f_bits:
        halves = value.reshape((2, value.shape[0] // 2) + value.shape[1:])
        mine, other = parted(halves, bit, 0)
        value = (mine.astype(F32) + cross(other, mask).astype(F32)).astype(BF16)
    return value


def scatter_depth(value):
    c_bits, _ = far_bits()
    for mask, bit in c_bits:
        halves = value.reshape((2, 2, value.shape[1] // 2) + value.shape[2:])
        mine, other = parted(halves, bit, 1)
        value = (mine.astype(F32) + cross(other, mask).astype(F32)).astype(BF16)
    return value


def spread_start(rows):
    mine = trade(jnp.broadcast_to(rows[None], (4,) + rows.shape))
    return mine.reshape((-1,) + rows.shape[1:])


def spread(rows):
    mine = spread_start(rows)
    return jnp.concatenate([mine, swap(mine)], axis=0)


def collect_start(part):
    half = part.shape[0] // 2
    own = part[:half].astype(F32) + swap(part[half:]).astype(F32)
    return own.astype(BF16).reshape(4, half // 4, part.shape[1])


def local(
    tokens,
    segments,
    cotangent,
    norm_input,
    query_weight,
    key_weight,
    value_weight,
    norm_query,
    norm_key,
    out_weight,
    norm_attention,
    norm_feed,
    gate_weight,
    up_weight,
    down_weight,
    norm_feed_out,
):
    micros, seqs, block_len, width = tokens.shape
    planes = lax.axis_size("fsdp")
    depths = lax.axis_size("ctx")
    chunks = planes * depths
    ctx_place = lax.axis_index("ctx")
    tp_place = lax.axis_index("tp")
    first_core = tp_place == 0
    half_len = block_len // lax.axis_size("tp")
    back_blocks = -(-WINDOW // block_len)
    rows_in = norm_input.shape[0]
    small = norm_query.shape[0]
    heads_half = query_weight.shape[1] // HEAD_DIM
    q_cols = query_weight.shape[1]
    units = -(-gate_weight.shape[1] // (4 * 128)) * 128
    spare = 4 * units - gate_weight.shape[1]
    numbers = jnp.arange(SEGMENT_NUMBERS, dtype=jnp.int32)
    counts = jnp.sum((segments[..., None] == numbers).astype(F32), axis=2).astype(BF16)
    kv_shard = jnp.where(first_core, key_weight, value_weight)
    gains = (norm_input, norm_attention, norm_feed, norm_feed_out, norm_query, norm_key)
    gain_sizes = [gain.shape[0] for gain in gains]
    first_cols = q_cols + HEAD_DIM

    def row(*values):
        values = jnp.stack(values)
        return jnp.pad(values, ((0, 0), (0, first_cols - values.shape[1])))

    more = [row(*gains[:4]), row(*gains[4:]), row(counts.reshape(-1))]
    more = more + [jnp.zeros((1, first_cols), BF16)]
    first_pack = jnp.concatenate([query_weight, kv_shard], axis=1)
    first_pack = jnp.concatenate([first_pack] + more, axis=0)
    first_pack = jnp.broadcast_to(first_pack[None], (depths,) + first_pack.shape)
    first_pack, gate_weight, up_weight, down_weight = together(
        first_pack, gate_weight, up_weight, down_weight
    )
    out_pack = copies_to(out_weight.T, "ctx")
    first_pack, out_pack = together(first_pack, out_pack)
    first_pack = lax.all_to_all(first_pack, "ctx", 0, 0)

    share = ((lax.axis_index("fsdp") & 1) * 2 + (ctx_place & 1)).reshape(1)
    shares = run(
        shares_kernel,
        [((3, rows_in, units), BF16)] * 4,
        share, gate_weight, up_weight, down_weight.T,
        in_specs=[pl.BlockSpec(memory_space=pltpu.SMEM)] + in_vmem(3),
    )
    feed_parts = trade_parts(*shares)
    first_pack, feed_parts = together(first_pack, feed_parts)
    counts_all = first_pack[:, rows_in + len(gains), : counts.size].astype(F32)
    counts_all = jnp.sum(counts_all, axis=0).reshape(counts.shape)

    feed_parts = feed_parts.reshape(2, 2, 3, rows_in, units)
    gate_near, up_near, down_near = (feed_parts[:, :, which] for which in range(3))
    gate_deep = gather_depth(gate_near)
    first_pack = copies_to(first_pack, "fsdp")
    first_pack, gate_deep, up_near, down_near, out_pack = together(
        first_pack, gate_deep, up_near, down_near, out_pack
    )

    first_pack = first_pack.reshape(chunks, rows_in + 8, first_cols)
    first_own = first_pack[:, :rows_in].reshape(width, first_cols)
    first_other = swap(first_own)
    gain_input, gain_attention, gain_feed, gain_feed_out, gain_query, gain_key = (
        first_pack[:, rows_in + at, :size].astype(F32).reshape(-1)
        for at, size in enumerate(gain_sizes)
    )
    up_deep = gather_depth(up_near)
    gate_w = gather_plane(gate_deep).reshape(width, units)

    half_at = tp_place * half_len
    seg_half = lax.dynamic_slice_in_dim(segments, half_at, half_len, 2)
    earlier = numbers < seg_half[..., None]
    starts = jnp.sum(jnp.where(earlier, counts_all[:, :, None, :], 0.0), axis=-1)
    starts = starts.astype(jnp.int32)
    token_place = ctx_place * block_len + half_at + jnp.arange(half_len, dtype=jnp.int32)
    cosines, sines = rotations((token_place - starts).astype(F32), HEAD_DIM)
    within = jnp.arange(half_len, dtype=jnp.int32)
    key_place = jnp.concatenate(
        [
            (ctx_place - back) * block_len + side * half_len + within
            for side in (tp_place, 1 - tp_place)
            for back in range(back_blocks + 1)
        ]
    )

    batch = micros * seqs
    rows = batch * half_len
    x_low = lax.dynamic_slice_in_dim(tokens, half_at, half_len, 2).reshape(rows, width)
    dy_low = lax.dynamic_slice_in_dim(cotangent, half_at, half_len, 2).reshape(rows, width)
    cos, sin = cosines.reshape(rows, -1), sines.reshape(rows, -1)
    starts = starts.reshape(rows, 1)
    core = tp_place.reshape(1)
    gains_wide = [
        gain[None]
        for gain in (gain_input, gain_attention, gain_feed, gain_feed_out, gain_query, gain_key)
    ]
    g_in, g_att, g_feed, g_out, g_query, g_key = gains_wide
    smem = [pl.BlockSpec(memory_space=pltpu.SMEM)]
    wide, cols_all = (rows, width), 2 * q_cols

    h1, query_raw, query_rot, key_full, pair = run(
        project_kernel,
        [(wide, BF16), ((rows, cols_all), F32), ((rows, cols_all), BF16)]
        + [((rows, HEAD_DIM), F32), ((rows, 2 * HEAD_DIM), BF16)],
        core, x_low, first_own, first_other, g_in, g_query, g_key, cos, sin,
        in_specs=smem + in_vmem(8),
    )
    up_deep, gate_w, out_pack, down_near = together(up_deep, gate_w, out_pack, down_near)
    down_deep = gather_depth(down_near)
    up_w = gather_plane(up_deep).reshape(width, units)
    out_own = copies_to(out_pack, "fsdp").reshape(width, q_cols)
    pair = pair.reshape(batch, half_len, 2 * HEAD_DIM)
    mine = jnp.concatenate(
        [pair] + [shift(pair, back) for back in range(1, back_blocks + 1)], axis=1
    )
    seen = jnp.concatenate([mine, swap(mine)], axis=1)
    seen, up_w, out_own, down_deep = together(seen, up_w, out_own, down_deep)
    out_other = swap(out_own)
    down_w = gather_plane(down_deep).reshape(width, units)
    span = seen.shape[1]
    token_rows, key_cols = token_place[:, None], key_place[None]
    place_specs = [same_spec(half_len, 1), same_spec(1, span), rows_spec(half_len, 1)]
    seen_spec = pl.BlockSpec((1, span, 2 * HEAD_DIM), lambda i: (i, 0, 0))
    row_spec, col_spec = rows_spec(half_len, width), rows_spec(half_len, cols_all)
    out_specs = [same_spec(width, q_cols)] * 2
    mixed, attention, middle, h2 = run(
        attend_kernel,
        [((rows, cols_all), BF16), (wide, F32), (wide, F32), (wide, BF16)],
        token_rows, key_cols, starts, query_rot, seen, x_low, out_own, out_other, g_att, g_feed,
        grid=(batch,),
        in_specs=place_specs
        + [col_spec, seen_spec, row_spec]
        + out_specs
        + [same_spec(1, width)] * 2,
        out_specs=[col_spec] + [row_spec] * 3,
    )

    h2_mine, down_w = together(spread_start(h2), down_w)
    h2_all = jnp.concatenate([h2_mine, swap(h2_mine)], axis=0)
    hidden, by_up, by_gate, part = feed_forward(h2_all, gate_w, up_w, down_w)
    feed_parts = trade(collect_start(part))
    layer_out, d_feed, d_gain_out = run(
        feed_norm_kernel,
        [(wide, BF16), (wide, BF16), ((8, width), F32)],
        g_out, feed_parts, middle, dy_low,
    )
    d_feed_all = spread(d_feed)
    grad_down = dot("td,tu->du", d_feed_all, hidden).astype(BF16)
    d_feed_all, grad_down = together(d_feed_all, grad_down)
    down_plane = scatter_plane(grad_down.reshape(planes, depths, rows_in, units))
    d_hidden = dot("td,du->tu", d_feed_all, down_w)
    d_gate = (d_hidden * by_gate.astype(F32)).astype(BF16)
    d_up = (d_hidden * by_up.astype(F32)).astype(BF16)
    d_h2_part = dot("tu,du->td", d_gate, gate_w) + dot("tu,du->td", d_up, up_w)
    d_h2_part, d_gate, d_up, down_plane = together(
        d_h2_part.astype(BF16), d_gate, d_up, down_plane
    )
    down_near = scatter_depth(down_plane)
    d_h2_parts = trade(collect_start(d_h2_part))
    grad_gate = dot("td,tu->du", h2_all, d_gate).astype(BF16)
    gate_plane = scatter_plane(grad_gate.reshape(planes, depths, rows_in, units))
    grad_up = dot("td,tu->du", h2_all, d_up).astype(BF16)
    d_h2_parts, down_near, gate_plane, grad_up = together(
        d_h2_parts, down_near, gate_plane, grad_up
    )
    gate_near = scatter_depth(gate_plane)
    up_plane = scatter_plane(grad_up.reshape(planes, depths, rows_in, units))

    side = span // 2
    near_spec = pl.BlockSpec((1, side, 2 * HEAD_DIM), lambda i: (i, 0, 0))
    turn_spec = rows_spec(half_len, HEAD_DIM // 2)
    d_middle, d_attention, d_query, d_near, d_far, d_gains, d_gain_query = run(
        attend_back_kernel,
        [(wide, F32), (wide, BF16), ((rows, cols_all), BF16)]
        + [((batch, side, 2 * HEAD_DIM), F32), ((batch, side, 2 * HEAD_DIM), BF16)]
        + [((8, width), F32), ((8, HEAD_DIM), F32)],
        token_rows, key_cols, starts, query_rot, seen, out_own, out_other,
        g_att, g_feed, g_query, cos, sin, d_h2_parts, middle, attention, dy_low, query_raw,
        grid=(batch,),
        in_specs=place_specs
        + [col_spec, seen_spec]
        + out_specs
        + [same_spec(1, width)] * 2
        + [same_spec(1, HEAD_DIM), turn_spec, turn_spec]
        + [pl.BlockSpec((4, half_len, width), lambda i: (0, i, 0))]
        + [row_spec] * 3
        + [col_spec],
        out_specs=[row_spec, row_spec, col_spec, near_spec, near_spec]
        + [same_spec(8, width), same_spec(8, HEAD_DIM)],
        scratch=[pltpu.VMEM((half_len, cols_all), BF16)],
    )
    d_near, d_far, d_query, d_attention, gate_near, up_plane = together(
        d_near, d_far, d_query, d_attention, gate_near, up_plane
    )
    d_mine = d_near + swap(d_far).astype(F32)
    both_left = jnp.concatenate(
        [dot("td,te->de", d_attention, mixed[:, :q_cols])]
        + [dot("td,te->de", h1, d_query[:, :q_cols])],
        axis=1,
    )
    both_right = jnp.concatenate(
        [dot("td,te->de", d_attention, mixed[:, q_cols:]).astype(BF16)]
        + [dot("td,te->de", h1, d_query[:, q_cols:]).astype(BF16)],
        axis=1,
    )
    both = swap(both_right)
    d_mine, both = together(d_mine, both)
    both = both_left + both.astype(F32)
    both = sum_of(both.reshape(planes, depths, rows_in, cols_all), "fsdp")
    d_kv = d_mine[:, :half_len]
    for back in range(1, back_blocks + 1):
        piece = d_mine[:, back * half_len : (back + 1) * half_len].astype(BF16)
        d_kv = d_kv + shift(piece, -back).astype(F32)
    d_kv, up_plane = together(d_kv, up_plane)
    up_near = scatter_depth(up_plane)
    input_grad, kv_left, kv_right, d_gain_in, d_gain_key = run(
        project_back_kernel,
        [(wide, F32), ((width, HEAD_DIM), F32), ((width, HEAD_DIM), BF16)]
        + [((8, width), F32), ((8, HEAD_DIM), F32)],
        core, d_kv.reshape(rows, 2 * HEAD_DIM), key_full, d_query, h1, x_low,
        first_own, first_other, g_in, g_key, cos, sin, d_middle,
        in_specs=smem + in_vmem(12),
    )
    gain_grads = (d_gain_in[0], d_gains[1], d_gains[0], d_gain_out[0])
    gain_grads = gain_grads + (d_gain_query[0], d_gain_key[0])

    gain_sums = [
        jnp.pad(grad.reshape(chunks, 1, -1), ((0, 0), (0, 0), (0, HEAD_DIM - size)))
        for grad, size in zip(gain_grads, gain_sizes)
    ]
    gain_sums = gain_sums + [jnp.zeros((chunks, 8 - len(gains), HEAD_DIM), F32)]
    gain_sums = jnp.concatenate(gain_sums, axis=1)
    gain_sums = gain_sums + swap(gain_sums.astype(BF16)).astype(F32)
    last = (kv_left + swap(kv_right).astype(F32)).reshape(chunks, rows_in, HEAD_DIM)
    last = jnp.concatenate([last, gain_sums], axis=1).astype(BF16)
    last, both, up_near = together(last, both, up_near)
    feed_grads = jnp.stack([gate_near, up_near, down_near], axis=2)
    own, near, wide, diagonal = trade_split(feed_grads.reshape(4, 3, rows_in, units))
    near = cross(near, 1)
    last = sum_of(last.reshape((planes, depths) + last.shape[1:]), "fsdp")
    last, near, wide, diagonal = together(last, near, wide, diagonal)
    wide, diagonal = cross(wide, depths), cross(diagonal, depths | 1)
    feed_grads = trade_join(own, near, wide, diagonal)
    both = jnp.pad(both, ((0, 0), (0, last.shape[1] - rows_in), (0, 0)))
    last = sum_of(jnp.concatenate([both, last], axis=-1), "ctx")
    both, last = last[:rows_in, :cols_all], last[:, cols_all:]
    out_out, out_query = both[:, :q_cols].T, both[:, q_cols:]
    feed_grads = feed_grads.astype(F32).transpose(1, 2, 0, 3)
    feed_grads = feed_grads.reshape(3, rows_in, 4 * units)[:, :, : 4 * units - spare]
    out_gate, out_up, out_down = feed_grads[0], feed_grads[1], feed_grads[2].T
    out_kv = last[:rows_in]
    kv_other = swap(out_kv)
    out_key = jnp.where(first_core, out_kv, kv_other)
    out_value = jnp.where(first_core, kv_other, out_kv)
    pieces = [last[rows_in + at, :size] for at, size in enumerate(gain_sizes)]

    return (
        layer_out.reshape(micros, seqs, half_len, width),
        input_grad.reshape(micros, seqs, half_len, width),
        pieces[0],
        out_query,
        out_key,
        out_value,
        pieces[4],
        pieces[5],
        out_out,
        pieces[1],
        pieces[2],
        out_gate,
        out_up,
        out_down,
        pieces[3],
    )


def solution(mesh):
    both = ("fsdp", "ctx")
    return jax.shard_map(
        local,
        mesh=mesh,
        in_specs=(
            P(None, "fsdp", "ctx", None),
            P(None, "fsdp", "ctx"),
            P(None, "fsdp", "ctx", None),
            P(both),
            P(both, "tp"),
            P(both, None),
            P(both, None),
            P(both),
            P(both),
            P("tp", both),
            P(both),
            P(both),
            P(both, "tp"),
            P(both, "tp"),
            P("tp", both),
            P(both),
        ),
        out_specs=(
            P(None, "fsdp", ("ctx", "tp"), None),
            P(None, "fsdp", ("ctx", "tp"), None),
            P(both),
            P(both, "tp"),
            P(both, None),
            P(both, None),
            P(both),
            P(both),
            P("tp", both),
            P(both),
            P(both),
            P(both, "tp"),
            P(both, "tp"),
            P("tp", both),
            P(both),
        ),
        check_vma=False,
    )
```
